32 devices in a mesh: dp: 8 (over y, x, core), seq: 4 (over z).
Axes of the slice: x: 2, y: 2, z: 4, core: 2. Of those that a mesh axis runs over, the one named last changes fastest.
Arguments:
- tokens: bfloat16 [8, 1024, 2048], P('dp', 'seq'), may hold values from -6 to 6
- segments: int32 [8, 1024], P('dp'), may hold values from 0 to 3, as said below
- w_query: bfloat16 [2048, 2048], P(('dp', 'seq')), may hold values from -0.125 to 0.125
- w_key: bfloat16 [2048, 2048], P(('dp', 'seq')), may hold values from -0.125 to 0.125
- w_value: bfloat16 [2048, 2048], P(('dp', 'seq')), may hold values from -0.125 to 0.125
- w_out: bfloat16 [2048, 2048], P(('dp', 'seq')), may hold values from -0.125 to 0.125
- g_query: bfloat16 [2048], P(('dp', 'seq')), may hold values from 0.25 to 1.75
- g_key: bfloat16 [2048], P(('dp', 'seq')), may hold values from 0.25 to 1.75
- g_attn: bfloat16 [2048], P(('dp', 'seq')), may hold values from 0.5 to 1.5
- w_gate: bfloat16 [2048, 8192], P(('dp', 'seq')), may hold values from -0.125 to 0.125
- w_up: bfloat16 [2048, 8192], P(('dp', 'seq')), may hold values from -0.125 to 0.125
- w_down: bfloat16 [8192, 2048], P(('dp', 'seq')), may hold values from -0.0625 to 0.0625
- g_ffn: bfloat16 [2048], P(('dp', 'seq')), may hold values from 0.5 to 1.5
- d_out: bfloat16 [8, 1024, 2048], P('dp', 'seq'), may hold values from -6 to 6
Outputs:
- out: bfloat16 [8, 1024, 2048], P('dp', 'seq')
- d_tokens: float32 [8, 1024, 2048], P('dp', 'seq')
- d_w_query: float32 [2048, 2048], P(('dp', 'seq'))
- d_w_key: float32 [2048, 2048], P(('dp', 'seq'))
- d_w_value: float32 [2048, 2048], P(('dp', 'seq'))
- d_w_out: float32 [2048, 2048], P(('dp', 'seq'))
- d_g_query: float32 [2048], P(('dp', 'seq'))
- d_g_key: float32 [2048], P(('dp', 'seq'))
- d_g_attn: float32 [2048], P(('dp', 'seq'))
- d_w_gate: float32 [2048, 8192], P(('dp', 'seq'))
- d_w_up: float32 [2048, 8192], P(('dp', 'seq'))
- d_w_down: float32 [8192, 2048], P(('dp', 'seq'))
- d_g_ffn: float32 [2048], P(('dp', 'seq'))
The draws below stay inside these ranges and needn't reach their ends.
Inputs may be any that keep to these rules, and one draw needn't show every extreme that they name: `segments`: each sequence packs 4 documents in order, numbered 0 to 3, each of 102 tokens or more.
All inputs are finite; a program needn't handle non-finite values.
Results may differ from the reference program's by a relative error of at most 0.023.
Values may be sent and summed in bfloat16 or wider, within the bound.
No kernel may reach another device: no remote copies, remote signals or barrier semaphores. Data moves between devices by JAX's collectives and lax.ppermute only.
A program may use at most 576 MiB of HBM per device.

```python
import jax
import jax.numpy as jnp
from jax import lax

D = 2048
H = 16
HD = 128
FF = 8192
LEN = 1024
DOCS = 4
SEQS = 8


def draw_segments(key, part):
    shares = jax.random.randint(key, (SEQS, DOCS), 1, 1001)
    least = LEN // 10
    spare = LEN - DOCS * least
    lengths = least + spare * shares // jnp.sum(shares, -1, keepdims=True)
    missing = LEN - jnp.sum(lengths, -1, keepdims=True)
    last_col = (jnp.arange(DOCS) == DOCS - 1).astype(jnp.int32)
    lengths = lengths + missing * last_col[None, :]
    ends = jnp.cumsum(lengths, -1)
    index_row = jnp.arange(LEN, dtype=jnp.int32)
    return jnp.sum((index_row[None, :, None] >= ends[:, None, :]).astype(jnp.int32), -1).astype(jnp.int32)


def shard_levels(key, extent, split, low, high):
    factor_of = 1.0
    for axis_at, shards_of in split:
        heights = jax.random.uniform(jax.random.fold_in(jax.random.fold_in(key, 6), axis_at), (shards_of,), jnp.float32, low / len(split), high / len(split))
        factor_of = factor_of * jnp.repeat(jnp.exp(heights), extent[axis_at] // shards_of).reshape((-1,) + (1,) * (len(extent) - 1 - axis_at))
    return factor_of


def scatter_about(rng, dims, deviation, bound, shards=(), kind=jnp.bfloat16):
    array = deviation * jax.random.normal(rng, dims, jnp.float32)
    if shards:
        array = array * shard_levels(rng, dims, shards, -0.22, 0.18)
    return jnp.clip(array, -bound, bound).astype(kind)


def setup_inputs(seed: int = 0) -> dict:
    splits = jax.random.split(jax.random.key(seed), 15)
    return {
        "tokens": scatter_about(splits[0], (SEQS, LEN, D), 1.0, 6.0, ((0, 8), (1, 4))),
        "segments": draw_segments(jax.random.fold_in(splits[14], 71), 0),
        "w_query": scatter_about(splits[2], (D, D), D ** -0.5, 0.125, ((0, 32),)),
        "w_key": scatter_about(splits[3], (D, D), D ** -0.5, 0.125, ((0, 32),)),
        "w_value": scatter_about(splits[4], (D, D), D ** -0.5, 0.125, ((0, 32),)),
        "w_out": scatter_about(splits[5], (D, D), D ** -0.5, 0.125, ((0, 32),)),
        "g_query": jnp.clip(1.0 + 0.15 * jax.random.normal(splits[6], (D,), jnp.float32), 0.25, 1.75).astype(jnp.bfloat16),
        "g_key": jnp.clip(1.0 + 0.15 * jax.random.normal(splits[7], (D,), jnp.float32), 0.25, 1.75).astype(jnp.bfloat16),
        "g_attn": jnp.clip(1.0 + 0.1 * jax.random.normal(splits[8], (D,), jnp.float32), 0.5, 1.5).astype(jnp.bfloat16),
        "w_gate": scatter_about(splits[9], (D, FF), D ** -0.5, 0.125, ((0, 32),)),
        "w_up": scatter_about(splits[10], (D, FF), D ** -0.5, 0.125, ((0, 32),)),
        "w_down": scatter_about(splits[11], (FF, D), FF ** -0.5, 0.0625, ((0, 32),)),
        "g_ffn": jnp.clip(1.0 + 0.1 * jax.random.normal(splits[12], (D,), jnp.float32), 0.5, 1.5).astype(jnp.bfloat16),
        "d_out": scatter_about(splits[13], (SEQS, LEN, D), 1.0, 6.0, ((0, 8), (1, 4))),
    }


epsilon = 1e-06
rope_base = 500000.0
masked_score = -1e+30

@jax.custom_vjp
def low(v):
    return lax.optimization_barrier(v.astype(jnp.bfloat16)).astype(jnp.float32)

@jax.custom_vjp
def low_back(v):
    return v

def low_keep(v):
    return (low(v), None)

def low_pass(kept, grad):
    return (grad,)

def back_keep(v):
    return (v, None)

def back_low(kept, grad):
    return (low(grad),)
low.defvjp(low_keep, low_pass)
low_back.defvjp(back_keep, back_low)

def both_ways(value):
    return low_back(low(value))

def matmul(left, right):
    return jnp.dot(left, right, precision=lax.Precision.HIGHEST, preferred_element_type=jnp.float32)

def rms_norm(values, gain):
    return values * lax.rsqrt(lax.optimization_barrier(jnp.mean(values * values, -1, keepdims=True)) + epsilon) * gain

def positions(seg_ids):
    doc_ids = jnp.arange(DOCS, dtype=jnp.int32)
    one_hot = (seg_ids[..., None] == doc_ids).astype(jnp.int32)
    counts = lax.optimization_barrier(jnp.sum(one_hot, axis=-2))
    starts = jnp.cumsum(counts, axis=-1) - counts
    token_start = lax.optimization_barrier(jnp.sum(one_hot * starts[..., None, :], axis=-1))
    return jnp.arange(seg_ids.shape[-1], dtype=jnp.int32) - token_start

def rope_tables(position_ids):
    freqs = rope_base ** (-jnp.arange(HD // 2, dtype=jnp.float32) * 2.0 / HD)
    angles = position_ids.astype(jnp.float32)[..., None] * freqs
    cosine = jnp.cos(angles)
    sine_tab = jnp.sin(angles)
    return (jnp.concatenate([cosine, cosine], -1)[..., None, :], jnp.concatenate([sine_tab, sine_tab], -1)[..., None, :])

def rotate(values):
    return jnp.concatenate([-values[..., HD // 2:], values[..., :HD // 2]], -1)

def apply_rope(values, cosine, sine_tab):
    return values * cosine + rotate(values) * sine_tab

def attend_one(query_vecs, key_vecs, value_vecs, seg_ids):
    scores = jnp.einsum('qhd,khd->hqk', query_vecs, key_vecs, precision=lax.Precision.HIGHEST) * HD ** (-0.5)
    scores = low_back(scores)
    index_row = jnp.arange(LEN)
    allowed = (seg_ids[:, None] == seg_ids[None, :]) & (index_row[None, :] <= index_row[:, None])
    scores = jnp.where(allowed[None], scores, masked_score)
    attn_probs = jax.nn.softmax(scores, axis=-1)
    return both_ways(jnp.einsum('hqk,khd->qhd', low(attn_probs), value_vecs, precision=lax.Precision.HIGHEST))

def forward(inputs, seg_ids, w_query, w_key, w_value, w_out, g_query, g_key, g_attn, w_gate, w_up, w_down, g_ffn):
    groups = inputs.shape[0]
    tok_rows = inputs.reshape(groups * LEN, D)
    q_raw = low_back(matmul(tok_rows, w_query))
    k_raw = low_back(matmul(tok_rows, w_key))
    v_all = both_ways(matmul(tok_rows, w_value))
    cosine, sine_tab = rope_tables(positions(seg_ids))
    query_vecs = both_ways(apply_rope(rms_norm(q_raw, g_query).reshape(groups, LEN, H, HD), cosine, sine_tab))
    key_vecs = both_ways(apply_rope(rms_norm(k_raw, g_key).reshape(groups, LEN, H, HD), cosine, sine_tab))
    value_vecs = v_all.reshape(groups, LEN, H, HD)
    attend_saved = jax.checkpoint(attend_one)
    attended = lax.map(lambda seq_item: attend_saved(seq_item[0], seq_item[1], seq_item[2], seq_item[3]), (query_vecs, key_vecs, value_vecs, seg_ids))
    a_proj = low_back(matmul(attended.reshape(groups * LEN, D), w_out))
    hidden = tok_rows + rms_norm(a_proj, g_attn)
    hidden_low = low(hidden)
    gate_proj = low_back(matmul(hidden_low, w_gate))
    up_proj = low_back(matmul(hidden_low, w_up))
    inner_act = low(jax.nn.silu(gate_proj) * up_proj)
    m_proj = low_back(matmul(inner_act, w_down))
    return (hidden + rms_norm(m_proj, g_ffn)).reshape(groups, LEN, D)

def reference(tokens, segments, w_query, w_key, w_value, w_out, g_query, g_key, g_attn, w_gate, w_up, w_down, g_ffn, d_out):
    params = tuple((weight_arr.astype(jnp.float32) for weight_arr in (w_query, w_key, w_value, w_out, g_query, g_key, g_attn, w_gate, w_up, w_down, g_ffn)))
    tok_groups = tokens.astype(jnp.float32).reshape(SEQS // 4, 4, LEN, D)
    seg_groups = segments.reshape(SEQS // 4, 4, LEN)
    cot_groups = d_out.astype(jnp.float32).reshape(SEQS // 4, 4, LEN, D)

    def group_step(totals, seq_item):
        tok_part, seg_part, cot_part = seq_item
        result, pullback = jax.vjp(lambda inputs, *weights: forward(inputs, seg_part, *weights), tok_part, *params)
        grad_vals = pullback(cot_part)
        totals = tuple((total_sum + grad_one for total_sum, grad_one in zip(totals, grad_vals[1:])))
        return (totals, (result, grad_vals[0]))
    zero_sums = tuple((jnp.zeros_like(weight_arr) for weight_arr in params))
    totals, outputs = lax.scan(group_step, zero_sums, (tok_groups, seg_groups, cot_groups))
    results, d_inputs = outputs
    return (results.reshape(SEQS, LEN, D).astype(jnp.bfloat16), d_inputs.reshape(SEQS, LEN, D), totals[0], totals[1], totals[2], totals[3], totals[4], totals[5], totals[6], totals[7], totals[8], totals[9], totals[10])
```

```python
import jax
import jax.numpy as jnp
from jax import lax
from jax.sharding import PartitionSpec as P

H = 16
HD = 128
DOCS = 4
CHUNKS = 2

epsilon = 1e-06
rope_base = 500000.0
masked_score = -1e30
bf16 = jnp.bfloat16
f32 = jnp.float32


def product(left, right):
    return jnp.dot(left, right, preferred_element_type=f32)


def against(left, right):
    return lax.dot_general(left, right, (((1,), (1,)), ((), ())), preferred_element_type=f32)


def weight_grad(left, right):
    return lax.dot_general(left, right, (((0,), (0,)), ((), ())), preferred_element_type=f32)


def rms_scale(values):
    return lax.rsqrt(jnp.mean(values * values, -1, keepdims=True) + epsilon)


def norm_back(values, scale_rows, grad_vals):
    return scale_rows * grad_vals - values * scale_rows**3 * jnp.mean(
        grad_vals * values, -1, keepdims=True
    )


def positions(seg_ids):
    doc_ids = jnp.arange(DOCS, dtype=jnp.int32)
    starts = jnp.sum((seg_ids[..., None, :] < doc_ids[:, None]).astype(jnp.int32), -1)
    one_hot = (seg_ids[..., None] == doc_ids).astype(jnp.int32)
    token_start = jnp.sum(one_hot * starts[..., None, :], axis=-1)
    return jnp.arange(seg_ids.shape[-1], dtype=jnp.int32) - token_start


def rope_tables(position_ids):
    freqs = rope_base ** (-jnp.arange(HD // 2, dtype=f32) * 2.0 / HD)
    angles = position_ids.astype(f32)[..., None] * freqs
    cosine = jnp.cos(angles)
    sine_tab = jnp.sin(angles)
    return (
        jnp.concatenate([cosine, cosine], -1)[..., None, :],
        jnp.concatenate([sine_tab, sine_tab], -1)[..., None, :],
    )


def rotate(values):
    return jnp.concatenate([-values[..., HD // 2 :], values[..., : HD // 2]], -1)


def apply_rope(values, cosine, sine_tab):
    return values * cosine + rotate(values) * sine_tab


def rope_back(grad_vals, cosine, sine_tab):
    return grad_vals * cosine - rotate(grad_vals * sine_tab)


def mask_for(seg_ids, row_start, row_count):
    query_ids = row_start + jnp.arange(row_count)
    key_ids = jnp.arange(seg_ids.shape[0])
    same_doc = seg_ids[row_start : row_start + row_count, None] == seg_ids[None, :]
    return same_doc & (key_ids[None, :] <= query_ids[:, None])


def attend(query_vecs, key_vecs, value_vecs, seg_ids):
    length = query_vecs.shape[0]
    q_block = min(512, length)
    score_scale = HD ** (-0.5)
    outputs = []
    log_sums = []
    for row_start in range(0, length, q_block):
        seen = row_start + q_block
        q_part = query_vecs[row_start:seen]
        scores = (
            jnp.einsum("qhd,khd->hqk", q_part, key_vecs[:seen], preferred_element_type=f32)
            * score_scale
        )
        scores = jnp.where(mask_for(seg_ids, row_start, q_block)[None, :, :seen], scores, masked_score)
        row_max = jnp.max(scores, -1, keepdims=True)
        expos = jnp.exp(scores - row_max)
        row_total = jnp.sum(expos, -1, keepdims=True)
        attn_probs = (expos / row_total).astype(bf16)
        block_out = jnp.einsum("hqk,khd->qhd", attn_probs, value_vecs[:seen], preferred_element_type=f32)
        outputs.append(block_out.astype(bf16))
        log_sums.append((row_max + jnp.log(row_total))[..., 0])
    return (jnp.concatenate(outputs, 0), jnp.concatenate(log_sums, 1))


def attend_back(query_vecs, key_vecs, value_vecs, d_attended, seg_ids, log_totals):
    length = query_vecs.shape[0]
    q_block = min(512, length)
    score_scale = HD ** (-0.5)
    d_query_parts = []
    d_keys = jnp.zeros(key_vecs.shape, f32)
    d_values = jnp.zeros(value_vecs.shape, f32)
    for row_start in range(0, length, q_block):
        seen = row_start + q_block
        q_part = query_vecs[row_start:seen]
        g_part = d_attended[row_start:seen]
        k_part = key_vecs[:seen]
        scores = jnp.einsum("qhd,khd->hqk", q_part, k_part, preferred_element_type=f32) * score_scale
        scores = jnp.where(mask_for(seg_ids, row_start, q_block)[None, :, :seen], scores, masked_score)
        attn_probs = jnp.exp(scores - log_totals[:, row_start:seen, None])
        d_probs = jnp.einsum("qhd,khd->hqk", g_part, value_vecs[:seen], preferred_element_type=f32)
        inner_sum = jnp.sum(attn_probs * d_probs, -1, keepdims=True)
        d_scores = (attn_probs * (d_probs - inner_sum)).astype(bf16)
        d_query_parts.append(
            jnp.einsum("hqk,khd->qhd", d_scores, k_part, preferred_element_type=f32) * score_scale
        )
        d_k_part = jnp.einsum("hqk,qhd->khd", d_scores, q_part, preferred_element_type=f32) * score_scale
        d_v_part = jnp.einsum("hqk,qhd->khd", attn_probs.astype(bf16), g_part, preferred_element_type=f32)
        d_keys = d_keys.at[:seen].add(d_k_part)
        d_values = d_values.at[:seen].add(d_v_part)
    return (jnp.concatenate(d_query_parts, 0), d_keys, d_values)


def line_gather(block, axis):
    size = lax.axis_size(axis)
    here = lax.axis_index(axis)
    up, down = [block], [block]
    for step in range(1, size):
        up.append(lax.ppermute(up[-1], axis, [(i, i + 1) for i in range(step - 1, size - 1)]))
        down.append(lax.ppermute(down[-1], axis, [(i, i - 1) for i in range(1, size - step + 1)]))
    return [block] + [
        jnp.where(here >= back, up[back], down[size - back]) for back in range(1, size)
    ]


def line_scatter_sum(parts, axis):
    size = lax.axis_size(axis)
    from_below = from_above = None
    for step in range(1, size):
        up, down = parts[step], parts[size - step]
        if step > 1:
            up = up.astype(f32) + from_below.astype(f32)
            down = down.astype(f32) + from_above.astype(f32)
        from_below = lax.ppermute(up.astype(bf16), axis, [(i, i + 1) for i in range(step)])
        from_above = lax.ppermute(down.astype(bf16), axis, [(i, i - 1) for i in range(size - step, size)])
    return parts[0].astype(f32) + from_below.astype(f32) + from_above.astype(f32)


def in_order(slots, axis):
    size = lax.axis_size(axis)
    rising = slots[:0:-1] + slots[:1]
    twice = jnp.concatenate([s[None] for s in rising + rising[: size - 1]], 0)
    start = lax.rem(2 * size - 1 - lax.axis_index(axis), size)
    return lax.dynamic_slice_in_dim(twice, start, size, 0)


def small_sum(values, axis):
    size = lax.axis_size(axis)
    total = values
    for step in range(1, size):
        total = total + lax.ppermute(values, axis, [(i, (i + step) % size) for i in range(size)])
    return total


def local(
    tokens,
    segments,
    w_query,
    w_key,
    w_value,
    w_out,
    g_query,
    g_key,
    g_attn,
    w_gate,
    w_up,
    w_down,
    g_ffn,
    d_out,
):
    seqs, local_len, width = tokens.shape
    rows = seqs * local_len
    copies, size = lax.axis_size("dp"), lax.axis_size("seq")
    here = lax.axis_index("seq")
    total_len = size * local_len
    part = width // size
    heads = H // size
    own_rows = w_gate.shape[0]
    ff_width = w_gate.shape[1]
    ff_part = ff_width // size
    ff_own = w_down.shape[0]
    everyone = ("dp", "seq")
    tok_rows = tokens.reshape(rows, width)

    qkv_own = jnp.stack([w_query, w_key, w_value], 1).reshape(own_rows, 3, size, part)
    qkv_own = lax.all_to_all(
        qkv_own.transpose(2, 0, 1, 3), "seq", split_axis=0, concat_axis=0, tiled=True
    ).reshape(size * own_rows, 3 * part)
    w_qkv = lax.all_gather(qkv_own, "dp", axis=0, tiled=True)
    gu_own = jnp.stack([w_gate, w_up], 1).reshape(own_rows, 2, copies, size, ff_own)
    gu_own = lax.all_to_all(
        gu_own.transpose(3, 0, 1, 2, 4), "seq", split_axis=0, concat_axis=0, tiled=True
    ).reshape(size * own_rows, 2 * ff_part)
    w_gu = lax.all_gather(gu_own, "dp", axis=0, tiled=True)
    w_gate_part, w_up_part = w_gu[:, :ff_part], w_gu[:, ff_part:]
    w_down_part = lax.all_gather(w_down, "dp", axis=0, tiled=True)
    w_out_all = lax.all_gather(
        lax.all_gather(w_out, "seq", axis=0, tiled=True), "dp", axis=0, tiled=True
    )
    gains = lax.all_gather(
        jnp.stack([g_query, g_key, g_attn, g_ffn], 0), everyone, axis=1, tiled=True
    ).astype(f32)
    gain_attn, gain_ffn = gains[2], gains[3]
    gain_qk = lax.dynamic_slice_in_dim(gains[:2], here * part, part, 1).reshape(2, heads, HD)

    x_all = in_order([s.reshape(seqs, local_len, width) for s in line_gather(tok_rows, "seq")], "seq")
    x_all = x_all.transpose(1, 0, 2, 3).reshape(seqs * total_len, width)
    qkv = product(x_all, w_qkv).reshape(seqs * total_len, 3, part)
    qk_raw = qkv[:, :2]
    squares = small_sum(jnp.sum(qk_raw * qk_raw, -1), "seq")
    qk_scale = lax.rsqrt(squares / width + epsilon)[..., None, None]
    qk_raw = qk_raw.reshape(seqs * total_len, 2, heads, HD)
    cosine, sine_tab = rope_tables(positions(segments).reshape(seqs * total_len))
    cosine, sine_tab = cosine[:, None], sine_tab[:, None]
    qk_unit = qk_raw * qk_scale
    qk_low = apply_rope(qk_unit * gain_qk, cosine, sine_tab).astype(bf16)
    head_shape = (seqs, total_len, heads, HD)
    query_low = qk_low[:, 0].reshape(head_shape)
    key_low = qk_low[:, 1].reshape(head_shape)
    value_low = qkv[:, 2].astype(bf16).reshape(head_shape)
    attended_heads, log_totals = jax.vmap(attend)(query_low, key_low, value_low, segments)
    attended = lax.all_to_all(
        attended_heads.reshape(seqs, total_len, part), "seq", split_axis=1, concat_axis=2, tiled=True
    ).reshape(rows, width)

    step = rows // CHUNKS
    cuts = [slice(at * step, (at + 1) * step) for at in range(CHUNKS)]
    d_out_rows = d_out.reshape(rows, width)
    a_parts, hidden_parts, hidden_all = [], [], []
    for cut in cuts:
        a_proj = product(attended[cut], w_out_all)
        a_scale = rms_scale(a_proj)
        hidden = tok_rows[cut].astype(f32) + a_proj * a_scale * gain_attn
        a_parts.append((a_proj, a_scale))
        hidden_parts.append(hidden)
        hidden_all.append(jnp.concatenate(line_gather(hidden.astype(bf16), "seq"), 0))
    gates, ups, inners, outs, dms, d_gain_ffn = [], [], [], [], [], 0.0
    for at, cut in enumerate(cuts):
        gate = product(hidden_all[at], w_gate_part)
        up = product(hidden_all[at], w_up_part)
        inner = (jax.nn.silu(gate) * up).astype(bf16)
        m_share = product(inner, w_down_part).astype(bf16)
        gates.append(gate)
        ups.append(up)
        inners.append(inner)
        m_proj = line_scatter_sum([m_share[o * step : (o + 1) * step] for o in range(size)], "seq")
        m_scale = rms_scale(m_proj)
        outs.append((hidden_parts[at] + m_proj * m_scale * gain_ffn).astype(bf16))
        grad_out = d_out_rows[cut].astype(f32)
        d_gain_ffn = d_gain_ffn + jnp.sum(grad_out * m_proj * m_scale, 0)
        dm_low = norm_back(m_proj, m_scale, grad_out * gain_ffn).astype(bf16)
        dms.append(jnp.concatenate(line_gather(dm_low, "seq"), 0))
    d_gates, d_ups, d_hiddens, das, d_attendeds, d_gain_attn = [], [], [], [], [], 0.0
    for at, cut in enumerate(cuts):
        gate, up = gates[at], ups[at]
        d_inner = against(dms[at], w_down_part)
        sigmoid_gate = jax.nn.sigmoid(gate)
        d_gate = (d_inner * up * sigmoid_gate * (1.0 + gate * (1.0 - sigmoid_gate))).astype(bf16)
        d_up = (d_inner * (gate * sigmoid_gate)).astype(bf16)
        d_gates.append(d_gate)
        d_ups.append(d_up)
        h_share = (against(d_gate, w_gate_part) + against(d_up, w_up_part)).astype(bf16)
        d_hidden = d_out_rows[cut].astype(f32) + line_scatter_sum(
            [h_share[o * step : (o + 1) * step] for o in range(size)], "seq"
        )
        a_proj, a_scale = a_parts[at]
        d_gain_attn = d_gain_attn + jnp.sum(d_hidden * a_proj * a_scale, 0)
        da_low = norm_back(a_proj, a_scale, d_hidden * gain_attn).astype(bf16)
        d_hiddens.append(d_hidden)
        das.append(da_low)
        d_attendeds.append(against(da_low, w_out_all).astype(bf16))
    out = jnp.concatenate(outs, 0).reshape(tokens.shape)
    d_hidden = jnp.concatenate(d_hiddens, 0)

    inner_all = jnp.concatenate(inners, 0)
    dm_all = jnp.concatenate(dms, 0)
    hidden_all = jnp.concatenate(hidden_all, 0)
    d_gu = jnp.concatenate(
        [
            weight_grad(hidden_all, jnp.concatenate(d_gates, 0)).astype(bf16),
            weight_grad(hidden_all, jnp.concatenate(d_ups, 0)).astype(bf16),
        ],
        1,
    )
    d_down = weight_grad(inner_all, dm_all).astype(bf16)
    d_w_out = weight_grad(attended, jnp.concatenate(das, 0)).astype(bf16)
    d_down = lax.psum_scatter(d_down, "dp", scatter_dimension=0, tiled=True).astype(f32)
    d_gu = lax.psum_scatter(d_gu, "dp", scatter_dimension=0, tiled=True)
    d_gu = lax.all_to_all(
        d_gu.reshape(size, own_rows, 2, copies, ff_own), "seq", split_axis=0, concat_axis=0, tiled=True
    )
    d_gu = d_gu.transpose(2, 1, 3, 0, 4).reshape(2, own_rows, ff_width).astype(f32)
    d_w_out = lax.psum_scatter(
        lax.psum_scatter(d_w_out, "dp", scatter_dimension=0, tiled=True),
        "seq",
        scatter_dimension=0,
        tiled=True,
    ).astype(f32)

    d_attended = jnp.concatenate(d_attendeds, 0).reshape(seqs, local_len, width)
    d_attended = lax.all_to_all(d_attended, "seq", split_axis=2, concat_axis=1, tiled=True).reshape(head_shape)
    dq, dk, dv = jax.vmap(attend_back)(query_low, key_low, value_low, d_attended, segments, log_totals)
    d_qk = jnp.stack([dq, dk], 2).reshape(seqs * total_len, 2, heads, HD).astype(bf16).astype(f32)
    d_qk = rope_back(d_qk, cosine, sine_tab)
    d_gain_qk = jnp.sum(d_qk * qk_unit, 0)
    d_qk = d_qk * gain_qk
    dots = small_sum(jnp.sum(d_qk * qk_raw, (-2, -1)), "seq")[..., None, None] / width
    d_qk = (qk_scale * d_qk - qk_raw * qk_scale**3 * dots).astype(bf16)
    d_qkv = jnp.concatenate(
        [d_qk.reshape(seqs * total_len, 2 * part), dv.astype(bf16).reshape(seqs * total_len, part)], 1
    )
    x_share = against(d_qkv, w_qkv).astype(bf16).reshape(seqs, size, local_len, width)
    x_share = [
        lax.dynamic_index_in_dim(x_share, lax.rem(here + size - o, size), 1, keepdims=False).reshape(rows, width)
        for o in range(size)
    ]
    d_tokens = d_hidden + line_scatter_sum(x_share, "seq")
    d_w_qkv = weight_grad(x_all, d_qkv).astype(bf16)
    d_w_qkv = lax.psum_scatter(d_w_qkv, "dp", scatter_dimension=0, tiled=True)
    d_w_qkv = lax.all_to_all(
        d_w_qkv.reshape(size, own_rows, 3, part), "seq", split_axis=0, concat_axis=0, tiled=True
    )
    d_w_qkv = d_w_qkv.transpose(2, 1, 0, 3).reshape(3, own_rows, width).astype(f32)

    d_gain_qk = lax.dynamic_update_slice_in_dim(
        jnp.zeros((2, width), f32), d_gain_qk.reshape(2, part), here * part, 1
    )
    d_gains = jnp.concatenate([d_gain_qk, d_gain_attn[None], d_gain_ffn[None]], 0)
    d_gains = lax.psum_scatter(d_gains, everyone, scatter_dimension=1, tiled=True)
    return (
        out,
        d_tokens.reshape(tokens.shape),
        d_w_qkv[0],
        d_w_qkv[1],
        d_w_qkv[2],
        d_w_out,
        d_gains[0],
        d_gains[1],
        d_gains[2],
        d_gu[0],
        d_gu[1],
        d_down,
        d_gains[3],
    )


def solution(mesh):
    rows = P("dp", "seq", None)
    mat = P(("dp", "seq"), None)
    vec = P(("dp", "seq"))
    in_specs = (rows, P("dp", None), mat, mat, mat, mat, vec, vec, vec, mat, mat, mat, vec, rows)
    out_specs = (rows, rows, mat, mat, mat, mat, vec, vec, vec, mat, mat, mat, vec)
    return jax.shard_map(local, mesh=mesh, in_specs=in_specs, out_specs=out_specs, check_vma=False)
```

```python
import jax
import jax.numpy as jnp
from jax import lax
from jax.sharding import PartitionSpec as P

H = 16
HD = 128
DOCS = 4

epsilon = 1e-06
rope_base = 500000.0
masked_score = -1e30
bf16 = jnp.bfloat16
f32 = jnp.float32


def product(left, right):
    return jnp.dot(left, right, preferred_element_type=f32)


def against(left, right):
    return lax.dot_general(left, right, (((1,), (1,)), ((), ())), preferred_element_type=f32)


def weight_grad(left, right):
    return lax.dot_general(left, right, (((0,), (0,)), ((), ())), preferred_element_type=f32)


def rms_scale(values):
    return lax.rsqrt(jnp.mean(values * values, -1, keepdims=True) + epsilon)


def norm_back(values, scale_rows, grad_vals):
    return scale_rows * grad_vals - values * scale_rows**3 * jnp.mean(
        grad_vals * values, -1, keepdims=True
    )


def positions(seg_ids):
    doc_ids = jnp.arange(DOCS, dtype=jnp.int32)
    starts = jnp.sum((seg_ids[..., None, :] < doc_ids[:, None]).astype(jnp.int32), -1)
    one_hot = (seg_ids[..., None] == doc_ids).astype(jnp.int32)
    token_start = jnp.sum(one_hot * starts[..., None, :], axis=-1)
    return jnp.arange(seg_ids.shape[-1], dtype=jnp.int32) - token_start


def rope_tables(position_ids):
    freqs = rope_base ** (-jnp.arange(HD // 2, dtype=f32) * 2.0 / HD)
    angles = position_ids.astype(f32)[..., None] * freqs
    cosine = jnp.cos(angles)
    sine_tab = jnp.sin(angles)
    return (
        jnp.concatenate([cosine, cosine], -1)[..., None, :],
        jnp.concatenate([sine_tab, sine_tab], -1)[..., None, :],
    )


def rotate(values):
    return jnp.concatenate([-values[..., HD // 2 :], values[..., : HD // 2]], -1)


def apply_rope(values, cosine, sine_tab):
    return values * cosine + rotate(values) * sine_tab


def rope_back(grad_vals, cosine, sine_tab):
    return grad_vals * cosine - rotate(grad_vals * sine_tab)


def mask_for(seg_ids, row_start, row_count):
    query_ids = row_start + jnp.arange(row_count)
    key_ids = jnp.arange(seg_ids.shape[0])
    same_doc = seg_ids[row_start : row_start + row_count, None] == seg_ids[None, :]
    return same_doc & (key_ids[None, :] <= query_ids[:, None])


def attend(query_vecs, key_vecs, value_vecs, seg_ids):
    length = query_vecs.shape[0]
    q_block = min(512, length)
    score_scale = HD ** (-0.5)
    outputs = []
    log_sums = []
    for row_start in range(0, length, q_block):
        seen = row_start + q_block
        q_part = query_vecs[row_start:seen]
        scores = (
            jnp.einsum("qhd,khd->hqk", q_part, key_vecs[:seen], preferred_element_type=f32)
            * score_scale
        )
        scores = jnp.where(mask_for(seg_ids, row_start, q_block)[None, :, :seen], scores, masked_score)
        row_max = jnp.max(scores, -1, keepdims=True)
        expos = jnp.exp(scores - row_max)
        row_total = jnp.sum(expos, -1, keepdims=True)
        attn_probs = (expos / row_total).astype(bf16)
        block_out = jnp.einsum("hqk,khd->qhd", attn_probs, value_vecs[:seen], preferred_element_type=f32)
        outputs.append(block_out.astype(bf16))
        log_sums.append((row_max + jnp.log(row_total))[..., 0])
    return (jnp.concatenate(outputs, 0), jnp.concatenate(log_sums, 1))


def attend_back(query_vecs, key_vecs, value_vecs, d_attended, seg_ids, log_totals):
    length = query_vecs.shape[0]
    q_block = min(512, length)
    score_scale = HD ** (-0.5)
    d_query_parts = []
    d_keys = jnp.zeros(key_vecs.shape, f32)
    d_values = jnp.zeros(value_vecs.shape, f32)
    for row_start in range(0, length, q_block):
        seen = row_start + q_block
        q_part = query_vecs[row_start:seen]
        g_part = d_attended[row_start:seen]
        k_part = key_vecs[:seen]
        scores = jnp.einsum("qhd,khd->hqk", q_part, k_part, preferred_element_type=f32) * score_scale
        scores = jnp.where(mask_for(seg_ids, row_start, q_block)[None, :, :seen], scores, masked_score)
        attn_probs = jnp.exp(scores - log_totals[:, row_start:seen, None])
        d_probs = jnp.einsum("qhd,khd->hqk", g_part, value_vecs[:seen], preferred_element_type=f32)
        inner_sum = jnp.sum(attn_probs * d_probs, -1, keepdims=True)
        d_scores = (attn_probs * (d_probs - inner_sum)).astype(bf16)
        d_query_parts.append(
            jnp.einsum("hqk,khd->qhd", d_scores, k_part, preferred_element_type=f32) * score_scale
        )
        d_k_part = jnp.einsum("hqk,qhd->khd", d_scores, q_part, preferred_element_type=f32) * score_scale
        d_v_part = jnp.einsum("hqk,qhd->khd", attn_probs.astype(bf16), g_part, preferred_element_type=f32)
        d_keys = d_keys.at[:seen].add(d_k_part)
        d_values = d_values.at[:seen].add(d_v_part)
    return (jnp.concatenate(d_query_parts, 0), d_keys, d_values)


def after(value, *done):
    ends = [lax.slice(d, (0,) * d.ndim, (1,) * d.ndim) for d in done]
    return lax.optimization_barrier((value, *ends))[0]


def next_one(block, axis):
    size = lax.axis_size(axis)
    return lax.ppermute(block, axis, [(i, (i + 1) % size) for i in range(size)])


def in_order(slots, axis):
    size, here = lax.axis_size(axis), lax.axis_index(axis)
    joined = jnp.zeros((size,) + slots[0].shape, slots[0].dtype)
    for back, slot in enumerate(slots):
        joined = lax.dynamic_update_index_in_dim(joined, slot, lax.rem(here + size - back, size), 0)
    return joined


def exchange(blocks, axis):
    size, here = lax.axis_size(axis), lax.axis_index(axis)
    got = []
    for step in range(size):
        block = lax.dynamic_index_in_dim(blocks, lax.rem(here + step, size), 0, keepdims=False)
        if step:
            block = lax.ppermute(block, axis, [(i, (i + step) % size) for i in range(size)])
        got.append(block)
    return got


def flipped(block, bit):
    size = lax.axis_size("dp")
    return lax.ppermute(block, "dp", [(i, i ^ bit) for i in range(size)])


def cube_bits():
    bits = [1 << b for b in range(1, (lax.axis_size("dp") - 1).bit_length())]
    return bits, bits[1:] + bits[:1]


class CubeGather:
    def __init__(self, pair):
        self.tables = [{0: block} for block in pair]
        self.orders = [bits + [1] for bits in cube_bits()]
        self.steps = len(self.orders[0])

    def step(self):
        got = []
        for table, order in zip(self.tables, self.orders):
            bit = order.pop(0)
            new = {m ^ bit: flipped(v, bit) for m, v in table.items()}
            table.update(new)
            got.extend(new.values())
        return got


def cube_rows(have):
    here, rows = lax.axis_index("dp"), have[0].shape[0]
    joined = jnp.zeros((len(have) * rows,) + have[0].shape[1:], have[0].dtype)
    for mask, block in have.items():
        joined = lax.dynamic_update_slice_in_dim(joined, block, (here ^ mask) * rows, 0)
    return joined


def cube_rows_halves(halves):
    here, rows = lax.axis_index("dp"), halves[0][0].shape[0]
    count = len(halves[0])
    joined = jnp.zeros((2 * count * rows,) + halves[0][0].shape[1:], halves[0][0].dtype)
    for at, have in enumerate(halves):
        for mask, block in have.items():
            joined = lax.dynamic_update_slice_in_dim(joined, block, ((here ^ mask) * 2 + at) * rows, 0)
    return joined


def split_columns(left):
    size, here = lax.axis_size("dp"), lax.axis_index("dp")
    block = left.shape[1] // size
    bits = (size - 1).bit_length()
    sides = []
    for side in (1, 0):
        masks = []
        for at in range(size // 2):
            mask = side
            for b in range(1, bits):
                mask |= ((at >> (bits - 1 - b)) & 1) << b
            masks.append(mask)
        sides.append(
            jnp.concatenate(
                [lax.dynamic_slice_in_dim(left, (here ^ m) * block, block, 1) for m in masks], 1
            )
        )
    return sides


def split_grad(sides, right):
    bits = (lax.axis_size("dp") - 1).bit_length()
    shape = (2,) * (bits - 1) + (-1, right.shape[1])
    return [weight_grad(side, right).astype(bf16).reshape(shape) for side in sides]


class CubeScatter:
    def __init__(self, pairs):
        self.pairs, self.orders = pairs, [list(bits) for bits in cube_bits()]
        self.dims = [sorted(bits) for bits in self.orders]
        self.totals = None
        self.steps = 1 + len(self.orders[0])

    def step(self, *done):
        if self.totals is None:
            got = [flipped(after(sent, *done) if done else sent, 1) for sent, _ in self.pairs]
            self.totals = [keep.astype(f32) + g.astype(f32) for (_, keep), g in zip(self.pairs, got)]
            return got
        got = []
        for which, total in enumerate(self.totals):
            bit = self.orders[which].pop(0)
            at = self.dims[which].index(bit)
            self.dims[which].remove(bit)
            away = lax.index_in_dim(total, 1, at, keepdims=False).astype(bf16)
            got.append(flipped(away, bit))
            self.totals[which] = lax.index_in_dim(total, 0, at, keepdims=False) + got[-1].astype(f32)
        return got


def halves_of(grad):
    cut = grad[0].shape[-1] // 2
    return [[g[..., :cut] for g in grad], [g[..., cut:] for g in grad]]


def gather_small(block):
    slots = in_order(exchange(jnp.broadcast_to(block, (lax.axis_size("seq"),) + block.shape), "seq"), "seq")
    block = slots.transpose(1, 0, 2).reshape(block.shape[0], -1)
    here, wide = lax.axis_index("dp"), block.shape[1]
    table = {0: block}
    for bit in cube_bits()[0] + [1]:
        table.update({m ^ bit: flipped(v, bit) for m, v in table.items()})
    joined = jnp.zeros((block.shape[0], wide * len(table)), block.dtype)
    for mask, piece in table.items():
        joined = lax.dynamic_update_slice_in_dim(joined, piece, (here ^ mask) * wide, 1)
    return joined


def scatter_small(values):
    copies, size, here = lax.axis_size("dp"), lax.axis_size("seq"), lax.axis_index("dp")
    blocks = values.reshape(values.shape[0], copies, size, -1).transpose(2, 1, 0, 3)
    total = sum(exchange(blocks, "seq"))
    for bit in reversed([1] + cube_bits()[0]):
        total = total.reshape((2, total.shape[0] // 2) + total.shape[1:])
        mine = (here // bit) % 2
        away = lax.dynamic_index_in_dim(total, 1 - mine, 0, keepdims=False)
        total = lax.dynamic_index_in_dim(total, mine, 0, keepdims=False) + flipped(away, bit)
    return total[0]


def small_sum(values, axis):
    size = lax.axis_size(axis)
    total = values
    for step in range(1, size):
        total = total + lax.ppermute(values, axis, [(i, (i + step) % size) for i in range(size)])
    return total


def local(
    tokens,
    segments,
    w_query,
    w_key,
    w_value,
    w_out,
    g_query,
    g_key,
    g_attn,
    w_gate,
    w_up,
    w_down,
    g_ffn,
    d_out,
):
    seqs, local_len, width = tokens.shape
    rows = seqs * local_len
    copies, size = lax.axis_size("dp"), lax.axis_size("seq")
    here = lax.axis_index("seq")
    total_len = size * local_len
    part = width // size
    heads = H // size
    own_rows = w_gate.shape[0]
    ff_width = w_gate.shape[1]
    ff_part = ff_width // size
    ff_own = w_down.shape[0]
    everyone = ("dp", "seq")
    tok_rows = tokens.reshape(rows, width)

    gains = gather_small(jnp.stack([g_query, g_key, g_attn, g_ffn], 0)).astype(f32)
    gain_attn, gain_ffn = gains[2], gains[3]
    gain_qk = lax.dynamic_slice_in_dim(gains[:2], here * part, part, 1).reshape(2, heads, HD)
    w_down_part = lax.all_gather(w_down, "dp", axis=0, tiled=True)
    w_out_all = lax.all_gather(w_out, everyone, axis=0, tiled=True)
    qkv_own = jnp.stack([w_query, w_key, w_value], 1).reshape(own_rows, 3, size, part)
    qkv_own = exchange(qkv_own.transpose(2, 0, 1, 3).reshape(size, own_rows, 3 * part), "seq")
    qkv_got = qkv_own[1:]
    qkv_own = in_order(qkv_own, "seq").reshape(size * own_rows, 3 * part)
    half = size * own_rows // 2
    cube_qkv = CubeGather([qkv_own[:half], qkv_own[half:]])
    for _ in range(cube_qkv.steps):
        cube_qkv.step()
    w_qkv = cube_rows_halves(cube_qkv.tables)

    def to_columns(weight, *done):
        blocks = weight.reshape(own_rows, copies, size, ff_own).transpose(2, 0, 1, 3)
        got = exchange(after(blocks.reshape(size, own_rows, ff_part), *done), "seq")
        return got[1:], in_order(got, "seq").reshape(size * own_rows, ff_part)

    gate_got, gate_own = to_columns(w_gate, *qkv_got)
    half_gate = [gate_own[:half], gate_own[half:]]
    cube_gate = CubeGather(half_gate)
    gate_done = [cube_gate.step()]
    x_slots = [tok_rows]
    for at in range(size - 1):
        block = x_slots[-1]
        if at == 0:
            block = after(block, *gate_got)
        if at == size - 2:
            block = after(block, *gate_done[0])
        x_slots.append(next_one(block, "seq"))
    for _ in range(cube_gate.steps - 1):
        gate_done.append(cube_gate.step())
    w_gate_part = cube_rows_halves(cube_gate.tables)
    up_got, up_own = to_columns(w_up, x_slots[-1])
    cube_up = CubeGather([up_own[:half], up_own[half:]])
    up_done = [cube_up.step() for _ in range(cube_up.steps)]
    w_up_part = cube_rows_halves(cube_up.tables)

    x_all = in_order([s.reshape(seqs, local_len, width) for s in x_slots], "seq")
    x_all = x_all.transpose(1, 0, 2, 3).reshape(seqs * total_len, width)
    qkv = product(after(x_all, w_down_part, *gate_done[-2]), w_qkv).reshape(seqs * total_len, 3, part)
    qk_raw = qkv[:, :2]
    squares = small_sum(jnp.sum(qk_raw * qk_raw, -1), "seq")
    qk_scale = lax.rsqrt(squares / width + epsilon)[..., None, None]
    qk_raw = qk_raw.reshape(seqs * total_len, 2, heads, HD)
    cosine, sine_tab = rope_tables(positions(segments).reshape(seqs * total_len))
    cosine, sine_tab = cosine[:, None], sine_tab[:, None]
    qk_unit = qk_raw * qk_scale
    qk_low = apply_rope(qk_unit * gain_qk, cosine, sine_tab).astype(bf16)
    head_shape = (seqs, total_len, heads, HD)
    qk_low = after(qk_low, *gate_done[-1], *up_got)
    query_low = qk_low[:, 0].reshape(head_shape)
    key_low = qk_low[:, 1].reshape(head_shape)
    value_low = qkv[:, 2].astype(bf16).reshape(head_shape)
    attended_heads, log_totals = jax.vmap(attend)(query_low, key_low, value_low, segments)
    attended_heads = after(attended_heads, w_out_all, *up_done[0])
    attended = lax.all_to_all(
        attended_heads.reshape(seqs, total_len, part), "seq", split_axis=1, concat_axis=2, tiled=True
    ).reshape(rows, width)
    attended = after(attended, *up_done[1])

    a_proj = product(attended, w_out_all)
    a_scale = rms_scale(a_proj)
    hidden = tok_rows.astype(f32) + a_proj * a_scale * gain_attn

    def ring(block, work):
        got, own = None, None
        for at in range(size):
            later = next_one(block, "seq") if at < size - 1 else None
            share = work(block)
            if at == 0:
                own = share
            else:
                if at > 1:
                    share = share + got.astype(f32)
                got = next_one(share.astype(bf16), "seq")
            block = later
        return own + got.astype(f32)

    h_slots, gates, ups, inners = [], [], [], []

    def forward(h_low):
        gate = product(h_low, w_gate_part)
        up = product(h_low, w_up_part)
        inner = (jax.nn.silu(gate) * up).astype(bf16)
        h_slots.append(h_low)
        gates.append(gate)
        ups.append(up)
        inners.append(inner)
        return product(inner, w_down_part)

    m_proj = ring(hidden.astype(bf16), forward)
    m_scale = rms_scale(m_proj)
    out = (hidden + m_proj * m_scale * gain_ffn).astype(bf16).reshape(tokens.shape)
    grad_out = d_out.reshape(rows, width).astype(f32)
    d_gain_ffn = jnp.sum(grad_out * m_proj * m_scale, 0)
    dm_low = norm_back(m_proj, m_scale, grad_out * gain_ffn).astype(bf16)
    dms, d_gates, d_ups = [], [], []

    def backward(dm_slot):
        at = len(dms)
        gate, up = gates[at], ups[at]
        d_inner = against(dm_slot, w_down_part)
        sigmoid_gate = jax.nn.sigmoid(gate)
        d_gate = (d_inner * up * sigmoid_gate * (1.0 + gate * (1.0 - sigmoid_gate))).astype(bf16)
        d_up = (d_inner * (gate * sigmoid_gate)).astype(bf16)
        dms.append(dm_slot)
        d_gates.append(d_gate)
        d_ups.append(d_up)
        return against(d_gate, w_gate_part) + against(d_up, w_up_part)

    d_sum = ring(dm_low, backward)
    d_down = weight_grad(jnp.concatenate(inners, 0), jnp.concatenate(dms, 0)).astype(bf16)
    h_sides = split_columns(jnp.concatenate(h_slots, 0))
    d_gate = split_grad(h_sides, jnp.concatenate(d_gates, 0))
    d_up = split_grad(h_sides, jnp.concatenate(d_ups, 0))
    d_hidden = grad_out + after(d_sum, d_down, *d_gate)
    d_gain_attn = jnp.sum(d_hidden * a_proj * a_scale, 0)
    da_low = norm_back(a_proj, a_scale, d_hidden * gain_attn).astype(bf16)
    d_attended = against(da_low, w_out_all).astype(bf16).reshape(seqs, local_len, width)
    d_attended = lax.all_to_all(d_attended, "seq", split_axis=2, concat_axis=1, tiled=True).reshape(head_shape)
    d_w_out = weight_grad(attended, da_low).astype(bf16)

    d_down = lax.psum_scatter(d_down, "dp", scatter_dimension=0, tiled=True).astype(f32)
    d_w_out = lax.psum_scatter(d_w_out, everyone, scatter_dimension=0, tiled=True).astype(f32)
    cube_gu = CubeScatter([d_gate, d_up])
    gu_done = [cube_gu.step() for _ in range(cube_gu.steps)]
    d_gu = jnp.stack(cube_gu.totals, 0).astype(bf16).reshape(2, size, own_rows, copies, ff_own)
    d_gu = lax.all_to_all(d_gu.transpose(1, 0, 2, 3, 4), "seq", split_axis=0, concat_axis=0, tiled=True)
    d_gu = d_gu.transpose(1, 2, 3, 0, 4).reshape(2, own_rows, ff_width).astype(f32)

    d_attended = after(d_attended, d_w_out, *gu_done[0])
    dq, dk, dv = jax.vmap(attend_back)(query_low, key_low, value_low, d_attended, segments, log_totals)
    d_qk = jnp.stack([dq, dk], 2).reshape(seqs * total_len, 2, heads, HD).astype(bf16)
    d_qk = after(d_qk, d_down, *gu_done[1]).astype(f32)
    d_qk = rope_back(d_qk, cosine, sine_tab)
    d_gain_qk = jnp.sum(d_qk * qk_unit, 0)
    d_qk = d_qk * gain_qk
    dots = small_sum(jnp.sum(d_qk * qk_raw, (-2, -1)), "seq")[..., None, None] / width
    d_qk = (qk_scale * d_qk - qk_raw * qk_scale**3 * dots).astype(bf16)
    d_qkv = jnp.concatenate(
        [d_qk.reshape(seqs * total_len, 2 * part), dv.astype(bf16).reshape(seqs * total_len, part)], 1
    )
    d_qkv = after(d_qkv, *gu_done[-1])
    x_share = against(d_qkv, w_qkv).astype(bf16).reshape(seqs, size, local_len, width)
    x_share = [
        lax.dynamic_index_in_dim(x_share, lax.rem(here + size - o, size), 1, keepdims=False).reshape(rows, width)
        for o in range(size)
    ]
    got = next_one(x_share[1], "seq")
    for o in range(2, size):
        got = next_one((x_share[o].astype(f32) + got.astype(f32)).astype(bf16), "seq")
    d_tokens = d_hidden + x_share[0].astype(f32) + got.astype(f32)
    cube_qkv = CubeScatter(halves_of(split_grad(split_columns(x_all), d_qkv)))
    for _ in range(cube_qkv.steps):
        cube_qkv.step()
    d_w_qkv = jnp.concatenate(cube_qkv.totals, 1).astype(bf16)
    d_w_qkv = in_order(exchange(d_w_qkv.reshape(size, own_rows, 3 * part), "seq"), "seq")
    d_w_qkv = d_w_qkv.reshape(size, own_rows, 3, part).transpose(2, 1, 0, 3).reshape(3, own_rows, width).astype(f32)

    d_gain_qk = lax.dynamic_update_slice_in_dim(
        jnp.zeros((2, width), f32), d_gain_qk.reshape(2, part), here * part, 1
    )
    d_gains = scatter_small(jnp.concatenate([d_gain_qk, d_gain_attn[None], d_gain_ffn[None]], 0))
    return (
        out,
        d_tokens.reshape(tokens.shape),
        d_w_qkv[0],
        d_w_qkv[1],
        d_w_qkv[2],
        d_w_out,
        d_gains[0],
        d_gains[1],
        d_gains[2],
        d_gu[0],
        d_gu[1],
        d_down,
        d_gains[3],
    )


def solution(mesh):
    rows = P("dp", "seq", None)
    mat = P(("dp", "seq"), None)
    vec = P(("dp", "seq"))
    in_specs = (rows, P("dp", None), mat, mat, mat, mat, vec, vec, vec, mat, mat, mat, vec, rows)
    out_specs = (rows, rows, mat, mat, mat, mat, vec, vec, vec, mat, mat, mat, vec)
    return jax.shard_map(local, mesh=mesh, in_specs=in_specs, out_specs=out_specs, check_vma=False)
```

```python
import functools

import jax
import jax.numpy as jnp
from jax import lax
from jax.experimental import pallas as pl
from jax.experimental.pallas import tpu as pltpu
from jax.sharding import PartitionSpec as P

H = 16
HD = 128
DOCS = 4

epsilon = 1e-06
rope_base = 500000.0
masked_score = -1e30
bf16 = jnp.bfloat16
f32 = jnp.float32


def product(left, right):
    return jnp.dot(left, right, preferred_element_type=f32)


def against(left, right):
    return lax.dot_general(left, right, (((1,), (1,)), ((), ())), preferred_element_type=f32)


def weight_grad(left, right):
    return lax.dot_general(left, right, (((0,), (0,)), ((), ())), preferred_element_type=f32)


def rms_scale(values):
    return lax.rsqrt(jnp.mean(values * values, -1, keepdims=True) + epsilon)


def norm_back(values, scale_rows, grad_vals):
    return scale_rows * grad_vals - values * scale_rows**3 * jnp.mean(
        grad_vals * values, -1, keepdims=True
    )


def positions(seg_ids):
    doc_ids = jnp.arange(DOCS, dtype=jnp.int32)
    starts = jnp.sum((seg_ids[..., None, :] < doc_ids[:, None]).astype(jnp.int32), -1)
    one_hot = (seg_ids[..., None] == doc_ids).astype(jnp.int32)
    token_start = jnp.sum(one_hot * starts[..., None, :], axis=-1)
    return jnp.arange(seg_ids.shape[-1], dtype=jnp.int32) - token_start


def rope_tables(position_ids):
    freqs = rope_base ** (-jnp.arange(HD // 2, dtype=f32) * 2.0 / HD)
    angles = position_ids.astype(f32)[..., None] * freqs
    cosine = jnp.cos(angles)
    sine_tab = jnp.sin(angles)
    return (
        jnp.concatenate([cosine, cosine], -1),
        jnp.concatenate([sine_tab, sine_tab], -1),
    )


def contract(left, right, left_dim, right_dim):
    return lax.dot_general(left, right, (((left_dim,), (right_dim,)), ((), ())), preferred_element_type=f32)


def vmem(shape, index=None):
    return pl.BlockSpec(shape, index or (lambda *_: (0,) * len(shape)))


def kernel_params(grid=0):
    return pltpu.CompilerParams(vmem_limit_bytes=48 * 2**20)


def relayout_body(moves, count, *refs):
    ins, outs = refs[:count], refs[count:]
    for (src, src_row, src_col), (dst, dst_row, dst_col), (rows, cols) in moves():
        outs[dst][pl.ds(dst_row, rows), pl.ds(dst_col, cols)] = ins[src][
            pl.ds(src_row, rows), pl.ds(src_col, cols)
        ].astype(outs[dst].dtype)


def relayout(arrays, shapes, dtype, moves):
    outs = [jax.ShapeDtypeStruct(shape, dtype) for shape in shapes]
    size = sum(a.size * a.dtype.itemsize for a in [*arrays, *outs])
    return pl.pallas_call(
        functools.partial(relayout_body, moves, len(arrays)),
        in_specs=[vmem(a.shape) for a in arrays],
        out_specs=[vmem(o.shape) for o in outs],
        out_shape=outs,
        compiler_params=kernel_params(),
        cost_estimate=pl.CostEstimate(flops=0, bytes_accessed=size, transcendentals=0),
    )(*arrays)


def turned(values):
    lane = lax.broadcasted_iota(jnp.int32, values.shape, 1)
    rolled = pltpu.roll(values, HD // 2, 1)
    return jnp.where(lane < HD // 2, -rolled, rolled)


def query_key_body(width, raw_ref, squares_ref, cos_ref, sin_ref, gain_ref, q_ref, k_ref, v_ref):
    part = q_ref.shape[1]
    scales = lax.rsqrt(squares_ref[...] / width + epsilon)
    for which, out in enumerate((q_ref, k_ref)):
        for first in range(0, part, HD):
            gain = gain_ref[which : which + 1, first : first + HD]
            unit = raw_ref[:, which * part + first : which * part + first + HD] * scales[:, which : which + 1] * gain
            out[:, first : first + HD] = (unit * cos_ref[...] + turned(unit) * sin_ref[...]).astype(bf16)
    v_ref[...] = raw_ref[:, 2 * part :].astype(bf16)


def query_key(raw, squares, cosine, sine_tab, gains, width):
    tokens, part = raw.shape[0], raw.shape[1] // 3
    block = min(256, tokens)
    shape = jax.ShapeDtypeStruct((tokens, part), bf16)

    def by_rows(cols):
        return vmem((block, cols), lambda at: (at, 0))

    return pl.pallas_call(
        functools.partial(query_key_body, width),
        grid=(tokens // block,),
        in_specs=[by_rows(3 * part), by_rows(2), by_rows(HD), by_rows(HD), vmem(gains.shape)],
        out_specs=[by_rows(part)] * 3,
        out_shape=[shape] * 3,
        compiler_params=kernel_params(),
    )(raw, squares, cosine, sine_tab, gains)


def key_weights(query, key, seg_query, seg_key, first, count):
    scores = contract(key, query, 1, 1) * HD ** (-0.5)
    shape = scores.shape
    allowed = (seg_key == seg_query) & (
        lax.broadcasted_iota(jnp.int32, shape, 0) <= first + lax.broadcasted_iota(jnp.int32, shape, 1)
    )
    scores = jnp.where(allowed, scores, masked_score)
    expos = jnp.exp(scores - jnp.max(scores, 0, keepdims=True))
    return expos * (1.0 / jnp.sum(expos, 0, keepdims=True))


def attend_body(blocks, q_ref, k_ref, v_ref, seg_q_ref, seg_k_ref, out_ref):
    rows = q_ref.shape[0]
    for at in range(blocks):
        seen = (at + 1) * rows

        @pl.when(pl.program_id(1) == at)
        def _():
            probs = key_weights(
                q_ref[...], k_ref[:seen], seg_q_ref[...], seg_k_ref[:seen], at * rows, seen
            ).astype(bf16)
            out_ref[...] = contract(probs, v_ref[:seen], 0, 0).astype(bf16)


def attention_specs(tokens, block):
    by_query = vmem((block, HD), lambda head, at: (at, head))
    by_head = vmem((tokens, HD), lambda head, at: (0, head))
    return by_query, by_head, [vmem((1, block), lambda head, at: (0, at)), vmem((tokens, 1))]


def attend(query, key, value, seg_ids):
    tokens, part = query.shape
    block = min(256, tokens)
    by_query, by_head, segs = attention_specs(tokens, block)
    return pl.pallas_call(
        functools.partial(attend_body, tokens // block),
        grid=(part // HD, tokens // block),
        in_specs=[by_query, by_head, by_head, *segs],
        out_specs=by_query,
        out_shape=jax.ShapeDtypeStruct(query.shape, bf16),
        compiler_params=kernel_params(),
    )(query, key, value, seg_ids[None, :], seg_ids[:, None])


def attend_back_body(
    blocks, q_ref, k_ref, v_ref, g_ref, seg_q_ref, seg_k_ref, dq_ref, dk_ref, dv_ref, dk_sum, dv_sum
):
    rows = q_ref.shape[0]
    scale = HD ** (-0.5)
    for at in range(blocks):
        seen = (at + 1) * rows

        @pl.when(pl.program_id(1) == at)
        def _():
            query, grad = q_ref[...], g_ref[...]
            probs = key_weights(query, k_ref[:seen], seg_q_ref[...], seg_k_ref[:seen], at * rows, seen)
            d_probs = contract(v_ref[:seen], grad, 1, 1)
            inner = jnp.sum(probs * d_probs, 0, keepdims=True)
            d_scores = (probs * (d_probs - inner)).astype(bf16)
            dq_ref[...] = (contract(d_scores, k_ref[:seen], 0, 0) * scale).astype(bf16)
            d_key = contract(d_scores, query, 1, 0) * scale
            d_value = contract(probs.astype(bf16), grad, 1, 0)
            old = seen - rows
            dk_sum[old:seen] = d_key[old:]
            dv_sum[old:seen] = d_value[old:]
            if at:
                dk_sum[:old] += d_key[:old]
                dv_sum[:old] += d_value[:old]
            if at == blocks - 1:
                dk_ref[...] = dk_sum[...].astype(bf16)
                dv_ref[...] = dv_sum[...].astype(bf16)


def attend_back(query, key, value, grad, seg_ids):
    tokens, part = query.shape
    block = min(256, tokens)
    by_query, by_head, segs = attention_specs(tokens, block)
    shape = jax.ShapeDtypeStruct(query.shape, bf16)
    return pl.pallas_call(
        functools.partial(attend_back_body, tokens // block),
        grid=(part // HD, tokens // block),
        in_specs=[by_query, by_head, by_head, by_query, *segs],
        out_specs=[by_query, by_head, by_head],
        out_shape=[shape] * 3,
        scratch_shapes=[pltpu.VMEM((tokens, HD), f32)] * 2,
        compiler_params=kernel_params(),
    )(query, key, value, grad, seg_ids[None, :], seg_ids[:, None])


def rope_back(grad, cosine, sine_tab):
    return grad * cosine - turned(grad * sine_tab)


def unrope_body(width, dq_ref, dk_ref, raw_ref, squares_ref, cos_ref, sin_ref, gain_ref, dots_ref, gains_ref):
    part = dq_ref.shape[1]
    scales = lax.rsqrt(squares_ref[...] / width + epsilon)

    @pl.when(pl.program_id(0) == 0)
    def _():
        gains_ref[...] = jnp.zeros_like(gains_ref)

    for which, ref in enumerate((dq_ref, dk_ref)):
        dots = 0.0
        for first in range(0, part, HD):
            raw = raw_ref[:, which * part + first : which * part + first + HD]
            grad = rope_back(ref[:, first : first + HD].astype(f32), cos_ref[...], sin_ref[...])
            both = grad * raw
            gain = gain_ref[which : which + 1, first : first + HD]
            dots = dots + jnp.sum(both * gain, 1, keepdims=True)
            gains_ref[which : which + 1, first : first + HD] += jnp.sum(
                both * scales[:, which : which + 1], 0, keepdims=True
            )
        dots_ref[:, which : which + 1] = dots


def unrope(d_query, d_key, raw, squares, cosine, sine_tab, gains, width):
    tokens, part = d_query.shape
    block = min(256, tokens)

    def by_rows(cols):
        return vmem((block, cols), lambda at: (at, 0))

    return pl.pallas_call(
        functools.partial(unrope_body, width),
        grid=(tokens // block,),
        in_specs=[by_rows(part)] * 2
        + [by_rows(3 * part), by_rows(2), by_rows(HD), by_rows(HD), vmem(gains.shape)],
        out_specs=[by_rows(2), vmem((2, part))],
        out_shape=[jax.ShapeDtypeStruct((tokens, 2), f32), jax.ShapeDtypeStruct((2, part), f32)],
        compiler_params=kernel_params(),
    )(d_query, d_key, raw, squares, cosine, sine_tab, gains)


def raw_grad_body(width, dq_ref, dk_ref, dv_ref, raw_ref, squares_ref, dots_ref, cos_ref, sin_ref, gain_ref, out_ref):
    part = dq_ref.shape[1]
    scales = lax.rsqrt(squares_ref[...] / width + epsilon)
    cubes = scales * scales * scales * dots_ref[...] / width
    for which, ref in enumerate((dq_ref, dk_ref)):
        for first in range(0, part, HD):
            at = slice(which * part + first, which * part + first + HD)
            grad = rope_back(ref[:, first : first + HD].astype(f32), cos_ref[...], sin_ref[...])
            grad = grad * gain_ref[which : which + 1, first : first + HD]
            out_ref[:, at] = (
                scales[:, which : which + 1] * grad - raw_ref[:, at] * cubes[:, which : which + 1]
            ).astype(bf16)
    out_ref[:, 2 * part :] = dv_ref[...]


def raw_grad(d_query, d_key, d_value, raw, squares, dots, cosine, sine_tab, gains, width):
    tokens, part = d_query.shape
    block = min(256, tokens)

    def by_rows(cols):
        return vmem((block, cols), lambda at: (at, 0))

    return pl.pallas_call(
        functools.partial(raw_grad_body, width),
        grid=(tokens // block,),
        in_specs=[by_rows(part)] * 3
        + [by_rows(3 * part), by_rows(2), by_rows(2), by_rows(HD), by_rows(HD), vmem(gains.shape)],
        out_specs=by_rows(3 * part),
        out_shape=jax.ShapeDtypeStruct((tokens, 3 * part), bf16),
        compiler_params=kernel_params(),
    )(d_query, d_key, d_value, raw, squares, dots, cosine, sine_tab, gains)


def together(*trees):
    return lax.optimization_barrier(trees)


def next_one(block, axis):
    size = lax.axis_size(axis)
    return lax.ppermute(block, axis, [(i, (i + 1) % size) for i in range(size)])


def flipped(block, bit):
    size = lax.axis_size("dp")
    return lax.ppermute(block, "dp", [(i, i ^ bit) for i in range(size)])


def exchange(blocks, axis):
    size, here = lax.axis_size(axis), lax.axis_index(axis)
    got = []
    for step in range(size):
        block = lax.dynamic_index_in_dim(blocks, lax.rem(here + step, size), 0, keepdims=False)
        if step:
            block = lax.ppermute(block, axis, [(i, (i + step) % size) for i in range(size)])
        got.append(block)
    return got


def send_ahead(blocks, axis):
    size = lax.axis_size(axis)
    return [blocks[0]] + [
        lax.ppermute(blocks[step], axis, [(i, (i + step) % size) for i in range(size)]) for step in range(1, size)
    ]


def share_out(block, axis):
    size = lax.axis_size(axis)
    return [block] + [
        lax.ppermute(block, axis, [(i, (i + step) % size) for i in range(size)]) for step in range(1, size)
    ]


def assemble_body(parts, places, count, *refs):
    pieces, out, held, in_sems, out_sems = refs[:count], *refs[count:]
    reads, writes, first = [], [], 0
    for at, ((which, start, rows), place) in enumerate(zip(parts, places())):
        here = held.at[pl.ds(first, rows)]
        reads.append(pltpu.make_async_copy(pieces[which].at[pl.ds(start, rows)], here, in_sems.at[at]))
        writes.append(pltpu.make_async_copy(here, out.at[pl.ds(place, rows)], out_sems.at[at]))
        first += rows
    for read in reads:
        read.start()
    for read, write in zip(reads, writes):
        read.wait()
        write.start()
    for write in writes:
        write.wait()


def assemble(pieces, parts, places):
    shape = (sum(rows for _, _, rows in parts), pieces[0].shape[1])
    anywhere = pl.BlockSpec(memory_space=pl.ANY)
    sems = pltpu.SemaphoreType.DMA((len(parts),))
    size = shape[0] * shape[1] * pieces[0].dtype.itemsize
    return pl.pallas_call(
        functools.partial(assemble_body, parts, places, len(pieces)),
        in_specs=[anywhere] * len(pieces),
        out_specs=anywhere,
        out_shape=jax.ShapeDtypeStruct(shape, pieces[0].dtype),
        scratch_shapes=[pltpu.VMEM(shape, pieces[0].dtype), sems, sems],
        compiler_params=pltpu.CompilerParams(vmem_limit_bytes=size + 2**20),
        cost_estimate=pl.CostEstimate(flops=0, bytes_accessed=2 * size, transcendentals=0),
    )(*pieces)


def stacked(pieces, parts=None):
    parts = parts or [(at, 0, p.shape[0]) for at, p in enumerate(pieces)]
    places = [sum(rows for _, _, rows in parts[:at]) for at in range(len(parts))]
    return assemble(pieces, parts, lambda: places)


def in_order(slots, axis, first=0, rows=None):
    size, rows = len(slots), rows or slots[0].shape[0]

    def places():
        here = lax.axis_index(axis)
        return [pl.multiple_of(lax.rem(here + (size - back), size) * rows, rows) for back in range(size)]

    return assemble(slots, [(at, first, rows) for at in range(size)], places)


def cube_bits():
    bits = [1 << b for b in range(1, (lax.axis_size("dp") - 1).bit_length())]
    return bits, bits[1:] + bits[:1]


class CubeGather:
    def __init__(self, pair, core=False):
        self.arrays = [[block] for block in pair]
        self.masks = [[[0]] for _ in pair]
        self.orders = [list(bits) + [1] * core for bits in cube_bits()]
        self.new = []

    def step(self):
        for at, arrays in enumerate(self.arrays):
            if len(arrays) > 1:
                self.arrays[at] = [stacked(arrays)]
                self.masks[at] = [sum(self.masks[at], [])]
        self.new = [flipped(arrays[0], order[0]) for arrays, order in zip(self.arrays, self.orders)]

    def set(self, new):
        for at, block in enumerate(new):
            bit = self.orders[at].pop(0)
            self.arrays[at].append(block)
            self.masks[at].append([m ^ bit for m in self.masks[at][0]])
        self.new = []

    def finish(self):
        self.set(self.new)
        while self.orders[0]:
            self.step()
            self.set(self.new)


def cube_join(cube, firsts, rows, fold=1):
    pieces, parts, where = [], [], []
    for (own, first), arrays, masks in zip(firsts, cube.arrays, cube.masks):
        step = arrays[0].shape[0] // len(masks[0])
        for array, blocks in zip(arrays, masks):
            for at, mask in enumerate(blocks):
                parts.append((len(pieces), at * step, step))
                where.append((own ^ mask, first))
            pieces.append(array)

    def places():
        here = lax.axis_index("dp")
        return [pl.multiple_of((here ^ mask) // fold * rows + first, step) for mask, first in where]

    return assemble(pieces, parts, places)


class CubeScatter:
    def __init__(self, pair, core=False):
        self.totals, self.got = list(pair), None
        self.orders = [[1] * core + list(bits) for bits in cube_bits()]
        self.dims = [sorted(order, reverse=True) for order in self.orders]

    def add(self):
        if self.got:
            self.totals = [t.astype(f32) + g.astype(f32) for t, g in zip(self.totals, self.got)]
        self.got = None
        return self.totals

    def step(self):
        self.add()
        got = []
        for which, total in enumerate(self.totals):
            bit = self.orders[which].pop(0)
            at = self.dims[which].index(bit)
            self.dims[which].remove(bit)
            mine = (lax.axis_index("dp") // bit) % 2
            away = lax.dynamic_index_in_dim(total, 1 - mine, at, keepdims=False).astype(bf16)
            got.append(flipped(away, bit))
            self.totals[which] = lax.dynamic_index_in_dim(total, mine, at, keepdims=False)
        self.got = got

    def finish(self):
        while self.orders[0]:
            self.step()
        return jnp.concatenate(self.add(), 1)


def column_halves(grad, core):
    bits = (lax.axis_size("dp") - 1).bit_length() - (not core)
    cut = grad.shape[1] // 2
    shape = (2,) * bits + (-1, cut)
    return [grad[:, :cut].reshape(shape), grad[:, cut:].reshape(shape)]


def gather_small(block):
    size, here = lax.axis_size("seq"), lax.axis_index("seq")
    joined = jnp.zeros((size,) + block.shape, block.dtype)
    for back, slot in enumerate(share_out(block, "seq")):
        joined = lax.dynamic_update_index_in_dim(joined, slot, lax.rem(here + size - back, size), 0)
    block = joined.transpose(1, 0, 2).reshape(block.shape[0], -1)
    here, wide = lax.axis_index("dp"), block.shape[1]
    table = {0: block}
    for bit in cube_bits()[0] + [1]:
        table.update({m ^ bit: flipped(v, bit) for m, v in table.items()})
    joined = jnp.zeros((block.shape[0], wide * len(table)), block.dtype)
    for mask, piece in table.items():
        joined = lax.dynamic_update_slice_in_dim(joined, piece, (here ^ mask) * wide, 1)
    return joined


def scatter_small(values):
    copies, size, here = lax.axis_size("dp"), lax.axis_size("seq"), lax.axis_index("dp")
    blocks = values.reshape(values.shape[0], copies, size, -1).transpose(2, 1, 0, 3)
    total = sum(exchange(blocks, "seq"))
    for bit in reversed([1] + cube_bits()[0]):
        total = total.reshape((2, total.shape[0] // 2) + total.shape[1:])
        mine = (here // bit) % 2
        away = lax.dynamic_index_in_dim(total, 1 - mine, 0, keepdims=False)
        total = lax.dynamic_index_in_dim(total, mine, 0, keepdims=False) + flipped(away, bit)
    return total[0]


def small_sum(values, axis):
    return sum(share_out(values.reshape(-1), axis)).reshape(values.shape)


def local(
    tokens,
    segments,
    w_query,
    w_key,
    w_value,
    w_out,
    g_query,
    g_key,
    g_attn,
    w_gate,
    w_up,
    w_down,
    g_ffn,
    d_out,
):
    seqs, local_len, width = tokens.shape
    rows = seqs * local_len
    copies, size = lax.axis_size("dp"), lax.axis_size("seq")
    here = lax.axis_index("seq")
    total_len = size * local_len
    part = width // size
    heads = H // size
    own_rows = w_gate.shape[0]
    ff_width = w_gate.shape[1]
    ff_part = ff_width // size
    ff_own = w_down.shape[0]
    tok_rows = tokens.reshape(rows, width)

    side = width // copies
    pairs = copies // 2
    ff_half = ff_part // 2
    slots = range(size)

    def before(back):
        return lax.rem(lax.axis_index("seq") + (size - back), size)

    def behind(ahead):
        return lax.rem(lax.axis_index("seq") + ahead, size)

    def ff_column(pair, other, seq_at):
        return pl.multiple_of(((pair * 2 + (lax.rem(lax.axis_index("dp"), 2) ^ other)) * size + seq_at) * ff_own, ff_own)

    def ff_pack(weight):
        if ff_own % 128:
            core = lax.rem(lax.axis_index("dp"), 2)
            blocks = weight.reshape(own_rows, pairs, 2, size, ff_own).transpose(2, 3, 0, 1, 4)
            blocks = blocks.reshape(2, size, own_rows, ff_half)
            blocks = jnp.concatenate(
                [lax.dynamic_index_in_dim(blocks, c, 0, keepdims=False) for c in (core, 1 - core)], 1
            )
            return [lax.dynamic_index_in_dim(blocks, behind(ahead), 0, keepdims=False) for ahead in slots]
        return relayout(
            [weight],
            [(2 * own_rows, ff_half)] * size,
            bf16,
            lambda: [
                ((0, 0, ff_column(pair, other, behind(ahead))), (ahead, other * own_rows, pair * ff_own), (own_rows, ff_own))
                for ahead in slots
                for other in (0, 1)
                for pair in range(pairs)
            ],
        )

    def ff_unpack(got):
        if ff_own % 128:
            core = lax.rem(lax.axis_index("dp"), 2)
            joined = in_order(got, "seq").reshape(size, 2, own_rows, pairs, ff_own)
            joined = jnp.where(core == 0, joined, joined[:, ::-1])
            return joined.transpose(2, 3, 1, 0, 4).reshape(own_rows, ff_width).astype(f32)
        return relayout(
            got,
            [(own_rows, ff_width)],
            f32,
            lambda: [
                ((back, other * own_rows, pair * ff_own), (0, 0, ff_column(pair, other, before(back))), (own_rows, ff_own))
                for back in slots
                for other in (0, 1)
                for pair in range(pairs)
            ],
        )[0]

    def ff_pair(got):
        mine, away = [in_order(got, "seq", first, own_rows) for first in (0, own_rows)]
        return [mine, flipped(away, 1)]

    def two_parts(got):
        joined = in_order(got, "seq")
        return [joined[: side // 2], joined[side // 2 :]]

    def part_column(seq_at):
        return pl.multiple_of(seq_at * part, part)

    def part_row(seq_at):
        return pl.multiple_of(seq_at * rows, rows)

    gains, w_down_own = together(gather_small(jnp.stack([g_query, g_key, g_attn, g_ffn], 0)), w_down)
    gains = gains.astype(f32)
    qkv_send = relayout(
        [w_query, w_key, w_value],
        [(own_rows, 3 * part)] * size,
        bf16,
        lambda: [
            ((which, 0, part_column(behind(ahead))), (ahead, 0, which * part), (own_rows, part))
            for ahead in slots
            for which in range(3)
        ],
    )
    qkv_got = send_ahead(qkv_send, "seq")
    cube_down = CubeGather([w_down_own[: ff_own // 2], w_down_own[ff_own // 2 :]])
    cube_down.step()
    gate_send, up_send = ff_pack(w_gate), ff_pack(w_up)
    qkv_got, new, gate_send, x_own, w_out_own = together(qkv_got, cube_down.new, gate_send, tok_rows, w_out)
    cube_down.set(new)

    gate_got = send_ahead(gate_send, "seq")
    cube_qkv = CubeGather(two_parts(qkv_got), core=True)
    cube_qkv.step()
    gate_got, new, x_own = together(gate_got, cube_qkv.new, x_own)
    cube_qkv.set(new)

    x_slots = [x_own]
    cube_qkv.step()
    cube_gate = CubeGather(ff_pair(gate_got))
    cube_gate.step()
    for at in range(size - 1):
        x_next = next_one(x_slots[-1], "seq")
        if at == 0:
            x_next, new, more = together(x_next, cube_qkv.new, cube_gate.new)
            cube_qkv.set(new)
            cube_gate.set(more)
            cube_qkv.step()
            cube_gate.step()
        elif at == 1:
            x_next, new, more = together(x_next, cube_qkv.new, cube_gate.new)
            cube_qkv.set(new)
            cube_gate.set(more)
            cube_down.step()
        x_slots.append(x_next)
    cube_qkv.finish()
    cube_gate.finish()
    w_qkv = cube_join(cube_qkv, ((0, 0), (0, side // 2)), side)

    x_all = in_order(x_slots, "seq")
    gain_attn, gain_ffn = gains[2], gains[3]
    gain_qk = lax.dynamic_slice_in_dim(gains[:2], here * part, part, 1)
    cosine, sine_tab = rope_tables(positions(segments).reshape(total_len))
    qkv = product(x_all, w_qkv)
    squares = jnp.stack([jnp.sum(jnp.square(qkv[:, first : first + part]), -1) for first in (0, part)], 0)
    squares = small_sum(squares, "seq")
    squares, new, w_out_own, up_send = together(squares, cube_down.new, w_out_own, up_send)
    cube_down.set(new)
    out_got = share_out(w_out_own, "seq")
    w_gate_part = cube_join(cube_gate, ((0, 0), (1, 0)), side)
    squares = squares.T
    query, key, value = query_key(qkv, squares, cosine, sine_tab, gain_qk, width)
    query, out_got, w_gate_part = together(query, out_got, w_gate_part)
    cube_out = CubeGather(two_parts(out_got), core=True)
    cube_out.step()
    up_got = send_ahead(up_send, "seq")
    seg_ids = segments.reshape(total_len)
    attended = attend(query, key, value, seg_ids)
    attended = relayout(
        [attended],
        [(rows, part)] * size,
        bf16,
        lambda: [((0, part_row(behind(ahead)), 0), (ahead, 0, 0), (rows, part)) for ahead in slots],
    )
    attended, up_got, new = together(attended, up_got, cube_out.new)
    cube_out.set(new)
    attended = send_ahead(attended, "seq")
    cube_out.step()
    cube_up = CubeGather(ff_pair(up_got))
    cube_down.finish()
    w_down_part = cube_join(cube_down, ((0, 0), (0, ff_own // 2)), ff_own, 2)
    attended, new, w_down_part = together(attended, cube_out.new, w_down_part)
    cube_out.set(new)
    cube_out.finish()
    cube_up.step()
    w_out_all = cube_join(cube_out, ((0, 0), (0, side // 2)), side)
    attended = relayout(
        attended,
        [(rows, width)],
        bf16,
        lambda: [((back, 0, 0), (0, 0, part_column(before(back))), (rows, part)) for back in slots],
    )[0]

    cube_up.finish()
    w_up_part = cube_join(cube_up, ((0, 0), (1, 0)), side)
    a_proj = product(attended, w_out_all)
    a_scale = rms_scale(a_proj)
    hidden = tok_rows.astype(f32) + a_proj * a_scale * gain_attn

    def ring(block, work, last=lambda: (), beside=lambda early: ()):
        got, own = None, None
        for at in range(size):
            later = next_one(block, "seq") if at < size - 1 else None
            share = work(stacked([block, flipped(block, 1)]))
            if later is None:
                share, early = together(share, last())
            share, away = share[:rows], share[rows:].astype(bf16)
            if later is not None:
                later, share, away = together(later, share, away)
            share = share + flipped(away, 1).astype(f32)
            if at == 0:
                own = share
            else:
                if at > 1:
                    share = share + got.astype(f32)
                got = next_one(share.astype(bf16), "seq")
            block = later
        got, extra = together(got, beside(early))
        return own + got.astype(f32), extra

    h_slots, gates, ups, inners = [], [], [], []

    def forward(h_low):
        gate = product(h_low, w_gate_part)
        up = product(h_low, w_up_part)
        inner = (jax.nn.silu(gate) * up).astype(bf16)
        h_slots.append(h_low)
        gates.append(gate)
        ups.append(up)
        inners.append(inner)
        return product(inner, w_down_part)

    m_proj, _ = ring(hidden.astype(bf16), forward)
    m_scale = rms_scale(m_proj)
    out = (hidden + m_proj * m_scale * gain_ffn).astype(bf16).reshape(tokens.shape)
    grad_out = d_out.reshape(rows, width).astype(f32)
    d_gain_ffn = jnp.sum(grad_out * m_proj * m_scale, 0)
    dm_low = norm_back(m_proj, m_scale, grad_out * gain_ffn).astype(bf16)
    dms, d_gates, d_ups = [], [], []

    def backward(dm_slot):
        at = len(dms)
        gate, up = gates[at], ups[at]
        d_inner = against(dm_slot, w_down_part)
        sigmoid_gate = jax.nn.sigmoid(gate)
        d_gate = (d_inner * up * sigmoid_gate * (1.0 + gate * (1.0 - sigmoid_gate))).astype(bf16)
        d_up = (d_inner * (gate * sigmoid_gate)).astype(bf16)
        dms.append(dm_slot)
        d_gates.append(d_gate)
        d_ups.append(d_up)
        return against(d_gate, w_gate_part) + against(d_up, w_up_part)

    def down_grad():
        return weight_grad(stacked(inners), stacked(dms)).astype(bf16)

    def grads(d_down):
        cube = CubeScatter(column_halves(d_down, False))
        cube.step()
        sums.append(cube)
        h_all = stacked(h_slots)
        d_gate = weight_grad(h_all, stacked(d_gates)).astype(bf16)
        d_up = weight_grad(h_all, stacked(d_ups)).astype(bf16)
        return d_gate, d_up, cube.got

    sums = []

    d_sum, (d_gate, d_up, got) = ring(dm_low, backward, down_grad, grads)
    cube_down = sums[0]
    cube_down.got = got

    def ff_rows(total):
        core = lax.rem(lax.axis_index("dp"), 2)
        total = total.astype(bf16).reshape(2, side, ff_half)
        mine, away = [lax.dynamic_index_in_dim(total, c, 0, keepdims=False) for c in (core, 1 - core)]
        away = flipped(away, 1)

        def moves():
            return [
                ((which, pl.multiple_of(behind(ahead) * own_rows, own_rows), 0), (ahead, which * own_rows, 0), (own_rows, ff_half))
                for ahead in slots
                for which in (0, 1)
            ]

        return relayout([mine, away], [(2 * own_rows, ff_half)] * size, bf16, moves)

    cube_down.step()
    cube_gate = CubeScatter(column_halves(d_gate, False))
    cube_gate.step()
    d_hidden = grad_out + d_sum
    d_gain_attn = jnp.sum(d_hidden * a_proj * a_scale, 0)
    da_low = norm_back(a_proj, a_scale, d_hidden * gain_attn).astype(bf16)
    d_attended = against(da_low, w_out_all).astype(bf16)
    d_attended = relayout(
        [d_attended],
        [(rows, part)] * size,
        bf16,
        lambda: [((0, 0, part_column(behind(ahead))), (ahead, 0, 0), (rows, part)) for ahead in slots],
    )
    d_attended = send_ahead(d_attended, "seq")
    d_w_out = weight_grad(attended, da_low).astype(bf16)
    d_attended, cube_gate.got, cube_down.got, d_w_out = together(d_attended, cube_gate.got, cube_down.got, d_w_out)
    d_down = cube_down.finish()
    cube_gate.step()
    cube_up = CubeScatter(column_halves(d_up, False))
    cube_up.step()
    d_attended = in_order(d_attended, "seq")

    d_query, d_key, d_value = attend_back(query, key, value, d_attended, seg_ids)
    d_query, cube_gate.got, cube_up.got = together(d_query, cube_gate.got, cube_up.got)
    cube_up.step()
    dots, d_gain_qk = unrope(d_query, d_key, qkv, squares, cosine, sine_tab, gain_qk, width)
    dots = small_sum(dots.T, "seq")
    gate_send = ff_rows(cube_gate.finish())
    dots, gate_send, cube_up.got = together(dots, gate_send, cube_up.got)
    gate_got = send_ahead(gate_send, "seq")
    d_qkv = raw_grad(d_query, d_key, d_value, qkv, squares, dots.T, cosine, sine_tab, gain_qk, width)
    up_send = ff_rows(cube_up.finish())
    d_slots = relayout(
        [d_qkv],
        [(rows, 3 * part)] * size,
        bf16,
        lambda: [((0, part_row(before(back)), 0), (back, 0, 0), (rows, 3 * part)) for back in slots],
    )
    cube_qkv = CubeScatter(column_halves(weight_grad(x_all, d_qkv).astype(bf16), True), core=True)
    cube_qkv.step()
    shares = [against(d_slots[back], w_qkv) for back in [*slots[1:], 0]]
    shares, gate_got, up_send, cube_qkv.got = together(shares, gate_got, up_send, cube_qkv.got)
    got = next_one(shares[0].astype(bf16), "seq")
    cube_qkv.step()
    up_got = send_ahead(up_send, "seq")
    got, cube_qkv.got, up_got = together(got, cube_qkv.got, up_got)
    cube_qkv.step()
    cube_out = CubeScatter(column_halves(d_w_out, True), core=True)
    cube_out.step()
    for back in range(2, size):
        got = next_one((shares[back - 1] + got.astype(f32)).astype(bf16), "seq")
        if back == 2:
            got, cube_qkv.got, cube_out.got = together(got, cube_qkv.got, cube_out.got)
            cube_out.step()
    d_w_qkv = cube_qkv.finish()
    d_w_out = cube_out.finish()
    d_tokens = d_hidden + shares[-1] + got.astype(f32)

    def row_blocks(total):
        wide = total.shape[1]
        return relayout(
            [total],
            [(own_rows, wide)] * size,
            bf16,
            lambda: [
                ((0, pl.multiple_of(behind(ahead) * own_rows, own_rows), 0), (ahead, 0, 0), (own_rows, wide))
                for ahead in slots
            ],
        )

    d_w_qkv = send_ahead(row_blocks(d_w_qkv), "seq")
    d_w_out = sum(g.astype(f32) for g in send_ahead(row_blocks(d_w_out), "seq"))
    d_w_qkv = relayout(
        d_w_qkv,
        [(own_rows, width)] * 3,
        f32,
        lambda: [
            ((back, 0, which * part), (which, 0, part_column(before(back))), (own_rows, part))
            for back in slots
            for which in range(3)
        ],
    )
    d_w_gate, d_w_up = ff_unpack(gate_got), ff_unpack(up_got)

    d_gain_qk = lax.dynamic_update_slice_in_dim(jnp.zeros((2, width), f32), d_gain_qk, here * part, 1)
    d_gains = scatter_small(jnp.concatenate([d_gain_qk, d_gain_attn[None], d_gain_ffn[None]], 0))
    return (
        out,
        d_tokens.reshape(tokens.shape),
        d_w_qkv[0],
        d_w_qkv[1],
        d_w_qkv[2],
        d_w_out,
        d_gains[0],
        d_gains[1],
        d_gains[2],
        d_w_gate,
        d_w_up,
        d_down,
        d_gains[3],
    )


def solution(mesh):
    rows = P("dp", "seq", None)
    mat = P(("dp", "seq"), None)
    vec = P(("dp", "seq"))
    in_specs = (rows, P("dp", None), mat, mat, mat, mat, vec, vec, vec, mat, mat, mat, vec, rows)
    out_specs = (rows, rows, mat, mat, mat, mat, vec, vec, vec, mat, mat, mat, vec)
    return jax.shard_map(local, mesh=mesh, in_specs=in_specs, out_specs=out_specs, check_vma=False)
```

```python
import functools

import jax
import jax.numpy as jnp
from jax import lax
from jax.experimental import pallas as pl
from jax.experimental.pallas import tpu as pltpu
from jax.sharding import PartitionSpec as P

H = 16
HD = 128
DOCS = 4

epsilon = 1e-06
rope_base = 500000.0
masked_score = -1e30
bf16 = jnp.bfloat16
f32 = jnp.float32


def product(left, right):
    return jnp.dot(left, right, preferred_element_type=f32)


def against(left, right):
    return lax.dot_general(left, right, (((1,), (1,)), ((), ())), preferred_element_type=f32)


def weight_grad(left, right):
    return lax.dot_general(left, right, (((0,), (0,)), ((), ())), preferred_element_type=f32)


def rms_scale(values):
    return lax.rsqrt(jnp.mean(values * values, -1, keepdims=True) + epsilon)


def norm_back(values, scale_rows, grad_vals):
    return scale_rows * grad_vals - values * scale_rows**3 * jnp.mean(
        grad_vals * values, -1, keepdims=True
    )


def positions(seg_ids):
    doc_ids = jnp.arange(DOCS, dtype=jnp.int32)
    starts = jnp.sum((seg_ids[..., None, :] < doc_ids[:, None]).astype(jnp.int32), -1)
    one_hot = (seg_ids[..., None] == doc_ids).astype(jnp.int32)
    token_start = jnp.sum(one_hot * starts[..., None, :], axis=-1)
    return jnp.arange(seg_ids.shape[-1], dtype=jnp.int32) - token_start


def rope_tables(position_ids):
    freqs = rope_base ** (-jnp.arange(HD // 2, dtype=f32) * 2.0 / HD)
    angles = position_ids.astype(f32)[..., None] * freqs
    cosine = jnp.cos(angles)
    sine_tab = jnp.sin(angles)
    return (
        jnp.concatenate([cosine, cosine], -1),
        jnp.concatenate([sine_tab, sine_tab], -1),
    )


def contract(left, right, left_dim, right_dim):
    return lax.dot_general(left, right, (((left_dim,), (right_dim,)), ((), ())), preferred_element_type=f32)


def vmem(shape, index=None):
    return pl.BlockSpec(shape, index or (lambda *_: (0,) * len(shape)))


def kernel_params(grid=0):
    return pltpu.CompilerParams(vmem_limit_bytes=48 * 2**20)


def relayout_body(moves, count, *refs):
    ins, outs = refs[:count], refs[count:]
    for (src, src_row, src_col), (dst, dst_row, dst_col), (rows, cols) in moves():
        outs[dst][pl.ds(dst_row, rows), pl.ds(dst_col, cols)] = ins[src][
            pl.ds(src_row, rows), pl.ds(src_col, cols)
        ].astype(outs[dst].dtype)


def relayout(arrays, shapes, dtype, moves):
    outs = [jax.ShapeDtypeStruct(shape, dtype) for shape in shapes]
    size = sum(a.size * a.dtype.itemsize for a in [*arrays, *outs])
    return pl.pallas_call(
        functools.partial(relayout_body, moves, len(arrays)),
        in_specs=[vmem(a.shape) for a in arrays],
        out_specs=[vmem(o.shape) for o in outs],
        out_shape=outs,
        compiler_params=kernel_params(),
        cost_estimate=pl.CostEstimate(flops=0, bytes_accessed=size, transcendentals=0),
    )(*arrays)


def turned(values):
    lane = lax.broadcasted_iota(jnp.int32, values.shape, 1)
    rolled = pltpu.roll(values, HD // 2, 1)
    return jnp.where(lane < HD // 2, -rolled, rolled)


def query_key_body(width, raw_ref, squares_ref, cos_ref, sin_ref, gain_ref, q_ref, k_ref, v_ref):
    part = q_ref.shape[1]
    scales = lax.rsqrt(squares_ref[...] / width + epsilon)
    for which, out in enumerate((q_ref, k_ref)):
        for first in range(0, part, HD):
            gain = gain_ref[which : which + 1, first : first + HD]
            unit = raw_ref[:, which * part + first : which * part + first + HD] * scales[:, which : which + 1] * gain
            out[:, first : first + HD] = (unit * cos_ref[...] + turned(unit) * sin_ref[...]).astype(bf16)
    v_ref[...] = raw_ref[:, 2 * part :].astype(bf16)


def query_key(raw, squares, cosine, sine_tab, gains, width):
    tokens, part = raw.shape[0], raw.shape[1] // 3
    block = min(256, tokens)
    shape = jax.ShapeDtypeStruct((tokens, part), bf16)

    def by_rows(cols):
        return vmem((block, cols), lambda at: (at, 0))

    return pl.pallas_call(
        functools.partial(query_key_body, width),
        grid=(tokens // block,),
        in_specs=[by_rows(3 * part), by_rows(2), by_rows(HD), by_rows(HD), vmem(gains.shape)],
        out_specs=[by_rows(part)] * 3,
        out_shape=[shape] * 3,
        compiler_params=kernel_params(),
    )(raw, squares, cosine, sine_tab, gains)


def key_weights(query, key, seg_query, seg_key, first, count):
    scores = contract(key, query, 1, 1) * HD ** (-0.5)
    shape = scores.shape
    allowed = (seg_key == seg_query) & (
        lax.broadcasted_iota(jnp.int32, shape, 0) <= first + lax.broadcasted_iota(jnp.int32, shape, 1)
    )
    scores = jnp.where(allowed, scores, masked_score)
    expos = jnp.exp(scores - jnp.max(scores, 0, keepdims=True))
    return expos * (1.0 / jnp.sum(expos, 0, keepdims=True))


def attend_body(blocks, q_ref, k_ref, v_ref, seg_q_ref, seg_k_ref, out_ref):
    rows = q_ref.shape[0]
    for at in range(blocks):
        seen = (at + 1) * rows

        @pl.when(pl.program_id(1) == at)
        def _():
            probs = key_weights(
                q_ref[...], k_ref[:seen], seg_q_ref[...], seg_k_ref[:seen], at * rows, seen
            ).astype(bf16)
            out_ref[...] = contract(probs, v_ref[:seen], 0, 0).astype(bf16)


def attention_specs(tokens, block):
    by_query = vmem((block, HD), lambda head, at: (at, head))
    by_head = vmem((tokens, HD), lambda head, at: (0, head))
    return by_query, by_head, [vmem((1, block), lambda head, at: (0, at)), vmem((tokens, 1))]


def attend(query, key, value, seg_ids):
    tokens, part = query.shape
    block = min(256, tokens)
    by_query, by_head, segs = attention_specs(tokens, block)
    return pl.pallas_call(
        functools.partial(attend_body, tokens // block),
        grid=(part // HD, tokens // block),
        in_specs=[by_query, by_head, by_head, *segs],
        out_specs=by_query,
        out_shape=jax.ShapeDtypeStruct(query.shape, bf16),
        compiler_params=kernel_params(),
    )(query, key, value, seg_ids[None, :], seg_ids[:, None])


def attend_back_body(
    blocks, q_ref, k_ref, v_ref, g_ref, seg_q_ref, seg_k_ref, dq_ref, dk_ref, dv_ref, dk_sum, dv_sum
):
    rows = q_ref.shape[0]
    scale = HD ** (-0.5)
    for at in range(blocks):
        seen = (at + 1) * rows

        @pl.when(pl.program_id(1) == at)
        def _():
            query, grad = q_ref[...], g_ref[...]
            probs = key_weights(query, k_ref[:seen], seg_q_ref[...], seg_k_ref[:seen], at * rows, seen)
            d_probs = contract(v_ref[:seen], grad, 1, 1)
            inner = jnp.sum(probs * d_probs, 0, keepdims=True)
            d_scores = (probs * (d_probs - inner)).astype(bf16)
            dq_ref[...] = (contract(d_scores, k_ref[:seen], 0, 0) * scale).astype(bf16)
            d_key = contract(d_scores, query, 1, 0) * scale
            d_value = contract(probs.astype(bf16), grad, 1, 0)
            old = seen - rows
            dk_sum[old:seen] = d_key[old:]
            dv_sum[old:seen] = d_value[old:]
            if at:
                dk_sum[:old] += d_key[:old]
                dv_sum[:old] += d_value[:old]
            if at == blocks - 1:
                dk_ref[...] = dk_sum[...].astype(bf16)
                dv_ref[...] = dv_sum[...].astype(bf16)


def attend_back(query, key, value, grad, seg_ids):
    tokens, part = query.shape
    block = min(256, tokens)
    by_query, by_head, segs = attention_specs(tokens, block)
    shape = jax.ShapeDtypeStruct(query.shape, bf16)
    return pl.pallas_call(
        functools.partial(attend_back_body, tokens // block),
        grid=(part // HD, tokens // block),
        in_specs=[by_query, by_head, by_head, by_query, *segs],
        out_specs=[by_query, by_head, by_head],
        out_shape=[shape] * 3,
        scratch_shapes=[pltpu.VMEM((tokens, HD), f32)] * 2,
        compiler_params=kernel_params(),
    )(query, key, value, grad, seg_ids[None, :], seg_ids[:, None])


def rope_back(grad, cosine, sine_tab):
    return grad * cosine - turned(grad * sine_tab)


def unrope_body(width, dq_ref, dk_ref, raw_ref, squares_ref, cos_ref, sin_ref, gain_ref, dots_ref, gains_ref):
    part = dq_ref.shape[1]
    scales = lax.rsqrt(squares_ref[...] / width + epsilon)

    @pl.when(pl.program_id(0) == 0)
    def _():
        gains_ref[...] = jnp.zeros_like(gains_ref)

    for which, ref in enumerate((dq_ref, dk_ref)):
        dots = 0.0
        for first in range(0, part, HD):
            raw = raw_ref[:, which * part + first : which * part + first + HD]
            grad = rope_back(ref[:, first : first + HD].astype(f32), cos_ref[...], sin_ref[...])
            both = grad * raw
            gain = gain_ref[which : which + 1, first : first + HD]
            dots = dots + jnp.sum(both * gain, 1, keepdims=True)
            gains_ref[which : which + 1, first : first + HD] += jnp.sum(
                both * scales[:, which : which + 1], 0, keepdims=True
            )
        dots_ref[:, which : which + 1] = dots


def unrope(d_query, d_key, raw, squares, cosine, sine_tab, gains, width):
    tokens, part = d_query.shape
    block = min(256, tokens)

    def by_rows(cols):
        return vmem((block, cols), lambda at: (at, 0))

    return pl.pallas_call(
        functools.partial(unrope_body, width),
        grid=(tokens // block,),
        in_specs=[by_rows(part)] * 2
        + [by_rows(3 * part), by_rows(2), by_rows(HD), by_rows(HD), vmem(gains.shape)],
        out_specs=[by_rows(2), vmem((2, part))],
        out_shape=[jax.ShapeDtypeStruct((tokens, 2), f32), jax.ShapeDtypeStruct((2, part), f32)],
        compiler_params=kernel_params(),
    )(d_query, d_key, raw, squares, cosine, sine_tab, gains)


def raw_grad_body(width, dq_ref, dk_ref, dv_ref, raw_ref, squares_ref, dots_ref, cos_ref, sin_ref, gain_ref, out_ref):
    part = dq_ref.shape[1]
    scales = lax.rsqrt(squares_ref[...] / width + epsilon)
    cubes = scales * scales * scales * dots_ref[...] / width
    for which, ref in enumerate((dq_ref, dk_ref)):
        for first in range(0, part, HD):
            at = slice(which * part + first, which * part + first + HD)
            grad = rope_back(ref[:, first : first + HD].astype(f32), cos_ref[...], sin_ref[...])
            grad = grad * gain_ref[which : which + 1, first : first + HD]
            out_ref[:, at] = (
                scales[:, which : which + 1] * grad - raw_ref[:, at] * cubes[:, which : which + 1]
            ).astype(bf16)
    out_ref[:, 2 * part :] = dv_ref[...]


def raw_grad(d_query, d_key, d_value, raw, squares, dots, cosine, sine_tab, gains, width):
    tokens, part = d_query.shape
    block = min(256, tokens)

    def by_rows(cols):
        return vmem((block, cols), lambda at: (at, 0))

    return pl.pallas_call(
        functools.partial(raw_grad_body, width),
        grid=(tokens // block,),
        in_specs=[by_rows(part)] * 3
        + [by_rows(3 * part), by_rows(2), by_rows(2), by_rows(HD), by_rows(HD), vmem(gains.shape)],
        out_specs=by_rows(3 * part),
        out_shape=jax.ShapeDtypeStruct((tokens, 3 * part), bf16),
        compiler_params=kernel_params(),
    )(d_query, d_key, d_value, raw, squares, dots, cosine, sine_tab, gains)


def together(*trees):
    return lax.optimization_barrier(trees)


def next_one(block, axis):
    size = lax.axis_size(axis)
    return lax.ppermute(block, axis, [(i, (i + 1) % size) for i in range(size)])


def flipped(block, bit):
    size = lax.axis_size("dp")
    return lax.ppermute(block, "dp", [(i, i ^ bit) for i in range(size)])


def exchange(blocks, axis):
    size, here = lax.axis_size(axis), lax.axis_index(axis)
    got = []
    for step in range(size):
        block = lax.dynamic_index_in_dim(blocks, lax.rem(here + step, size), 0, keepdims=False)
        if step:
            block = lax.ppermute(block, axis, [(i, (i + step) % size) for i in range(size)])
        got.append(block)
    return got


def send_ahead(blocks, axis):
    size = lax.axis_size(axis)
    return [blocks[0]] + [
        lax.ppermute(blocks[step], axis, [(i, (i + step) % size) for i in range(size)]) for step in range(1, size)
    ]


def share_out(block, axis):
    size = lax.axis_size(axis)
    return [block] + [
        lax.ppermute(block, axis, [(i, (i + step) % size) for i in range(size)]) for step in range(1, size)
    ]


def assemble_body(parts, places, count, cuts, *refs):
    pieces, outs, (held, in_sems, out_sems) = refs[:count], refs[count : count + len(cuts)], refs[count + len(cuts) :]
    reads, writes, first = [], [], 0
    for at, ((which, start, rows), place) in enumerate(zip(parts, places())):
        here = held.at[pl.ds(first, rows)]
        reads.append(pltpu.make_async_copy(pieces[which].at[pl.ds(start, rows)], here, in_sems.at[at]))
        writes.append(
            [
                pltpu.make_async_copy(
                    held.at[pl.ds(first, rows), pl.ds(left, wide)],
                    out.at[pl.ds(place, rows)],
                    out_sems.at[at * len(cuts) + n],
                )
                for n, (out, (left, wide)) in enumerate(zip(outs, cuts))
            ]
        )
        first += rows
    for read in reads:
        read.start()
    for read, copies in zip(reads, writes):
        read.wait()
        for write in copies:
            write.start()
    for copies in writes:
        for write in copies:
            write.wait()


def assemble(pieces, parts, places, cuts=None):
    shape = (sum(rows for _, _, rows in parts), pieces[0].shape[1])
    several, cuts = cuts is not None, cuts or [(0, shape[1])]
    anywhere = pl.BlockSpec(memory_space=pl.ANY)
    dtype = pieces[0].dtype
    size = shape[0] * shape[1] * dtype.itemsize
    results = pl.pallas_call(
        functools.partial(assemble_body, parts, places, len(pieces), cuts),
        in_specs=[anywhere] * len(pieces),
        out_specs=[anywhere] * len(cuts),
        out_shape=[jax.ShapeDtypeStruct((shape[0], wide), dtype) for _, wide in cuts],
        scratch_shapes=[
            pltpu.VMEM(shape, dtype),
            pltpu.SemaphoreType.DMA((len(parts),)),
            pltpu.SemaphoreType.DMA((len(parts) * len(cuts),)),
        ],
        compiler_params=pltpu.CompilerParams(vmem_limit_bytes=size + 2**20),
        cost_estimate=pl.CostEstimate(flops=0, bytes_accessed=2 * size, transcendentals=0),
    )(*pieces)
    return results if several else results[0]


def stacked(pieces, parts=None):
    parts = parts or [(at, 0, p.shape[0]) for at, p in enumerate(pieces)]
    places = [sum(rows for _, _, rows in parts[:at]) for at in range(len(parts))]
    return assemble(pieces, parts, lambda: places)


def in_order(slots, axis, first=0, rows=None):
    size, rows = len(slots), rows or slots[0].shape[0]

    def places():
        here = lax.axis_index(axis)
        return [pl.multiple_of(lax.rem(here + (size - back), size) * rows, rows) for back in range(size)]

    return assemble(slots, [(at, first, rows) for at in range(size)], places)


def cube_bits():
    bits = [1 << b for b in range(1, (lax.axis_size("dp") - 1).bit_length())]
    return bits, bits[1:] + bits[:1]


class CubeGather:
    def __init__(self, pair, core=False):
        self.arrays = [[block] for block in pair]
        self.masks = [[[0]] for _ in pair]
        self.orders = [list(bits) + [1] * core for bits in cube_bits()]
        self.new = []

    def step(self):
        for at, arrays in enumerate(self.arrays):
            if len(arrays) > 1:
                self.arrays[at] = [stacked(arrays)]
                self.masks[at] = [sum(self.masks[at], [])]
        self.new = [flipped(arrays[0], order[0]) for arrays, order in zip(self.arrays, self.orders)]

    def set(self, new):
        for at, block in enumerate(new):
            bit = self.orders[at].pop(0)
            self.arrays[at].append(block)
            self.masks[at].append([m ^ bit for m in self.masks[at][0]])
        self.new = []

    def finish(self):
        self.set(self.new)
        while self.orders[0]:
            self.step()
            self.set(self.new)


def cube_join(cube, firsts, rows, fold=1, cuts=None):
    pieces, parts, where = [], [], []
    for (own, first), arrays, masks in zip(firsts, cube.arrays, cube.masks):
        step = arrays[0].shape[0] // len(masks[0])
        for array, blocks in zip(arrays, masks):
            for at, mask in enumerate(blocks):
                parts.append((len(pieces), at * step, step))
                where.append((own ^ mask, first))
            pieces.append(array)

    def places():
        here = lax.axis_index("dp")
        return [pl.multiple_of((here ^ mask) // fold * rows + first, step) for mask, first in where]

    return assemble(pieces, parts, places, cuts)


class CubeScatter:
    def __init__(self, pair, core=False):
        self.totals, self.got = list(pair), None
        self.orders = [[1] * core + list(bits) for bits in cube_bits()]
        self.dims = [sorted(order, reverse=True) for order in self.orders]

    def add(self):
        if self.got:
            self.totals = [t.astype(f32) + g.astype(f32) for t, g in zip(self.totals, self.got)]
        self.got = None
        return self.totals

    def step(self):
        self.add()
        got = []
        for which, total in enumerate(self.totals):
            bit = self.orders[which].pop(0)
            at = self.dims[which].index(bit)
            self.dims[which].remove(bit)
            mine = (lax.axis_index("dp") // bit) % 2
            away = lax.dynamic_index_in_dim(total, 1 - mine, at, keepdims=False).astype(bf16)
            got.append(flipped(away, bit))
            self.totals[which] = lax.dynamic_index_in_dim(total, mine, at, keepdims=False)
        self.got = got

    def finish(self):
        while self.orders[0]:
            self.step()
        return jnp.concatenate(self.add(), 1)


def column_halves(grad, core, more=None):
    bits = (lax.axis_size("dp") - 1).bit_length() - (not core)
    cut = grad.shape[1] // 2
    halves = [grad[:, :cut], grad[:, cut:]]
    if more is not None:
        halves[1] = jnp.concatenate([halves[1], more], 1)
    return [half.reshape((2,) * bits + (-1, half.shape[1])) for half in halves]


def small_sum(values, axis):
    return sum(share_out(values.reshape(-1), axis)).reshape(values.shape)


def local(
    tokens,
    segments,
    w_query,
    w_key,
    w_value,
    w_out,
    g_query,
    g_key,
    g_attn,
    w_gate,
    w_up,
    w_down,
    g_ffn,
    d_out,
):
    seqs, local_len, width = tokens.shape
    rows = seqs * local_len
    copies, size = lax.axis_size("dp"), lax.axis_size("seq")
    here = lax.axis_index("seq")
    total_len = size * local_len
    part = width // size
    heads = H // size
    own_rows = w_gate.shape[0]
    ff_width = w_gate.shape[1]
    ff_part = ff_width // size
    ff_own = w_down.shape[0]
    tok_rows = tokens.reshape(rows, width)

    side = width // copies
    pairs = copies // 2
    ff_half = ff_part // 2
    slots = range(size)

    def before(back):
        return lax.rem(lax.axis_index("seq") + (size - back), size)

    def behind(ahead):
        return lax.rem(lax.axis_index("seq") + ahead, size)

    def ff_column(pair, other, seq_at):
        return pl.multiple_of(((pair * 2 + (lax.rem(lax.axis_index("dp"), 2) ^ other)) * size + seq_at) * ff_own, ff_own)

    def ff_pack(weight):
        if ff_own % 128:
            core = lax.rem(lax.axis_index("dp"), 2)
            blocks = weight.reshape(own_rows, pairs, 2, size, ff_own).transpose(2, 3, 0, 1, 4)
            blocks = blocks.reshape(2, size, own_rows, ff_half)
            blocks = jnp.concatenate(
                [lax.dynamic_index_in_dim(blocks, c, 0, keepdims=False) for c in (core, 1 - core)], 1
            )
            return [lax.dynamic_index_in_dim(blocks, behind(ahead), 0, keepdims=False) for ahead in slots]
        return relayout(
            [weight],
            [(2 * own_rows, ff_half)] * size,
            bf16,
            lambda: [
                ((0, 0, ff_column(pair, other, behind(ahead))), (ahead, other * own_rows, pair * ff_own), (own_rows, ff_own))
                for ahead in slots
                for other in (0, 1)
                for pair in range(pairs)
            ],
        )

    def ff_unpack(got):
        if ff_own % 128:
            core = lax.rem(lax.axis_index("dp"), 2)
            joined = in_order(got, "seq").reshape(size, 2, own_rows, pairs, ff_own)
            joined = jnp.where(core == 0, joined, joined[:, ::-1])
            return joined.transpose(2, 3, 1, 0, 4).reshape(own_rows, ff_width).astype(f32)
        return relayout(
            got,
            [(own_rows, ff_width)],
            f32,
            lambda: [
                ((back, other * own_rows, pair * ff_own), (0, 0, ff_column(pair, other, before(back))), (own_rows, ff_own))
                for back in slots
                for other in (0, 1)
                for pair in range(pairs)
            ],
        )[0]

    def ff_pair(got):
        mine, away = [in_order(got, "seq", first, own_rows) for first in (0, own_rows)]
        return [mine, flipped(away, 1)]

    def two_parts(got):
        joined = in_order(got, "seq")
        return [joined[: side // 2], joined[side // 2 :]]

    def part_column(seq_at):
        return pl.multiple_of(seq_at * part, part)

    def part_row(seq_at):
        return pl.multiple_of(seq_at * rows, rows)

    lanes = 128
    own_gains = jnp.stack([g_query, g_key, g_attn, g_ffn], 1)
    own_gains = jnp.pad(own_gains, ((0, 0), (0, lanes - own_gains.shape[1])))
    qkv_send = relayout(
        [w_query, w_key, w_value, own_gains],
        [(own_rows, 3 * part + lanes)] * size,
        bf16,
        lambda: [
            ((which, 0, part_column(behind(ahead))), (ahead, 0, which * part), (own_rows, part))
            for ahead in slots
            for which in range(3)
        ]
        + [((3, 0, 0), (ahead, 0, 3 * part), (own_rows, lanes)) for ahead in slots],
    )
    qkv_got = send_ahead(qkv_send, "seq")
    cube_down = CubeGather([w_down[: ff_own // 2], w_down[ff_own // 2 :]])
    cube_down.step()
    gate_send, up_send = ff_pack(w_gate), ff_pack(w_up)
    qkv_got, new, gate_send, up_send, x_own = together(qkv_got, cube_down.new, gate_send, up_send, tok_rows)
    cube_down.set(new)

    gate_got = send_ahead(gate_send, "seq")
    cube_qkv = CubeGather(two_parts(qkv_got), core=True)
    cube_qkv.step()
    gate_got, new, up_send = together(gate_got, cube_qkv.new, up_send)
    cube_qkv.set(new)
    up_got = send_ahead(up_send, "seq")
    cube_qkv.step()
    cube_gate = CubeGather(ff_pair(gate_got))
    up_got, new, x_own, gate_own = together(up_got, cube_qkv.new, x_own, cube_gate.arrays)
    cube_qkv.set(new)
    cube_gate.arrays = gate_own
    cube_up = CubeGather(ff_pair(up_got))
    cosine, sine_tab = rope_tables(positions(segments).reshape(total_len))

    x_slots = [x_own]
    for at in range(size - 1):
        x_next = next_one(x_slots[-1], "seq")
        if at == 0:
            cube_gate.step()
            cube_down.step()
            x_next, new = together(x_next, cube_gate.new)
            cube_gate.set(new)
        elif at == 1:
            cube_gate.step()
            cube_qkv.step()
            x_next, new, more, cosine, sine_tab = together(x_next, cube_down.new, cube_qkv.new, cosine, sine_tab)
            cube_down.set(new)
            cube_qkv.set(more)
        elif at == size - 2:
            cube_up.step()
            x_next, new, more, w_out_own = together(x_next, cube_gate.new, cube_up.new, w_out)
            cube_gate.set(new)
            cube_up.set(more)
        x_slots.append(x_next)
    cube_qkv.finish()
    w_qkv, gains = cube_join(
        cube_qkv, ((0, 0), (0, side // 2)), side, cuts=[(0, 3 * part), (3 * part, lanes)]
    )

    x_all = in_order(x_slots, "seq")
    out_got = share_out(w_out_own, "seq")
    cube_up.step()
    qkv = product(x_all, w_qkv)
    squares = jnp.stack([jnp.sum(jnp.square(qkv[:, first : first + part]), -1) for first in (0, part)], 0)
    squares = small_sum(squares, "seq")
    gains = gains[:, :4].T.astype(f32)
    gain_attn, gain_ffn = gains[2], gains[3]
    gain_qk = lax.dynamic_slice_in_dim(gains[:2], here * part, part, 1)
    squares, out_got, gain_qk = together(squares, out_got, gain_qk)
    cube_out = CubeGather(two_parts(out_got), core=True)
    cube_out.step()
    squares = squares.T
    query, key, value = query_key(qkv, squares, cosine, sine_tab, gain_qk, width)
    seg_ids = segments.reshape(total_len)
    attended = attend(query, key, value, seg_ids)
    attended = relayout(
        [attended],
        [(rows, part)] * size,
        bf16,
        lambda: [((0, part_row(behind(ahead)), 0), (ahead, 0, 0), (rows, part)) for ahead in slots],
    )
    attended, new, more = together(attended, cube_out.new, cube_up.new)
    cube_out.set(new)
    cube_up.set(more)
    attended = send_ahead(attended, "seq")
    cube_out.step()
    for cube in (cube_down, cube_gate, cube_up):
        cube.finish()
    w_down_part = cube_join(cube_down, ((0, 0), (0, ff_own // 2)), ff_own, 2)
    w_gate_part, w_up_part = [cube_join(cube, ((0, 0), (1, 0)), side) for cube in (cube_gate, cube_up)]
    attended, new, w_down_part, w_gate_part, w_up_part = together(
        attended, cube_out.new, w_down_part, w_gate_part, w_up_part
    )
    cube_out.set(new)
    cube_out.finish()
    w_out_all = cube_join(cube_out, ((0, 0), (0, side // 2)), side)
    attended = relayout(
        attended,
        [(rows, width)],
        bf16,
        lambda: [((back, 0, 0), (0, 0, part_column(before(back))), (rows, part)) for back in slots],
    )[0]

    a_proj = product(attended, w_out_all)
    a_scale = rms_scale(a_proj)
    hidden = tok_rows.astype(f32) + a_proj * a_scale * gain_attn

    def ring(block, work, last=lambda: (), beside=lambda early: ()):
        got, own = None, None
        for at in range(size):
            later = next_one(block, "seq") if at < size - 1 else None
            share = work(stacked([block, flipped(block, 1)]))
            if later is None:
                share, early = together(share, last())
            share, away = share[:rows], share[rows:].astype(bf16)
            if later is not None:
                later, share, away = together(later, share, away)
            share = share + flipped(away, 1).astype(f32)
            if at == 0:
                own = share
            else:
                if at > 1:
                    share = share + got.astype(f32)
                got = next_one(share.astype(bf16), "seq")
            block = later
        got, extra = together(got, beside(early))
        return own + got.astype(f32), extra

    h_slots, gates, ups, inners = [], [], [], []

    def forward(h_low):
        gate = product(h_low, w_gate_part)
        up = product(h_low, w_up_part)
        inner = (jax.nn.silu(gate) * up).astype(bf16)
        h_slots.append(h_low)
        gates.append(gate)
        ups.append(up)
        inners.append(inner)
        return product(inner, w_down_part)

    m_proj, _ = ring(hidden.astype(bf16), forward)
    m_scale = rms_scale(m_proj)
    out = (hidden + m_proj * m_scale * gain_ffn).astype(bf16).reshape(tokens.shape)
    grad_out = d_out.reshape(rows, width).astype(f32)
    d_gain_ffn = jnp.sum(grad_out * m_proj * m_scale, 0)
    dm_low = norm_back(m_proj, m_scale, grad_out * gain_ffn).astype(bf16)
    dms, d_gates, d_ups = [], [], []

    def backward(dm_slot):
        at = len(dms)
        gate, up = gates[at], ups[at]
        d_inner = against(dm_slot, w_down_part)
        sigmoid_gate = jax.nn.sigmoid(gate)
        d_gate = (d_inner * up * sigmoid_gate * (1.0 + gate * (1.0 - sigmoid_gate))).astype(bf16)
        d_up = (d_inner * (gate * sigmoid_gate)).astype(bf16)
        dms.append(dm_slot)
        d_gates.append(d_gate)
        d_ups.append(d_up)
        return against(d_gate, w_gate_part) + against(d_up, w_up_part)

    def down_grad():
        return weight_grad(stacked(inners), stacked(dms)).astype(bf16)

    def grads(d_down):
        for grad in (d_down, weight_grad(h_alls[0], stacked(d_gates)).astype(bf16)):
            cubes.append(CubeScatter(column_halves(grad, False)))
            cubes[-1].step()
        d_up = weight_grad(h_alls[0], stacked(d_ups)).astype(bf16)
        return d_up, [cube.got for cube in cubes]

    h_alls, cubes = [stacked(h_slots)], []
    d_sum, (d_up, gots) = ring(dm_low, backward, down_grad, grads)
    cube_down, cube_gate = cubes
    cube_down.got, cube_gate.got = gots

    def ff_rows(total):
        core = lax.rem(lax.axis_index("dp"), 2)
        total = total.astype(bf16).reshape(2, side, ff_half)
        mine, away = [lax.dynamic_index_in_dim(total, c, 0, keepdims=False) for c in (core, 1 - core)]
        away = flipped(away, 1)

        def moves():
            return [
                ((which, pl.multiple_of(behind(ahead) * own_rows, own_rows), 0), (ahead, which * own_rows, 0), (own_rows, ff_half))
                for ahead in slots
                for which in (0, 1)
            ]

        return relayout([mine, away], [(2 * own_rows, ff_half)] * size, bf16, moves)

    def row_blocks(total):
        wide = total.shape[1]
        return relayout(
            [total],
            [(own_rows, wide)] * size,
            bf16,
            lambda: [
                ((0, pl.multiple_of(behind(ahead) * own_rows, own_rows), 0), (ahead, 0, 0), (own_rows, wide))
                for ahead in slots
            ],
        )

    cube_gate.step()
    d_hidden = grad_out + d_sum
    d_gain_attn = jnp.sum(d_hidden * a_proj * a_scale, 0)
    da_low = norm_back(a_proj, a_scale, d_hidden * gain_attn).astype(bf16)
    d_attended = against(da_low, w_out_all).astype(bf16)
    d_attended = relayout(
        [d_attended],
        [(rows, part)] * size,
        bf16,
        lambda: [((0, 0, part_column(behind(ahead))), (ahead, 0, 0), (rows, part)) for ahead in slots],
    )
    d_attended, cube_gate.got, d_up = together(d_attended, cube_gate.got, d_up)
    d_attended = send_ahead(d_attended, "seq")
    cube_up = CubeScatter(column_halves(d_up, False))
    cube_up.step()
    d_w_out = weight_grad(attended, da_low).astype(bf16)
    gate_send = ff_rows(cube_gate.finish())
    d_attended, cube_up.got, d_w_out, gate_send = together(d_attended, cube_up.got, d_w_out, gate_send)
    d_attended = in_order(d_attended, "seq")

    gate_got = send_ahead(gate_send, "seq")
    cube_up.step()
    d_query, d_key, d_value = attend_back(query, key, value, d_attended, seg_ids)
    d_query, gate_got, cube_up.got = together(d_query, gate_got, cube_up.got)
    up_send = ff_rows(cube_up.finish())
    dots, d_gain_qk = unrope(d_query, d_key, qkv, squares, cosine, sine_tab, gain_qk, width)
    dots = small_sum(dots.T, "seq")
    d_gain_qk = lax.dynamic_update_slice_in_dim(jnp.zeros((2, width), f32), d_gain_qk, here * part, 1)
    d_gains = jnp.concatenate([d_gain_qk, d_gain_attn[None], d_gain_ffn[None]], 0).T.astype(bf16)
    d_gains = jnp.pad(d_gains, ((0, 0), (0, lanes - d_gains.shape[1])))
    cube_out = CubeScatter(column_halves(d_w_out, True, d_gains), core=True)
    cube_out.step()
    d_qkv = raw_grad(d_query, d_key, d_value, qkv, squares, dots.T, cosine, sine_tab, gain_qk, width)
    d_qkv, up_send, cube_out.got = together(d_qkv, up_send, cube_out.got)
    d_slots = relayout(
        [d_qkv],
        [(rows, 3 * part)] * size,
        bf16,
        lambda: [((0, part_row(before(back)), 0), (back, 0, 0), (rows, 3 * part)) for back in slots],
    )
    got = next_one(against(d_slots[1], w_qkv).astype(bf16), "seq")
    up_got = send_ahead(up_send, "seq")
    cube_out.step()
    cube_qkv = CubeScatter(column_halves(weight_grad(x_all, d_qkv).astype(bf16), True), core=True)
    cube_qkv.step()
    shares = [against(d_slots[back], w_qkv) for back in [*slots[2:], 0]]
    got, up_got, cube_out.got, cube_qkv.got, shares = together(got, up_got, cube_out.got, cube_qkv.got, shares)
    for back in range(2, size):
        got = next_one((shares[back - 2] + got.astype(f32)).astype(bf16), "seq")
        if back == 2:
            cube_qkv.step()
            cube_out.step()
            got, cube_qkv.got, cube_out.got = together(got, cube_qkv.got, cube_out.got)
        elif back == 3:
            cube_qkv.step()
            out_send = row_blocks(cube_out.finish())
            got, cube_qkv.got, out_send = together(got, cube_qkv.got, out_send)
    out_got = send_ahead(out_send, "seq")
    d_w_qkv = send_ahead(row_blocks(cube_qkv.finish()), "seq")
    d_down = cube_down.finish()
    d_tokens = d_hidden + shares[-1] + got.astype(f32)
    out_sum = sum(g.astype(f32) for g in out_got)
    d_w_out, d_gains = out_sum[:, :width], out_sum[:, width : width + 4].T
    d_w_qkv = relayout(
        d_w_qkv,
        [(own_rows, width)] * 3,
        f32,
        lambda: [
            ((back, 0, which * part), (which, 0, part_column(before(back))), (own_rows, part))
            for back in slots
            for which in range(3)
        ],
    )
    d_w_gate, d_w_up = ff_unpack(gate_got), ff_unpack(up_got)
    return (
        out,
        d_tokens.reshape(tokens.shape),
        d_w_qkv[0],
        d_w_qkv[1],
        d_w_qkv[2],
        d_w_out,
        d_gains[0],
        d_gains[1],
        d_gains[2],
        d_w_gate,
        d_w_up,
        d_down,
        d_gains[3],
    )


def solution(mesh):
    rows = P("dp", "seq", None)
    mat = P(("dp", "seq"), None)
    vec = P(("dp", "seq"))
    in_specs = (rows, P("dp", None), mat, mat, mat, mat, vec, vec, vec, mat, mat, mat, vec, rows)
    out_specs = (rows, rows, mat, mat, mat, mat, vec, vec, vec, mat, mat, mat, vec)
    return jax.shard_map(local, mesh=mesh, in_specs=in_specs, out_specs=out_specs, check_vma=False)
```

```python
import functools

import jax
import jax.numpy as jnp
from jax import lax
from jax.experimental import pallas as pl
from jax.experimental.pallas import tpu as pltpu
from jax.sharding import PartitionSpec as P

H = 16
HD = 128
DOCS = 4

epsilon = 1e-06
rope_base = 500000.0
masked_score = -1e30
bf16 = jnp.bfloat16
f32 = jnp.float32


def product(left, right):
    return jnp.dot(left, right, preferred_element_type=f32)


def against(left, right):
    return lax.dot_general(left, right, (((1,), (1,)), ((), ())), preferred_element_type=f32)


def weight_grad(left, right):
    return lax.dot_general(left, right, (((0,), (0,)), ((), ())), preferred_element_type=f32)


def rms_scale(values):
    return lax.rsqrt(jnp.mean(values * values, -1, keepdims=True) + epsilon)


def norm_back(values, scale_rows, grad_vals):
    return scale_rows * grad_vals - values * scale_rows**3 * jnp.mean(
        grad_vals * values, -1, keepdims=True
    )


def positions(seg_ids):
    doc_ids = jnp.arange(DOCS, dtype=jnp.int32)
    starts = jnp.sum((seg_ids[..., None, :] < doc_ids[:, None]).astype(jnp.int32), -1)
    one_hot = (seg_ids[..., None] == doc_ids).astype(jnp.int32)
    token_start = jnp.sum(one_hot * starts[..., None, :], axis=-1)
    return jnp.arange(seg_ids.shape[-1], dtype=jnp.int32) - token_start


def rope_tables(position_ids):
    freqs = rope_base ** (-jnp.arange(HD // 2, dtype=f32) * 2.0 / HD)
    angles = position_ids.astype(f32)[..., None] * freqs
    cosine = jnp.cos(angles)
    sine_tab = jnp.sin(angles)
    return (
        jnp.concatenate([cosine, cosine], -1),
        jnp.concatenate([sine_tab, sine_tab], -1),
    )


def contract(left, right, left_dim, right_dim):
    return lax.dot_general(left, right, (((left_dim,), (right_dim,)), ((), ())), preferred_element_type=f32)


def vmem(shape, index=None):
    return pl.BlockSpec(shape, index or (lambda *_: (0,) * len(shape)))


def kernel_params(grid=0):
    return pltpu.CompilerParams(vmem_limit_bytes=48 * 2**20)


def relayout_body(moves, count, *refs):
    ins, outs = refs[:count], refs[count:]
    for (src, src_row, src_col), (dst, dst_row, dst_col), (rows, cols) in moves():
        outs[dst][pl.ds(dst_row, rows), pl.ds(dst_col, cols)] = ins[src][
            pl.ds(src_row, rows), pl.ds(src_col, cols)
        ].astype(outs[dst].dtype)


def relayout(arrays, shapes, dtype, moves):
    outs = [jax.ShapeDtypeStruct(shape, dtype) for shape in shapes]
    size = sum(a.size * a.dtype.itemsize for a in [*arrays, *outs])
    return pl.pallas_call(
        functools.partial(relayout_body, moves, len(arrays)),
        in_specs=[vmem(a.shape) for a in arrays],
        out_specs=[vmem(o.shape) for o in outs],
        out_shape=outs,
        compiler_params=kernel_params(),
        cost_estimate=pl.CostEstimate(flops=0, bytes_accessed=size, transcendentals=0),
    )(*arrays)


def turned(values):
    lane = lax.broadcasted_iota(jnp.int32, values.shape, 1)
    rolled = pltpu.roll(values, HD // 2, 1)
    return jnp.where(lane < HD // 2, -rolled, rolled)


def query_key_body(width, raw_ref, squares_ref, cos_ref, sin_ref, gain_ref, q_ref, k_ref, v_ref):
    part = q_ref.shape[1]
    scales = lax.rsqrt(squares_ref[...] / width + epsilon)
    for which, out in enumerate((q_ref, k_ref)):
        for first in range(0, part, HD):
            gain = gain_ref[which : which + 1, first : first + HD]
            unit = raw_ref[:, which * part + first : which * part + first + HD] * scales[:, which : which + 1] * gain
            out[:, first : first + HD] = (unit * cos_ref[...] + turned(unit) * sin_ref[...]).astype(bf16)
    v_ref[...] = raw_ref[:, 2 * part :].astype(bf16)


def query_key(raw, squares, cosine, sine_tab, gains, width):
    tokens, part = raw.shape[0], raw.shape[1] // 3
    block = min(256, tokens)
    shape = jax.ShapeDtypeStruct((tokens, part), bf16)

    def by_rows(cols):
        return vmem((block, cols), lambda at: (at, 0))

    return pl.pallas_call(
        functools.partial(query_key_body, width),
        grid=(tokens // block,),
        in_specs=[by_rows(3 * part), by_rows(2), by_rows(HD), by_rows(HD), vmem(gains.shape)],
        out_specs=[by_rows(part)] * 3,
        out_shape=[shape] * 3,
        compiler_params=kernel_params(),
    )(raw, squares, cosine, sine_tab, gains)


def ffn_backward_body(steps, left_ref, down_w, gate_ref, up_ref, gate_w, up_w, d_gate_ref, d_up_ref, share_ref):
    step = pl.program_id(0)
    d_inner = contract(left_ref[...], down_w[...], 1, 1)
    gate = gate_ref[...]
    sigmoid = jax.nn.sigmoid(gate)
    d_gate = (d_inner * up_ref[...] * sigmoid * (1.0 + gate * (1.0 - sigmoid))).astype(bf16)
    d_up = (d_inner * (gate * sigmoid)).astype(bf16)
    d_gate_ref[...] = d_gate
    d_up_ref[...] = d_up
    share = contract(d_gate, gate_w[...], 1, 1) + contract(d_up, up_w[...], 1, 1)

    @pl.when(step == 0)
    def _():
        share_ref[...] = share

    if steps > 1:

        @pl.when(step > 0)
        def _():
            share_ref[...] += share


def ffn_backward(left, gate, up, w_down, w_gate, w_up):
    rows, width = left.shape
    extent = gate.shape[1]
    tile = min(512, extent)
    by_columns = vmem((rows, tile), lambda at: (0, at))
    return pl.pallas_call(
        functools.partial(ffn_backward_body, extent // tile),
        grid=(extent // tile,),
        in_specs=[
            vmem(left.shape),
            vmem((tile, width), lambda at: (at, 0)),
            by_columns,
            by_columns,
            vmem((width, tile), lambda at: (0, at)),
            vmem((width, tile), lambda at: (0, at)),
        ],
        out_specs=[by_columns, by_columns, vmem(left.shape)],
        out_shape=[
            jax.ShapeDtypeStruct(gate.shape, bf16),
            jax.ShapeDtypeStruct(gate.shape, bf16),
            jax.ShapeDtypeStruct(left.shape, f32),
        ],
        compiler_params=kernel_params(),
        cost_estimate=pl.CostEstimate(
            flops=6 * rows * width * extent, bytes_accessed=6 * width * extent, transcendentals=rows * extent
        ),
    )(left, w_down, gate, up, w_gate, w_up)


def grad_halves_body(left_ref, right_ref, one_ref, two_ref):
    total = contract(left_ref[...], right_ref[...], 0, 0).astype(bf16)
    cut = one_ref.shape[1]
    one_ref[...] = total[:, :cut]
    two_ref[...] = total[:, cut:]


def grad_halves(left, right, core):
    bits = (lax.axis_size("dp") - 1).bit_length() - (not core)
    (tokens, depth), cut = left.shape, right.shape[1] // 2
    block = min(256, depth)
    half = jax.ShapeDtypeStruct((depth, cut), bf16)
    halves = pl.pallas_call(
        grad_halves_body,
        grid=(depth // block,),
        in_specs=[vmem((tokens, block), lambda at: (0, at)), vmem(right.shape)],
        out_specs=[vmem((block, cut), lambda at: (at, 0))] * 2,
        out_shape=[half, half],
        compiler_params=kernel_params(),
        cost_estimate=pl.CostEstimate(
            flops=4 * tokens * depth * cut, bytes_accessed=4 * tokens * depth, transcendentals=0
        ),
    )(left, right)
    return [half.reshape((2,) * bits + (-1, cut)) for half in halves]


def key_weights(query, key, seg_query, seg_key, first, count):
    scores = contract(key, query, 1, 1) * HD ** (-0.5)
    shape = scores.shape
    allowed = (seg_key == seg_query) & (
        lax.broadcasted_iota(jnp.int32, shape, 0) <= first + lax.broadcasted_iota(jnp.int32, shape, 1)
    )
    scores = jnp.where(allowed, scores, masked_score)
    expos = jnp.exp(scores - jnp.max(scores, 0, keepdims=True))
    return expos * (1.0 / jnp.sum(expos, 0, keepdims=True))


def attend_body(blocks, q_ref, k_ref, v_ref, seg_q_ref, seg_k_ref, out_ref):
    rows = q_ref.shape[0]
    for at in range(blocks):
        seen = (at + 1) * rows

        @pl.when(pl.program_id(1) == at)
        def _():
            probs = key_weights(
                q_ref[...], k_ref[:seen], seg_q_ref[...], seg_k_ref[:seen], at * rows, seen
            ).astype(bf16)
            out_ref[...] = contract(probs, v_ref[:seen], 0, 0).astype(bf16)


def attention_specs(tokens, block):
    by_query = vmem((block, HD), lambda head, at: (at, head))
    by_head = vmem((tokens, HD), lambda head, at: (0, head))
    return by_query, by_head, [vmem((1, block), lambda head, at: (0, at)), vmem((tokens, 1))]


def attend(query, key, value, seg_ids):
    tokens, part = query.shape
    block = min(256, tokens)
    by_query, by_head, segs = attention_specs(tokens, block)
    return pl.pallas_call(
        functools.partial(attend_body, tokens // block),
        grid=(part // HD, tokens // block),
        in_specs=[by_query, by_head, by_head, *segs],
        out_specs=by_query,
        out_shape=jax.ShapeDtypeStruct(query.shape, bf16),
        compiler_params=kernel_params(),
    )(query, key, value, seg_ids[None, :], seg_ids[:, None])


def attend_back_body(
    blocks, q_ref, k_ref, v_ref, g_ref, seg_q_ref, seg_k_ref, dq_ref, dk_ref, dv_ref, dk_sum, dv_sum
):
    rows = q_ref.shape[0]
    scale = HD ** (-0.5)
    for at in range(blocks):
        seen = (at + 1) * rows

        @pl.when(pl.program_id(1) == at)
        def _():
            query, grad = q_ref[...], g_ref[...]
            probs = key_weights(query, k_ref[:seen], seg_q_ref[...], seg_k_ref[:seen], at * rows, seen)
            d_probs = contract(v_ref[:seen], grad, 1, 1)
            inner = jnp.sum(probs * d_probs, 0, keepdims=True)
            d_scores = (probs * (d_probs - inner)).astype(bf16)
            dq_ref[...] = (contract(d_scores, k_ref[:seen], 0, 0) * scale).astype(bf16)
            d_key = contract(d_scores, query, 1, 0) * scale
            d_value = contract(probs.astype(bf16), grad, 1, 0)
            old = seen - rows
            dk_sum[old:seen] = d_key[old:]
            dv_sum[old:seen] = d_value[old:]
            if at:
                dk_sum[:old] += d_key[:old]
                dv_sum[:old] += d_value[:old]
            if at == blocks - 1:
                dk_ref[...] = dk_sum[...].astype(bf16)
                dv_ref[...] = dv_sum[...].astype(bf16)


def attend_back(query, key, value, grad, seg_ids):
    tokens, part = query.shape
    block = min(256, tokens)
    by_query, by_head, segs = attention_specs(tokens, block)
    shape = jax.ShapeDtypeStruct(query.shape, bf16)
    return pl.pallas_call(
        functools.partial(attend_back_body, tokens // block),
        grid=(part // HD, tokens // block),
        in_specs=[by_query, by_head, by_head, by_query, *segs],
        out_specs=[by_query, by_head, by_head],
        out_shape=[shape] * 3,
        scratch_shapes=[pltpu.VMEM((tokens, HD), f32)] * 2,
        compiler_params=kernel_params(),
    )(query, key, value, grad, seg_ids[None, :], seg_ids[:, None])


def rope_back(grad, cosine, sine_tab):
    return grad * cosine - turned(grad * sine_tab)


def unrope_body(width, dq_ref, dk_ref, raw_ref, squares_ref, cos_ref, sin_ref, gain_ref, dots_ref, gains_ref):
    part = dq_ref.shape[1]
    scales = lax.rsqrt(squares_ref[...] / width + epsilon)

    @pl.when(pl.program_id(0) == 0)
    def _():
        gains_ref[...] = jnp.zeros_like(gains_ref)

    for which, ref in enumerate((dq_ref, dk_ref)):
        dots = 0.0
        for first in range(0, part, HD):
            raw = raw_ref[:, which * part + first : which * part + first + HD]
            grad = rope_back(ref[:, first : first + HD].astype(f32), cos_ref[...], sin_ref[...])
            both = grad * raw
            gain = gain_ref[which : which + 1, first : first + HD]
            dots = dots + jnp.sum(both * gain, 1, keepdims=True)
            gains_ref[which : which + 1, first : first + HD] += jnp.sum(
                both * scales[:, which : which + 1], 0, keepdims=True
            )
        dots_ref[:, which : which + 1] = dots


def unrope(d_query, d_key, raw, squares, cosine, sine_tab, gains, width):
    tokens, part = d_query.shape
    block = min(256, tokens)

    def by_rows(cols):
        return vmem((block, cols), lambda at: (at, 0))

    return pl.pallas_call(
        functools.partial(unrope_body, width),
        grid=(tokens // block,),
        in_specs=[by_rows(part)] * 2
        + [by_rows(3 * part), by_rows(2), by_rows(HD), by_rows(HD), vmem(gains.shape)],
        out_specs=[by_rows(2), vmem((2, part))],
        out_shape=[jax.ShapeDtypeStruct((tokens, 2), f32), jax.ShapeDtypeStruct((2, part), f32)],
        compiler_params=kernel_params(),
    )(d_query, d_key, raw, squares, cosine, sine_tab, gains)


def raw_grad_body(width, dq_ref, dk_ref, dv_ref, raw_ref, squares_ref, dots_ref, cos_ref, sin_ref, gain_ref, out_ref):
    part = dq_ref.shape[1]
    scales = lax.rsqrt(squares_ref[...] / width + epsilon)
    cubes = scales * scales * scales * dots_ref[...] / width
    for which, ref in enumerate((dq_ref, dk_ref)):
        for first in range(0, part, HD):
            at = slice(which * part + first, which * part + first + HD)
            grad = rope_back(ref[:, first : first + HD].astype(f32), cos_ref[...], sin_ref[...])
            grad = grad * gain_ref[which : which + 1, first : first + HD]
            out_ref[:, at] = (
                scales[:, which : which + 1] * grad - raw_ref[:, at] * cubes[:, which : which + 1]
            ).astype(bf16)
    out_ref[:, 2 * part :] = dv_ref[...]


def raw_grad(d_query, d_key, d_value, raw, squares, dots, cosine, sine_tab, gains, width):
    tokens, part = d_query.shape
    block = min(256, tokens)

    def by_rows(cols):
        return vmem((block, cols), lambda at: (at, 0))

    return pl.pallas_call(
        functools.partial(raw_grad_body, width),
        grid=(tokens // block,),
        in_specs=[by_rows(part)] * 3
        + [by_rows(3 * part), by_rows(2), by_rows(2), by_rows(HD), by_rows(HD), vmem(gains.shape)],
        out_specs=by_rows(3 * part),
        out_shape=jax.ShapeDtypeStruct((tokens, 3 * part), bf16),
        compiler_params=kernel_params(),
    )(d_query, d_key, d_value, raw, squares, dots, cosine, sine_tab, gains)


def together(*trees):
    return lax.optimization_barrier(trees)


def next_one(block, axis):
    size = lax.axis_size(axis)
    return lax.ppermute(block, axis, [(i, (i + 1) % size) for i in range(size)])


def flipped(block, bit):
    size = lax.axis_size("dp")
    return lax.ppermute(block, "dp", [(i, i ^ bit) for i in range(size)])


def exchange(blocks, axis):
    size, here = lax.axis_size(axis), lax.axis_index(axis)
    got = []
    for step in range(size):
        block = lax.dynamic_index_in_dim(blocks, lax.rem(here + step, size), 0, keepdims=False)
        if step:
            block = lax.ppermute(block, axis, [(i, (i + step) % size) for i in range(size)])
        got.append(block)
    return got


def send_ahead(blocks, axis):
    size = lax.axis_size(axis)
    return [blocks[0]] + [
        lax.ppermute(blocks[step], axis, [(i, (i + step) % size) for i in range(size)]) for step in range(1, size)
    ]


def share_out(block, axis):
    size = lax.axis_size(axis)
    return [block] + [
        lax.ppermute(block, axis, [(i, (i + step) % size) for i in range(size)]) for step in range(1, size)
    ]


def assemble_body(parts, places, count, cuts, *refs):
    pieces, outs, (held, in_sems, out_sems) = refs[:count], refs[count : count + len(cuts)], refs[count + len(cuts) :]
    reads, writes, first = [], [], 0
    for at, ((which, start, rows), place) in enumerate(zip(parts, places())):
        here = held.at[pl.ds(first, rows)]
        reads.append(pltpu.make_async_copy(pieces[which].at[pl.ds(start, rows)], here, in_sems.at[at]))
        writes.append(
            [
                pltpu.make_async_copy(
                    held.at[pl.ds(first, rows), pl.ds(left, wide)],
                    out.at[pl.ds(place, rows)],
                    out_sems.at[at * len(cuts) + n],
                )
                for n, (out, (left, wide)) in enumerate(zip(outs, cuts))
            ]
        )
        first += rows
    for read in reads:
        read.start()
    for read, copies in zip(reads, writes):
        read.wait()
        for write in copies:
            write.start()
    for copies in writes:
        for write in copies:
            write.wait()


def assemble(pieces, parts, places, cuts=None, room=0):
    shape = (sum(rows for _, _, rows in parts), pieces[0].shape[1])
    several, cuts = cuts is not None, cuts or [(0, shape[1])]
    anywhere = pl.BlockSpec(memory_space=pl.ANY)
    dtype = pieces[0].dtype
    size = shape[0] * shape[1] * dtype.itemsize
    results = pl.pallas_call(
        functools.partial(assemble_body, parts, places, len(pieces), cuts),
        in_specs=[anywhere] * len(pieces),
        out_specs=[anywhere] * len(cuts),
        out_shape=[jax.ShapeDtypeStruct((shape[0], wide), dtype) for _, wide in cuts],
        scratch_shapes=[
            pltpu.VMEM(shape, dtype),
            pltpu.SemaphoreType.DMA((len(parts),)),
            pltpu.SemaphoreType.DMA((len(parts) * len(cuts),)),
        ],
        compiler_params=pltpu.CompilerParams(vmem_limit_bytes=max(room, size + 2**20)),
        cost_estimate=pl.CostEstimate(flops=0, bytes_accessed=2 * size, transcendentals=0),
    )(*pieces)
    return results if several else results[0]


def stacked(pieces, room=0):
    parts = [(at, 0, p.shape[0]) for at, p in enumerate(pieces)]
    places = [sum(rows for _, _, rows in parts[:at]) for at in range(len(parts))]
    return assemble(pieces, parts, lambda: places, room=room)


def in_order(slots, axis, first=0, rows=None):
    size, rows = len(slots), rows or slots[0].shape[0]

    def places():
        here = lax.axis_index(axis)
        return [pl.multiple_of(lax.rem(here + (size - back), size) * rows, rows) for back in range(size)]

    return assemble(slots, [(at, first, rows) for at in range(size)], places)


def cube_bits():
    bits = [1 << b for b in range(1, (lax.axis_size("dp") - 1).bit_length())]
    return bits, bits[1:] + bits[:1]


class CubeGather:
    def __init__(self, pair, core=False):
        self.arrays = [[block] for block in pair]
        self.masks = [[[0]] for _ in pair]
        self.orders = [list(bits) + [1] * core for bits in cube_bits()]
        self.new = []

    def step(self):
        for at, arrays in enumerate(self.arrays):
            if len(arrays) > 1:
                self.arrays[at] = [stacked(arrays)]
                self.masks[at] = [sum(self.masks[at], [])]
        self.new = [flipped(arrays[0], order[0]) for arrays, order in zip(self.arrays, self.orders)]

    def set(self, new):
        for at, block in enumerate(new):
            bit = self.orders[at].pop(0)
            self.arrays[at].append(block)
            self.masks[at].append([m ^ bit for m in self.masks[at][0]])
        self.new = []

    def finish(self):
        self.set(self.new)
        while self.orders[0]:
            self.step()
            self.set(self.new)


def cube_join(cube, firsts, rows, fold=1, cuts=None):
    pieces, parts, where = [], [], []
    for (own, first), arrays, masks in zip(firsts, cube.arrays, cube.masks):
        step = arrays[0].shape[0] // len(masks[0])
        for array, blocks in zip(arrays, masks):
            for at, mask in enumerate(blocks):
                parts.append((len(pieces), at * step, step))
                where.append((own ^ mask, first))
            pieces.append(array)

    def places():
        here = lax.axis_index("dp")
        return [pl.multiple_of((here ^ mask) // fold * rows + first, step) for mask, first in where]

    return assemble(pieces, parts, places, cuts)


class CubeScatter:
    def __init__(self, pair, core=False):
        self.totals, self.got = list(pair), None
        self.orders = [[1] * core + list(bits) for bits in cube_bits()]
        self.dims = [sorted(order, reverse=True) for order in self.orders]

    def add(self):
        if self.got:
            self.totals = [t.astype(f32) + g.astype(f32) for t, g in zip(self.totals, self.got)]
        self.got = None
        return self.totals

    def prepare(self):
        self.add()
        self.away, self.bits = [], [order.pop(0) for order in self.orders]
        for which, (total, bit) in enumerate(zip(self.totals, self.bits)):
            at = self.dims[which].index(bit)
            self.dims[which].remove(bit)
            mine = (lax.axis_index("dp") // bit) % 2
            self.away.append(lax.dynamic_index_in_dim(total, 1 - mine, at, keepdims=False).astype(bf16))
            self.totals[which] = lax.dynamic_index_in_dim(total, mine, at, keepdims=False)

    def send(self):
        self.got = [flipped(away, bit) for away, bit in zip(self.away, self.bits)]

    def step(self):
        self.prepare()
        self.send()

    def finish(self):
        while self.orders[0]:
            self.step()
        return jnp.concatenate(self.add(), 1)


def small_sum(values, axis):
    return sum(share_out(values.reshape(-1), axis)).reshape(values.shape)


def local(
    tokens,
    segments,
    w_query,
    w_key,
    w_value,
    w_out,
    g_query,
    g_key,
    g_attn,
    w_gate,
    w_up,
    w_down,
    g_ffn,
    d_out,
):
    seqs, local_len, width = tokens.shape
    rows = seqs * local_len
    copies, size = lax.axis_size("dp"), lax.axis_size("seq")
    here = lax.axis_index("seq")
    total_len = size * local_len
    part = width // size
    heads = H // size
    own_rows = w_gate.shape[0]
    ff_width = w_gate.shape[1]
    ff_part = ff_width // size
    ff_own = w_down.shape[0]
    tok_rows = tokens.reshape(rows, width)

    side = width // copies
    pairs = copies // 2
    ff_half = ff_part // 2
    slots = range(size)

    def before(back):
        return lax.rem(lax.axis_index("seq") + (size - back), size)

    def behind(ahead):
        return lax.rem(lax.axis_index("seq") + ahead, size)

    def ff_column(pair, other, seq_at):
        return pl.multiple_of(((pair * 2 + (lax.rem(lax.axis_index("dp"), 2) ^ other)) * size + seq_at) * ff_own, ff_own)

    def ff_pack(weight):
        if ff_own % 128:
            core = lax.rem(lax.axis_index("dp"), 2)
            blocks = weight.reshape(own_rows, pairs, 2, size, ff_own).transpose(2, 3, 0, 1, 4)
            blocks = blocks.reshape(2, size, own_rows, ff_half)
            blocks = jnp.concatenate(
                [lax.dynamic_index_in_dim(blocks, c, 0, keepdims=False) for c in (core, 1 - core)], 1
            )
            return [lax.dynamic_index_in_dim(blocks, behind(ahead), 0, keepdims=False) for ahead in slots]
        return relayout(
            [weight],
            [(2 * own_rows, ff_half)] * size,
            bf16,
            lambda: [
                ((0, 0, ff_column(pair, other, behind(ahead))), (ahead, other * own_rows, pair * ff_own), (own_rows, ff_own))
                for ahead in slots
                for other in (0, 1)
                for pair in range(pairs)
            ],
        )

    def ff_unpack(got):
        if ff_own % 128:
            core = lax.rem(lax.axis_index("dp"), 2)
            joined = in_order(got, "seq").reshape(size, 2, own_rows, pairs, ff_own)
            joined = jnp.where(core == 0, joined, joined[:, ::-1])
            return joined.transpose(2, 3, 1, 0, 4).reshape(own_rows, ff_width).astype(f32)
        return relayout(
            got,
            [(own_rows, ff_width)],
            f32,
            lambda: [
                ((back, other * own_rows, pair * ff_own), (0, 0, ff_column(pair, other, before(back))), (own_rows, ff_own))
                for back in slots
                for other in (0, 1)
                for pair in range(pairs)
            ],
        )[0]

    def ff_pair(got):
        mine, away = [in_order(got, "seq", first, own_rows) for first in (0, own_rows)]
        return [mine, flipped(away, 1)]

    def two_parts(got):
        joined = in_order(got, "seq")
        return [joined[: side // 2], joined[side // 2 :]]

    def part_column(seq_at):
        return pl.multiple_of(seq_at * part, part)

    def part_row(seq_at):
        return pl.multiple_of(seq_at * rows, rows)

    lanes = 128
    own_gains = jnp.stack([g_query, g_key, g_attn, g_ffn], 1)
    own_gains = jnp.pad(own_gains, ((0, 0), (0, lanes - own_gains.shape[1])))
    qkv_send = relayout(
        [w_query, w_key, w_value, own_gains],
        [(own_rows, 3 * part + lanes)] * size,
        bf16,
        lambda: [
            ((which, 0, part_column(behind(ahead))), (ahead, 0, which * part), (own_rows, part))
            for ahead in slots
            for which in range(3)
        ]
        + [((3, 0, 0), (ahead, 0, 3 * part), (own_rows, lanes)) for ahead in slots],
    )
    qkv_got = send_ahead(qkv_send, "seq")
    cube_down = CubeGather([w_down[: ff_own // 2], w_down[ff_own // 2 :]])
    cube_down.step()
    gate_send, up_send = ff_pack(w_gate), ff_pack(w_up)
    qkv_got, new, gate_send, up_send, x_own = together(qkv_got, cube_down.new, gate_send, up_send, tok_rows)
    cube_down.set(new)

    gate_got = send_ahead(gate_send, "seq")
    cube_qkv = CubeGather(two_parts(qkv_got), core=True)
    cube_qkv.step()
    gate_got, new, up_send = together(gate_got, cube_qkv.new, up_send)
    cube_qkv.set(new)
    up_got = send_ahead(up_send, "seq")
    cube_qkv.step()
    cube_gate = CubeGather(ff_pair(gate_got))
    up_got, new, x_own, gate_own = together(up_got, cube_qkv.new, x_own, cube_gate.arrays)
    cube_qkv.set(new)
    cube_gate.arrays = gate_own
    cube_up = CubeGather(ff_pair(up_got))
    cosine, sine_tab = rope_tables(positions(segments).reshape(total_len))

    x_slots = [x_own]
    for at in range(size - 1):
        x_next = next_one(x_slots[-1], "seq")
        if at == 0:
            cube_gate.step()
            cube_down.step()
            x_next, new = together(x_next, cube_gate.new)
            cube_gate.set(new)
        elif at == 1:
            cube_gate.step()
            cube_qkv.step()
            x_next, new, more, cosine, sine_tab = together(x_next, cube_down.new, cube_qkv.new, cosine, sine_tab)
            cube_down.set(new)
            cube_qkv.set(more)
        elif at == size - 2:
            cube_up.step()
            x_next, new, more, w_out_own = together(x_next, cube_gate.new, cube_up.new, w_out)
            cube_gate.set(new)
            cube_up.set(more)
        x_slots.append(x_next)
    cube_qkv.finish()
    w_qkv, gains = cube_join(
        cube_qkv, ((0, 0), (0, side // 2)), side, cuts=[(0, 3 * part), (3 * part, lanes)]
    )

    x_all = in_order(x_slots, "seq")
    out_got = share_out(w_out_own, "seq")
    cube_up.step()
    qkv = product(x_all, w_qkv)
    squares = jnp.stack([jnp.sum(jnp.square(qkv[:, first : first + part]), -1) for first in (0, part)], 0)
    squares = small_sum(squares, "seq")
    gains = gains[:, :4].T.astype(f32)
    gain_attn, gain_ffn = gains[2], gains[3]
    gain_qk = lax.dynamic_slice_in_dim(gains[:2], here * part, part, 1)
    squares, out_got, gain_qk = together(squares, out_got, gain_qk)
    cube_out = CubeGather(two_parts(out_got), core=True)
    cube_out.step()
    squares = squares.T
    query, key, value = query_key(qkv, squares, cosine, sine_tab, gain_qk, width)
    seg_ids = segments.reshape(total_len)
    attended = attend(query, key, value, seg_ids)
    attended = relayout(
        [attended],
        [(rows, part)] * size,
        bf16,
        lambda: [((0, part_row(behind(ahead)), 0), (ahead, 0, 0), (rows, part)) for ahead in slots],
    )
    attended, new, more = together(attended, cube_out.new, cube_up.new)
    cube_out.set(new)
    cube_up.set(more)
    attended = send_ahead(attended, "seq")
    cube_out.step()
    for cube in (cube_down, cube_gate, cube_up):
        cube.finish()
    w_down_part = cube_join(cube_down, ((0, 0), (0, ff_own // 2)), ff_own, 2)
    w_gate_part, w_up_part = [cube_join(cube, ((0, 0), (1, 0)), side) for cube in (cube_gate, cube_up)]
    attended, new, w_down_part, w_gate_part, w_up_part = together(
        attended, cube_out.new, w_down_part, w_gate_part, w_up_part
    )
    cube_out.set(new)
    cube_out.finish()
    w_out_all = cube_join(cube_out, ((0, 0), (0, side // 2)), side)
    attended = relayout(
        attended,
        [(rows, width)],
        bf16,
        lambda: [((back, 0, 0), (0, 0, part_column(before(back))), (rows, part)) for back in slots],
    )[0]

    a_proj = product(attended, w_out_all)
    a_scale = rms_scale(a_proj)
    hidden = tok_rows.astype(f32) + a_proj * a_scale * gain_attn

    def ring(block, work, beside=lambda: ()):
        got, own = None, None
        for at in range(size):
            later = next_one(block, "seq") if at < size - 1 else None
            share = work(stacked([block, flipped(block, 1)]))
            share, away = share[:rows], share[rows:].astype(bf16)
            if later is not None:
                later, share, away, got = together(later, share, away, got)
            share = share + flipped(away, 1).astype(f32)
            if at == 0:
                own = share
            else:
                if at > 1:
                    share = share + got.astype(f32)
                send, later = together(share.astype(bf16), later)
                got = next_one(send, "seq")
            block = later
        got, extra = together(got, beside(send))
        return own + got.astype(f32), extra

    h_slots, gates, ups, inners = [], [], [], []

    def forward(h_low):
        gate = product(h_low, w_gate_part)
        up = product(h_low, w_up_part)
        inner = (jax.nn.silu(gate) * up).astype(bf16)
        h_slots.append(h_low)
        gates.append(gate)
        ups.append(up)
        inners.append(inner)
        return product(inner, w_down_part)

    m_proj, _ = ring(hidden.astype(bf16), forward, lambda send: ())
    m_scale = rms_scale(m_proj)
    out = (hidden + m_proj * m_scale * gain_ffn).astype(bf16).reshape(tokens.shape)
    grad_out = d_out.reshape(rows, width).astype(f32)
    d_gain_ffn = jnp.sum(grad_out * m_proj * m_scale, 0)
    dm_low = norm_back(m_proj, m_scale, grad_out * gain_ffn).astype(bf16)
    dms, d_gates, d_ups = [], [], []

    def backward(dm_slot):
        at = len(dms)
        gate, up = gates[at], ups[at]
        if at == size - 1:
            d_gate, d_up, share = ffn_backward(dm_slot, gate, up, w_down_part, w_gate_part, w_up_part)
            dms.append(dm_slot)
            d_gates.append(d_gate)
            d_ups.append(d_up)
            return share
        d_inner = against(dm_slot, w_down_part)
        sigmoid_gate = jax.nn.sigmoid(gate)
        d_gate = (d_inner * up * sigmoid_gate * (1.0 + gate * (1.0 - sigmoid_gate))).astype(bf16)
        d_up = (d_inner * (gate * sigmoid_gate)).astype(bf16)
        dms.append(dm_slot)
        d_gates.append(d_gate)
        d_ups.append(d_up)
        return against(d_gate, w_gate_part) + against(d_up, w_up_part)

    def grads(send):
        _, all_gates = together(send, stacked(d_gates, 56 * 2**20))
        return grad_halves(h_all, all_gates, False)

    h_all = stacked(h_slots, 56 * 2**20)
    d_sum, d_gate = ring(dm_low, backward, grads)
    cube_gate = CubeScatter(d_gate)
    cube_gate.step()

    def ff_rows(total):
        core = lax.rem(lax.axis_index("dp"), 2)
        total = total.astype(bf16).reshape(2, side, ff_half)
        mine, away = [lax.dynamic_index_in_dim(total, c, 0, keepdims=False) for c in (core, 1 - core)]
        away = flipped(away, 1)

        def moves():
            return [
                ((which, pl.multiple_of(behind(ahead) * own_rows, own_rows), 0), (ahead, which * own_rows, 0), (own_rows, ff_half))
                for ahead in slots
                for which in (0, 1)
            ]

        return relayout([mine, away], [(2 * own_rows, ff_half)] * size, bf16, moves)

    def row_blocks(total):
        wide = total.shape[1]
        return relayout(
            [total],
            [(own_rows, wide)] * size,
            bf16,
            lambda: [
                ((0, pl.multiple_of(behind(ahead) * own_rows, own_rows), 0), (ahead, 0, 0), (own_rows, wide))
                for ahead in slots
            ],
        )

    d_hidden = grad_out + d_sum
    d_gain_attn = jnp.sum(d_hidden * a_proj * a_scale, 0)
    da_low = norm_back(a_proj, a_scale, d_hidden * gain_attn).astype(bf16)
    d_attended = against(da_low, w_out_all).astype(bf16)
    d_attended = relayout(
        [d_attended],
        [(rows, part)] * size,
        bf16,
        lambda: [((0, 0, part_column(behind(ahead))), (ahead, 0, 0), (rows, part)) for ahead in slots],
    )
    all_ups = stacked(d_ups, 56 * 2**20)
    d_attended, cube_gate.got, da_low, all_ups = together(d_attended, cube_gate.got, da_low, all_ups)
    d_attended = send_ahead(d_attended, "seq")
    cube_gate.step()
    d_up = grad_halves(h_all, all_ups, False)
    d_w_out = grad_halves(attended, da_low, True)
    d_attended, d_w_out, cube_gate.got, d_up = together(d_attended, d_w_out, cube_gate.got, d_up)
    d_attended = in_order(d_attended, "seq")

    cube_up = CubeScatter(d_up)
    cube_up.step()
    gate_got = send_ahead(ff_rows(cube_gate.finish()), "seq")
    d_query, d_key, d_value = attend_back(query, key, value, d_attended, seg_ids)
    d_query, gate_got, cube_up.got, d_w_out = together(d_query, gate_got, cube_up.got, d_w_out)
    cube_up.step()
    dots, d_gain_qk = unrope(d_query, d_key, qkv, squares, cosine, sine_tab, gain_qk, width)
    dots = small_sum(dots.T, "seq")
    dots, cube_up.got, d_w_out = together(dots, cube_up.got, d_w_out)
    up_send = ff_rows(cube_up.finish())
    up_got = send_ahead(up_send, "seq")
    cube_out = CubeScatter(d_w_out, core=True)
    cube_out.step()
    d_qkv = raw_grad(d_query, d_key, d_value, qkv, squares, dots.T, cosine, sine_tab, gain_qk, width)
    d_slots = relayout(
        [d_qkv],
        [(rows, 3 * part)] * size,
        bf16,
        lambda: [((0, part_row(before(back)), 0), (back, 0, 0), (rows, 3 * part)) for back in slots],
    )
    d_slots, cube_out.got = together(d_slots, cube_out.got)
    cube_out.prepare()
    first, d_qkv, d_slots, d_gain_qk, up_got, cube_out.away, dms, d_gain_attn = together(
        against(d_slots[1], w_qkv).astype(bf16), d_qkv, d_slots, d_gain_qk, up_got, cube_out.away, dms, d_gain_attn
    )
    got = next_one(first, "seq")
    cube_out.send()
    d_gain_qk = lax.dynamic_update_slice_in_dim(jnp.zeros((2, width), f32), d_gain_qk, here * part, 1)
    d_gains = jnp.concatenate([d_gain_qk, d_gain_attn[None], d_gain_ffn[None]], 0)
    d_w_qkv = grad_halves(x_all, d_qkv, True)
    shares = [against(d_slots[2], w_qkv)]
    got, d_w_qkv, shares, cube_out.got, d_slots, dms, d_gains = together(
        got, d_w_qkv, shares, cube_out.got, d_slots, dms, d_gains
    )
    cube_qkv = CubeScatter(d_w_qkv, core=True)
    for back in range(2, size):
        got = next_one((shares[back - 2] + got.astype(f32)).astype(bf16), "seq")
        if back == 2:
            cube_qkv.step()
            cube_out.step()
            shares += [against(d_slots[at], w_qkv) for at in [*slots[3:], 0]]
            got, shares, cube_out.got, cube_qkv.got, dms = together(got, shares, cube_out.got, cube_qkv.got, dms)
        elif back == 3:
            cube_qkv.step()
            out_got = send_ahead(row_blocks(cube_out.finish()), "seq")
            d_down = grad_halves(stacked(inners, 56 * 2**20), stacked(dms, 56 * 2**20), False)
            got, cube_qkv.got, d_down = together(got, cube_qkv.got, d_down)
            cube_down = CubeScatter(d_down)
            cube_down.step()
    d_w_qkv = row_blocks(cube_qkv.finish())
    d_w_qkv, out_got, cube_down.got, d_gains = together(d_w_qkv, out_got, cube_down.got, d_gains)
    d_w_qkv = send_ahead(d_w_qkv, "seq")
    d_down = cube_down.finish()
    d_gains = small_sum(d_gains, "seq")
    for bit in [1] + cube_bits()[0]:
        d_gains = d_gains + flipped(d_gains.reshape(-1), bit).reshape(d_gains.shape)
    d_gains = lax.dynamic_slice_in_dim(d_gains, (lax.axis_index("dp") * size + here) * own_rows, own_rows, 1)
    d_tokens = d_hidden + shares[-1] + got.astype(f32)
    d_w_out = sum(g.astype(f32) for g in out_got)
    d_w_qkv = relayout(
        d_w_qkv,
        [(own_rows, width)] * 3,
        f32,
        lambda: [
            ((back, 0, which * part), (which, 0, part_column(before(back))), (own_rows, part))
            for back in slots
            for which in range(3)
        ],
    )
    d_w_gate, d_w_up = ff_unpack(gate_got), ff_unpack(up_got)
    return (
        out,
        d_tokens.reshape(tokens.shape),
        d_w_qkv[0],
        d_w_qkv[1],
        d_w_qkv[2],
        d_w_out,
        d_gains[0],
        d_gains[1],
        d_gains[2],
        d_w_gate,
        d_w_up,
        d_down,
        d_gains[3],
    )


def solution(mesh):
    rows = P("dp", "seq", None)
    mat = P(("dp", "seq"), None)
    vec = P(("dp", "seq"))
    in_specs = (rows, P("dp", None), mat, mat, mat, mat, vec, vec, vec, mat, mat, mat, vec, rows)
    out_specs = (rows, rows, mat, mat, mat, mat, vec, vec, vec, mat, mat, mat, vec)
    return jax.shard_map(local, mesh=mesh, in_specs=in_specs, out_specs=out_specs, check_vma=False)
```

```python
import functools

import jax
import jax.numpy as jnp
from jax import lax
from jax.experimental import pallas as pl
from jax.experimental.pallas import tpu as pltpu
from jax.sharding import PartitionSpec as P

H = 16
HD = 128
DOCS = 4

epsilon = 1e-06
rope_base = 500000.0
masked_score = -1e30
bf16 = jnp.bfloat16
f32 = jnp.float32


def product(left, right):
    return jnp.dot(left, right, preferred_element_type=f32)


def against(left, right):
    return lax.dot_general(left, right, (((1,), (1,)), ((), ())), preferred_element_type=f32)


def weight_grad(left, right):
    return lax.dot_general(left, right, (((0,), (0,)), ((), ())), preferred_element_type=f32)


def rms_scale(values):
    return lax.rsqrt(jnp.mean(values * values, -1, keepdims=True) + epsilon)


def norm_back(values, scale_rows, grad_vals):
    return scale_rows * grad_vals - values * scale_rows**3 * jnp.mean(
        grad_vals * values, -1, keepdims=True
    )


def positions(seg_ids):
    doc_ids = jnp.arange(DOCS, dtype=jnp.int32)
    starts = jnp.sum((seg_ids[..., None, :] < doc_ids[:, None]).astype(jnp.int32), -1)
    one_hot = (seg_ids[..., None] == doc_ids).astype(jnp.int32)
    token_start = jnp.sum(one_hot * starts[..., None, :], axis=-1)
    return jnp.arange(seg_ids.shape[-1], dtype=jnp.int32) - token_start


def rope_tables(position_ids):
    freqs = rope_base ** (-jnp.arange(HD // 2, dtype=f32) * 2.0 / HD)
    angles = position_ids.astype(f32)[..., None] * freqs
    cosine = jnp.cos(angles)
    sine_tab = jnp.sin(angles)
    return (
        jnp.concatenate([cosine, cosine], -1),
        jnp.concatenate([sine_tab, sine_tab], -1),
    )


def contract(left, right, left_dim, right_dim):
    return lax.dot_general(left, right, (((left_dim,), (right_dim,)), ((), ())), preferred_element_type=f32)


def vmem(shape, index=None):
    return pl.BlockSpec(shape, index or (lambda *_: (0,) * len(shape)))


def kernel_params(grid=0):
    return pltpu.CompilerParams(vmem_limit_bytes=48 * 2**20)


def relayout_body(moves, count, *refs):
    ins, outs = refs[:count], refs[count:]
    for (src, src_row, src_col), (dst, dst_row, dst_col), (rows, cols) in moves():
        outs[dst][pl.ds(dst_row, rows), pl.ds(dst_col, cols)] = ins[src][
            pl.ds(src_row, rows), pl.ds(src_col, cols)
        ].astype(outs[dst].dtype)


def relayout(arrays, shapes, dtype, moves):
    outs = [jax.ShapeDtypeStruct(shape, dtype) for shape in shapes]
    size = sum(a.size * a.dtype.itemsize for a in [*arrays, *outs])
    return pl.pallas_call(
        functools.partial(relayout_body, moves, len(arrays)),
        in_specs=[vmem(a.shape) for a in arrays],
        out_specs=[vmem(o.shape) for o in outs],
        out_shape=outs,
        compiler_params=kernel_params(),
        cost_estimate=pl.CostEstimate(flops=0, bytes_accessed=size, transcendentals=0),
    )(*arrays)


def turned(values):
    lane = lax.broadcasted_iota(jnp.int32, values.shape, 1)
    rolled = pltpu.roll(values, HD // 2, 1)
    return jnp.where(lane < HD // 2, -rolled, rolled)


def query_key_body(width, raw_ref, squares_ref, cos_ref, sin_ref, gain_ref, q_ref, k_ref, v_ref):
    part = q_ref.shape[1]
    scales = lax.rsqrt(squares_ref[...] / width + epsilon)
    for which, out in enumerate((q_ref, k_ref)):
        for first in range(0, part, HD):
            gain = gain_ref[which : which + 1, first : first + HD]
            unit = raw_ref[:, which * part + first : which * part + first + HD] * scales[:, which : which + 1] * gain
            out[:, first : first + HD] = (unit * cos_ref[...] + turned(unit) * sin_ref[...]).astype(bf16)
    v_ref[...] = raw_ref[:, 2 * part :].astype(bf16)


def query_key(raw, squares, cosine, sine_tab, gains, width):
    tokens, part = raw.shape[0], raw.shape[1] // 3
    block = min(256, tokens)
    shape = jax.ShapeDtypeStruct((tokens, part), bf16)

    def by_rows(cols):
        return vmem((block, cols), lambda at: (at, 0))

    return pl.pallas_call(
        functools.partial(query_key_body, width),
        grid=(tokens // block,),
        in_specs=[by_rows(3 * part), by_rows(2), by_rows(HD), by_rows(HD), vmem(gains.shape)],
        out_specs=[by_rows(part)] * 3,
        out_shape=[shape] * 3,
        compiler_params=kernel_params(),
    )(raw, squares, cosine, sine_tab, gains)


def ffn_backward_body(steps, left_ref, down_w, gate_ref, up_ref, gate_w, up_w, d_gate_ref, d_up_ref, share_ref):
    step = pl.program_id(0)
    d_inner = contract(left_ref[...], down_w[...], 1, 1)
    gate = gate_ref[...]
    sigmoid = jax.nn.sigmoid(gate)
    d_gate = (d_inner * up_ref[...] * sigmoid * (1.0 + gate * (1.0 - sigmoid))).astype(bf16)
    d_up = (d_inner * (gate * sigmoid)).astype(bf16)
    d_gate_ref[...] = d_gate
    d_up_ref[...] = d_up
    share = contract(d_gate, gate_w[...], 1, 1) + contract(d_up, up_w[...], 1, 1)

    @pl.when(step == 0)
    def _():
        share_ref[...] = share

    if steps > 1:

        @pl.when(step > 0)
        def _():
            share_ref[...] += share


def ffn_backward(left, gate, up, w_down, w_gate, w_up):
    rows, width = left.shape
    extent = gate.shape[1]
    tile = min(512, extent)
    by_columns = vmem((rows, tile), lambda at: (0, at))
    return pl.pallas_call(
        functools.partial(ffn_backward_body, extent // tile),
        grid=(extent // tile,),
        in_specs=[
            vmem(left.shape),
            vmem((tile, width), lambda at: (at, 0)),
            by_columns,
            by_columns,
            vmem((width, tile), lambda at: (0, at)),
            vmem((width, tile), lambda at: (0, at)),
        ],
        out_specs=[by_columns, by_columns, vmem(left.shape)],
        out_shape=[
            jax.ShapeDtypeStruct(gate.shape, bf16),
            jax.ShapeDtypeStruct(gate.shape, bf16),
            jax.ShapeDtypeStruct(left.shape, f32),
        ],
        compiler_params=kernel_params(),
        cost_estimate=pl.CostEstimate(
            flops=6 * rows * width * extent, bytes_accessed=6 * width * extent, transcendentals=rows * extent
        ),
    )(left, w_down, gate, up, w_gate, w_up)


def grad_halves_body(left_ref, right_ref, one_ref, two_ref):
    total = contract(left_ref[...], right_ref[...], 0, 0).astype(bf16)
    cut = one_ref.shape[1]
    one_ref[...] = total[:, :cut]
    two_ref[...] = total[:, cut:]


def grad_halves(left, right, core):
    bits = (lax.axis_size("dp") - 1).bit_length() - (not core)
    (tokens, depth), cut = left.shape, right.shape[1] // 2
    block = min(256, depth)
    half = jax.ShapeDtypeStruct((depth, cut), bf16)
    halves = pl.pallas_call(
        grad_halves_body,
        grid=(depth // block,),
        in_specs=[vmem((tokens, block), lambda at: (0, at)), vmem(right.shape)],
        out_specs=[vmem((block, cut), lambda at: (at, 0))] * 2,
        out_shape=[half, half],
        compiler_params=kernel_params(),
        cost_estimate=pl.CostEstimate(
            flops=4 * tokens * depth * cut, bytes_accessed=4 * tokens * depth, transcendentals=0
        ),
    )(left, right)
    return [half.reshape((2,) * bits + (-1, cut)) for half in halves]


def key_weights(query, key, seg_query, seg_key, first, count):
    scores = contract(key, query, 1, 1) * HD ** (-0.5)
    shape = scores.shape
    allowed = (seg_key == seg_query) & (
        lax.broadcasted_iota(jnp.int32, shape, 0) <= first + lax.broadcasted_iota(jnp.int32, shape, 1)
    )
    scores = jnp.where(allowed, scores, masked_score)
    expos = jnp.exp(scores - jnp.max(scores, 0, keepdims=True))
    return expos * (1.0 / jnp.sum(expos, 0, keepdims=True))


def attend_body(blocks, q_ref, k_ref, v_ref, seg_q_ref, seg_k_ref, out_ref):
    rows = q_ref.shape[0]
    for at in range(blocks):
        seen = (at + 1) * rows

        @pl.when(pl.program_id(1) == at)
        def _():
            probs = key_weights(
                q_ref[...], k_ref[:seen], seg_q_ref[...], seg_k_ref[:seen], at * rows, seen
            ).astype(bf16)
            out_ref[...] = contract(probs, v_ref[:seen], 0, 0).astype(bf16)


def attention_specs(tokens, block):
    by_query = vmem((block, HD), lambda head, at: (at, head))
    by_head = vmem((tokens, HD), lambda head, at: (0, head))
    return by_query, by_head, [vmem((1, block), lambda head, at: (0, at)), vmem((tokens, 1))]


def attend(query, key, value, seg_ids):
    tokens, part = query.shape
    block = min(256, tokens)
    by_query, by_head, segs = attention_specs(tokens, block)
    return pl.pallas_call(
        functools.partial(attend_body, tokens // block),
        grid=(part // HD, tokens // block),
        in_specs=[by_query, by_head, by_head, *segs],
        out_specs=by_query,
        out_shape=jax.ShapeDtypeStruct(query.shape, bf16),
        compiler_params=kernel_params(),
    )(query, key, value, seg_ids[None, :], seg_ids[:, None])


def attend_back_body(
    blocks, q_ref, k_ref, v_ref, g_ref, seg_q_ref, seg_k_ref, dq_ref, dk_ref, dv_ref, dk_sum, dv_sum
):
    rows = q_ref.shape[0]
    scale = HD ** (-0.5)
    for at in range(blocks):
        seen = (at + 1) * rows

        @pl.when(pl.program_id(1) == at)
        def _():
            query, grad = q_ref[...], g_ref[...]
            probs = key_weights(query, k_ref[:seen], seg_q_ref[...], seg_k_ref[:seen], at * rows, seen)
            d_probs = contract(v_ref[:seen], grad, 1, 1)
            inner = jnp.sum(probs * d_probs, 0, keepdims=True)
            d_scores = (probs * (d_probs - inner)).astype(bf16)
            dq_ref[...] = (contract(d_scores, k_ref[:seen], 0, 0) * scale).astype(bf16)
            d_key = contract(d_scores, query, 1, 0) * scale
            d_value = contract(probs.astype(bf16), grad, 1, 0)
            old = seen - rows
            dk_sum[old:seen] = d_key[old:]
            dv_sum[old:seen] = d_value[old:]
            if at:
                dk_sum[:old] += d_key[:old]
                dv_sum[:old] += d_value[:old]
            if at == blocks - 1:
                dk_ref[...] = dk_sum[...].astype(bf16)
                dv_ref[...] = dv_sum[...].astype(bf16)


def attend_back(query, key, value, grad, seg_ids):
    tokens, part = query.shape
    block = min(256, tokens)
    by_query, by_head, segs = attention_specs(tokens, block)
    shape = jax.ShapeDtypeStruct(query.shape, bf16)
    return pl.pallas_call(
        functools.partial(attend_back_body, tokens // block),
        grid=(part // HD, tokens // block),
        in_specs=[by_query, by_head, by_head, by_query, *segs],
        out_specs=[by_query, by_head, by_head],
        out_shape=[shape] * 3,
        scratch_shapes=[pltpu.VMEM((tokens, HD), f32)] * 2,
        compiler_params=kernel_params(),
    )(query, key, value, grad, seg_ids[None, :], seg_ids[:, None])


def rope_back(grad, cosine, sine_tab):
    return grad * cosine - turned(grad * sine_tab)


def unrope_body(width, dq_ref, dk_ref, raw_ref, squares_ref, cos_ref, sin_ref, gain_ref, dots_ref, gains_ref):
    part = dq_ref.shape[1]
    scales = lax.rsqrt(squares_ref[...] / width + epsilon)

    @pl.when(pl.program_id(0) == 0)
    def _():
        gains_ref[...] = jnp.zeros_like(gains_ref)

    for which, ref in enumerate((dq_ref, dk_ref)):
        dots = 0.0
        for first in range(0, part, HD):
            raw = raw_ref[:, which * part + first : which * part + first + HD]
            grad = rope_back(ref[:, first : first + HD].astype(f32), cos_ref[...], sin_ref[...])
            both = grad * raw
            gain = gain_ref[which : which + 1, first : first + HD]
            dots = dots + jnp.sum(both * gain, 1, keepdims=True)
            gains_ref[which : which + 1, first : first + HD] += jnp.sum(
                both * scales[:, which : which + 1], 0, keepdims=True
            )
        dots_ref[:, which : which + 1] = dots


def unrope(d_query, d_key, raw, squares, cosine, sine_tab, gains, width):
    tokens, part = d_query.shape
    block = min(256, tokens)

    def by_rows(cols):
        return vmem((block, cols), lambda at: (at, 0))

    return pl.pallas_call(
        functools.partial(unrope_body, width),
        grid=(tokens // block,),
        in_specs=[by_rows(part)] * 2
        + [by_rows(3 * part), by_rows(2), by_rows(HD), by_rows(HD), vmem(gains.shape)],
        out_specs=[by_rows(2), vmem((2, part))],
        out_shape=[jax.ShapeDtypeStruct((tokens, 2), f32), jax.ShapeDtypeStruct((2, part), f32)],
        compiler_params=kernel_params(),
    )(d_query, d_key, raw, squares, cosine, sine_tab, gains)


def raw_grad_body(width, dq_ref, dk_ref, dv_ref, raw_ref, squares_ref, dots_ref, cos_ref, sin_ref, gain_ref, out_ref):
    part = dq_ref.shape[1]
    scales = lax.rsqrt(squares_ref[...] / width + epsilon)
    cubes = scales * scales * scales * dots_ref[...] / width
    for which, ref in enumerate((dq_ref, dk_ref)):
        for first in range(0, part, HD):
            at = slice(which * part + first, which * part + first + HD)
            grad = rope_back(ref[:, first : first + HD].astype(f32), cos_ref[...], sin_ref[...])
            grad = grad * gain_ref[which : which + 1, first : first + HD]
            out_ref[:, at] = (
                scales[:, which : which + 1] * grad - raw_ref[:, at] * cubes[:, which : which + 1]
            ).astype(bf16)
    out_ref[:, 2 * part :] = dv_ref[...]


def raw_grad(d_query, d_key, d_value, raw, squares, dots, cosine, sine_tab, gains, width):
    tokens, part = d_query.shape
    block = min(256, tokens)

    def by_rows(cols):
        return vmem((block, cols), lambda at: (at, 0))

    return pl.pallas_call(
        functools.partial(raw_grad_body, width),
        grid=(tokens // block,),
        in_specs=[by_rows(part)] * 3
        + [by_rows(3 * part), by_rows(2), by_rows(2), by_rows(HD), by_rows(HD), vmem(gains.shape)],
        out_specs=by_rows(3 * part),
        out_shape=jax.ShapeDtypeStruct((tokens, 3 * part), bf16),
        compiler_params=kernel_params(),
    )(d_query, d_key, d_value, raw, squares, dots, cosine, sine_tab, gains)


def together(*trees):
    return lax.optimization_barrier(trees)


def next_one(block, axis):
    size = lax.axis_size(axis)
    return lax.ppermute(block, axis, [(i, (i + 1) % size) for i in range(size)])


def flipped(block, bit):
    size = lax.axis_size("dp")
    return lax.ppermute(block, "dp", [(i, i ^ bit) for i in range(size)])


def exchange(blocks, axis):
    size, here = lax.axis_size(axis), lax.axis_index(axis)
    got = []
    for step in range(size):
        block = lax.dynamic_index_in_dim(blocks, lax.rem(here + step, size), 0, keepdims=False)
        if step:
            block = lax.ppermute(block, axis, [(i, (i + step) % size) for i in range(size)])
        got.append(block)
    return got


def send_ahead(blocks, axis):
    size = lax.axis_size(axis)
    return [blocks[0]] + [
        lax.ppermute(blocks[step], axis, [(i, (i + step) % size) for i in range(size)]) for step in range(1, size)
    ]


def share_out(block, axis):
    size = lax.axis_size(axis)
    return [block] + [
        lax.ppermute(block, axis, [(i, (i + step) % size) for i in range(size)]) for step in range(1, size)
    ]


def assemble_body(parts, places, count, cuts, *refs):
    pieces, outs, (held, in_sems, out_sems) = refs[:count], refs[count : count + len(cuts)], refs[count + len(cuts) :]
    reads, writes, first = [], [], 0
    for at, ((which, start, rows), place) in enumerate(zip(parts, places())):
        here = held.at[pl.ds(first, rows)]
        reads.append(pltpu.make_async_copy(pieces[which].at[pl.ds(start, rows)], here, in_sems.at[at]))
        writes.append(
            [
                pltpu.make_async_copy(
                    held.at[pl.ds(first, rows), pl.ds(left, wide)],
                    out.at[pl.ds(place, rows)],
                    out_sems.at[at * len(cuts) + n],
                )
                for n, (out, (left, wide)) in enumerate(zip(outs, cuts))
            ]
        )
        first += rows
    for read in reads:
        read.start()
    for read, copies in zip(reads, writes):
        read.wait()
        for write in copies:
            write.start()
    for copies in writes:
        for write in copies:
            write.wait()


def assemble(pieces, parts, places, cuts=None, room=0):
    shape = (sum(rows for _, _, rows in parts), pieces[0].shape[1])
    several, cuts = cuts is not None, cuts or [(0, shape[1])]
    anywhere = pl.BlockSpec(memory_space=pl.ANY)
    dtype = pieces[0].dtype
    size = shape[0] * shape[1] * dtype.itemsize
    results = pl.pallas_call(
        functools.partial(assemble_body, parts, places, len(pieces), cuts),
        in_specs=[anywhere] * len(pieces),
        out_specs=[anywhere] * len(cuts),
        out_shape=[jax.ShapeDtypeStruct((shape[0], wide), dtype) for _, wide in cuts],
        scratch_shapes=[
            pltpu.VMEM(shape, dtype),
            pltpu.SemaphoreType.DMA((len(parts),)),
            pltpu.SemaphoreType.DMA((len(parts) * len(cuts),)),
        ],
        compiler_params=pltpu.CompilerParams(vmem_limit_bytes=max(room, size + 2**20)),
        cost_estimate=pl.CostEstimate(flops=0, bytes_accessed=2 * size, transcendentals=0),
    )(*pieces)
    return results if several else results[0]


def stacked(pieces, room=0):
    parts = [(at, 0, p.shape[0]) for at, p in enumerate(pieces)]
    places = [sum(rows for _, _, rows in parts[:at]) for at in range(len(parts))]
    return assemble(pieces, parts, lambda: places, room=room)


def in_order(slots, axis, first=0, rows=None):
    size, rows = len(slots), rows or slots[0].shape[0]

    def places():
        here = lax.axis_index(axis)
        return [pl.multiple_of(lax.rem(here + (size - back), size) * rows, rows) for back in range(size)]

    return assemble(slots, [(at, first, rows) for at in range(size)], places)


def cube_bits():
    bits = [1 << b for b in range(1, (lax.axis_size("dp") - 1).bit_length())]
    return bits, bits[1:] + bits[:1]


class CubeGather:
    def __init__(self, pair, core=False):
        self.arrays = [[block] for block in pair]
        self.masks = [[[0]] for _ in pair]
        self.orders = [list(bits) + [1] * core for bits in cube_bits()]
        self.new = []

    def step(self):
        for at, arrays in enumerate(self.arrays):
            if len(arrays) > 1:
                self.arrays[at] = [stacked(arrays)]
                self.masks[at] = [sum(self.masks[at], [])]
        self.new = [flipped(arrays[0], order[0]) for arrays, order in zip(self.arrays, self.orders)]

    def set(self, new):
        for at, block in enumerate(new):
            bit = self.orders[at].pop(0)
            self.arrays[at].append(block)
            self.masks[at].append([m ^ bit for m in self.masks[at][0]])
        self.new = []

    def finish(self):
        self.set(self.new)
        while self.orders[0]:
            self.step()
            self.set(self.new)


def cube_join(cube, firsts, rows, fold=1, cuts=None):
    pieces, parts, where = [], [], []
    for (own, first), arrays, masks in zip(firsts, cube.arrays, cube.masks):
        step = arrays[0].shape[0] // len(masks[0])
        for array, blocks in zip(arrays, masks):
            for at, mask in enumerate(blocks):
                parts.append((len(pieces), at * step, step))
                where.append((own ^ mask, first))
            pieces.append(array)

    def places():
        here = lax.axis_index("dp")
        return [pl.multiple_of((here ^ mask) // fold * rows + first, step) for mask, first in where]

    return assemble(pieces, parts, places, cuts)


class CubeScatter:
    def __init__(self, pair, core=False):
        self.totals, self.got = list(pair), None
        self.orders = [[1] * core + list(bits) for bits in cube_bits()]
        self.dims = [sorted(order, reverse=True) for order in self.orders]

    def add(self):
        if self.got:
            self.totals = [t.astype(f32) + g.astype(f32) for t, g in zip(self.totals, self.got)]
        self.got = None
        return self.totals

    def prepare(self):
        self.add()
        self.away, self.bits = [], [order.pop(0) for order in self.orders]
        for which, (total, bit) in enumerate(zip(self.totals, self.bits)):
            at = self.dims[which].index(bit)
            self.dims[which].remove(bit)
            mine = (lax.axis_index("dp") // bit) % 2
            self.away.append(lax.dynamic_index_in_dim(total, 1 - mine, at, keepdims=False).astype(bf16))
            self.totals[which] = lax.dynamic_index_in_dim(total, mine, at, keepdims=False)

    def send(self):
        self.got = [flipped(away, bit) for away, bit in zip(self.away, self.bits)]

    def step(self):
        self.prepare()
        self.send()

    def finish(self):
        while self.orders[0]:
            self.step()
        return jnp.concatenate(self.add(), 1)


def small_sum(values, axis):
    return sum(share_out(values.reshape(-1), axis)).reshape(values.shape)


def local(
    tokens,
    segments,
    w_query,
    w_key,
    w_value,
    w_out,
    g_query,
    g_key,
    g_attn,
    w_gate,
    w_up,
    w_down,
    g_ffn,
    d_out,
):
    seqs, local_len, width = tokens.shape
    rows = seqs * local_len
    copies, size = lax.axis_size("dp"), lax.axis_size("seq")
    here = lax.axis_index("seq")
    total_len = size * local_len
    part = width // size
    heads = H // size
    own_rows = w_gate.shape[0]
    ff_width = w_gate.shape[1]
    ff_part = ff_width // size
    ff_own = w_down.shape[0]
    tok_rows = tokens.reshape(rows, width)

    side = width // copies
    pairs = copies // 2
    ff_half = ff_part // 2
    slots = range(size)

    def before(back):
        return lax.rem(lax.axis_index("seq") + (size - back), size)

    def behind(ahead):
        return lax.rem(lax.axis_index("seq") + ahead, size)

    def ff_column(pair, other, seq_at):
        return pl.multiple_of(((pair * 2 + (lax.rem(lax.axis_index("dp"), 2) ^ other)) * size + seq_at) * ff_own, ff_own)

    def ff_pack(weight):
        if ff_own % 128:
            core = lax.rem(lax.axis_index("dp"), 2)
            blocks = weight.reshape(own_rows, pairs, 2, size, ff_own).transpose(2, 3, 0, 1, 4)
            blocks = blocks.reshape(2, size, own_rows, ff_half)
            blocks = jnp.concatenate(
                [lax.dynamic_index_in_dim(blocks, c, 0, keepdims=False) for c in (core, 1 - core)], 1
            )
            return [lax.dynamic_index_in_dim(blocks, behind(ahead), 0, keepdims=False) for ahead in slots]
        return relayout(
            [weight],
            [(2 * own_rows, ff_half)] * size,
            bf16,
            lambda: [
                ((0, 0, ff_column(pair, other, behind(ahead))), (ahead, other * own_rows, pair * ff_own), (own_rows, ff_own))
                for ahead in slots
                for other in (0, 1)
                for pair in range(pairs)
            ],
        )

    def ff_unpack(got):
        if ff_own % 128:
            core = lax.rem(lax.axis_index("dp"), 2)
            joined = in_order(got, "seq").reshape(size, 2, own_rows, pairs, ff_own)
            joined = jnp.where(core == 0, joined, joined[:, ::-1])
            return joined.transpose(2, 3, 1, 0, 4).reshape(own_rows, ff_width).astype(f32)
        return relayout(
            got,
            [(own_rows, ff_width)],
            f32,
            lambda: [
                ((back, other * own_rows, pair * ff_own), (0, 0, ff_column(pair, other, before(back))), (own_rows, ff_own))
                for back in slots
                for other in (0, 1)
                for pair in range(pairs)
            ],
        )[0]

    def ff_pair(got):
        mine, away = [in_order(got, "seq", first, own_rows) for first in (0, own_rows)]
        return [mine, flipped(away, 1)]

    def two_parts(got):
        joined = in_order(got, "seq")
        return [joined[: side // 2], joined[side // 2 :]]

    def part_column(seq_at):
        return pl.multiple_of(seq_at * part, part)

    def part_row(seq_at):
        return pl.multiple_of(seq_at * rows, rows)

    lanes = 128
    own_gains = jnp.stack([g_query, g_key, g_attn, g_ffn], 1)
    own_gains = jnp.pad(own_gains, ((0, 0), (0, lanes - own_gains.shape[1])))
    qkv_send = relayout(
        [w_query, w_key, w_value, own_gains],
        [(own_rows, 3 * part + lanes)] * size,
        bf16,
        lambda: [
            ((which, 0, part_column(behind(ahead))), (ahead, 0, which * part), (own_rows, part))
            for ahead in slots
            for which in range(3)
        ]
        + [((3, 0, 0), (ahead, 0, 3 * part), (own_rows, lanes)) for ahead in slots],
    )
    qkv_got = send_ahead(qkv_send, "seq")
    cube_down = CubeGather([w_down[: ff_own // 2], w_down[ff_own // 2 :]])
    cube_down.step()
    gate_send, up_send = ff_pack(w_gate), ff_pack(w_up)
    qkv_got, new, gate_send, up_send, x_own = together(qkv_got, cube_down.new, gate_send, up_send, tok_rows)
    cube_down.set(new)

    gate_got = send_ahead(gate_send, "seq")
    cube_qkv = CubeGather(two_parts(qkv_got), core=True)
    cube_qkv.step()
    gate_got, new, up_send = together(gate_got, cube_qkv.new, up_send)
    cube_qkv.set(new)
    up_got = send_ahead(up_send, "seq")
    cube_qkv.step()
    cube_gate = CubeGather(ff_pair(gate_got))
    up_got, new, x_own, gate_own = together(up_got, cube_qkv.new, x_own, cube_gate.arrays)
    cube_qkv.set(new)
    cube_gate.arrays = gate_own
    cube_up = CubeGather(ff_pair(up_got))
    cosine, sine_tab = rope_tables(positions(segments).reshape(total_len))

    x_slots = [x_own]
    for at in range(size - 1):
        x_next = next_one(x_slots[-1], "seq")
        if at == 0:
            cube_gate.step()
            cube_down.step()
            x_next, new = together(x_next, cube_gate.new)
            cube_gate.set(new)
        elif at == 1:
            cube_gate.step()
            cube_qkv.step()
            x_next, new, more, cosine, sine_tab = together(x_next, cube_down.new, cube_qkv.new, cosine, sine_tab)
            cube_down.set(new)
            cube_qkv.set(more)
        elif at == size - 2:
            cube_up.step()
            x_next, new, more, w_out_own = together(x_next, cube_gate.new, cube_up.new, w_out)
            cube_gate.set(new)
            cube_up.set(more)
        x_slots.append(x_next)
    cube_qkv.finish()
    w_qkv, gains = cube_join(
        cube_qkv, ((0, 0), (0, side // 2)), side, cuts=[(0, 3 * part), (3 * part, lanes)]
    )

    x_all = in_order(x_slots, "seq")
    out_got = share_out(w_out_own, "seq")
    cube_up.step()
    qkv = product(x_all, w_qkv)
    squares = jnp.stack([jnp.sum(jnp.square(qkv[:, first : first + part]), -1) for first in (0, part)], 0)
    squares = small_sum(squares, "seq")
    gains = gains[:, :4].T.astype(f32)
    gain_attn, gain_ffn = gains[2], gains[3]
    gain_qk = lax.dynamic_slice_in_dim(gains[:2], here * part, part, 1)
    squares, out_got, gain_qk = together(squares, out_got, gain_qk)
    cube_out = CubeGather(two_parts(out_got), core=True)
    cube_out.step()
    squares = squares.T
    query, key, value = query_key(qkv, squares, cosine, sine_tab, gain_qk, width)
    seg_ids = segments.reshape(total_len)
    attended = attend(query, key, value, seg_ids)
    attended = relayout(
        [attended],
        [(rows, part)] * size,
        bf16,
        lambda: [((0, part_row(behind(ahead)), 0), (ahead, 0, 0), (rows, part)) for ahead in slots],
    )
    attended, new, more = together(attended, cube_out.new, cube_up.new)
    cube_out.set(new)
    cube_up.set(more)
    attended = send_ahead(attended, "seq")
    cube_out.step()
    for cube in (cube_down, cube_gate, cube_up):
        cube.finish()
    w_down_part = cube_join(cube_down, ((0, 0), (0, ff_own // 2)), ff_own, 2)
    w_gate_part, w_up_part = [cube_join(cube, ((0, 0), (1, 0)), side) for cube in (cube_gate, cube_up)]
    attended, new, w_down_part, w_gate_part, w_up_part = together(
        attended, cube_out.new, w_down_part, w_gate_part, w_up_part
    )
    cube_out.set(new)
    cube_out.finish()
    w_out_all = cube_join(cube_out, ((0, 0), (0, side // 2)), side)
    attended = relayout(
        attended,
        [(rows, width)],
        bf16,
        lambda: [((back, 0, 0), (0, 0, part_column(before(back))), (rows, part)) for back in slots],
    )[0]

    a_proj = product(attended, w_out_all)
    a_scale = rms_scale(a_proj)
    hidden = tok_rows.astype(f32) + a_proj * a_scale * gain_attn

    def ring(block, work, beside=lambda: ()):
        got, own, held = None, None, block
        for at in range(size):
            later = next_one(block, "seq") if at < size - 1 else None
            share = work(stacked([held, flipped(held, 1)]))
            share, away = share[:rows], share[rows:].astype(bf16)
            if later is not None:
                later, share, away, got = together(later, share, away, got)
            share = share + flipped(away, 1).astype(f32)
            if at == 0:
                own = share
            else:
                if at > 1:
                    share = share + got.astype(f32)
                send, held = together(share.astype(bf16), later)
                got = next_one(send, "seq")
            block, held = later, later if at == 0 else held
        got, extra = together(got, beside(send))
        return own + got.astype(f32), extra

    h_slots, gates, ups, inners = [], [], [], []

    def forward(h_low):
        gate = product(h_low, w_gate_part)
        up = product(h_low, w_up_part)
        inner = (jax.nn.silu(gate) * up).astype(bf16)
        h_slots.append(h_low)
        gates.append(gate)
        ups.append(up)
        inners.append(inner)
        return product(inner, w_down_part)

    m_proj, h_all = ring(hidden.astype(bf16), forward, lambda send: stacked(h_slots, 56 * 2**20))
    m_scale = rms_scale(m_proj)
    out = (hidden + m_proj * m_scale * gain_ffn).astype(bf16).reshape(tokens.shape)
    grad_out = d_out.reshape(rows, width).astype(f32)
    d_gain_ffn = jnp.sum(grad_out * m_proj * m_scale, 0)
    dm_low = norm_back(m_proj, m_scale, grad_out * gain_ffn).astype(bf16)
    dms, d_gates, d_ups = [], [], []

    def backward(dm_slot):
        at = len(dms)
        gate, up = gates[at], ups[at]
        if at == size - 1:
            d_gate, d_up, share = ffn_backward(dm_slot, gate, up, w_down_part, w_gate_part, w_up_part)
            dms.append(dm_slot)
            d_gates.append(d_gate)
            d_ups.append(d_up)
            return share
        d_inner = against(dm_slot, w_down_part)
        sigmoid_gate = jax.nn.sigmoid(gate)
        d_gate = (d_inner * up * sigmoid_gate * (1.0 + gate * (1.0 - sigmoid_gate))).astype(bf16)
        d_up = (d_inner * (gate * sigmoid_gate)).astype(bf16)
        dms.append(dm_slot)
        d_gates.append(d_gate)
        d_ups.append(d_up)
        return against(d_gate, w_gate_part) + against(d_up, w_up_part)

    def grads(send):
        _, all_gates = together(send, stacked(d_gates, 56 * 2**20))
        return grad_halves(h_all, all_gates, False)

    d_sum, d_gate = ring(dm_low, backward, grads)
    cube_gate = CubeScatter(d_gate)
    cube_gate.step()

    def ff_rows(total):
        core = lax.rem(lax.axis_index("dp"), 2)
        total = total.astype(bf16).reshape(2, side, ff_half)
        mine, away = [lax.dynamic_index_in_dim(total, c, 0, keepdims=False) for c in (core, 1 - core)]
        away = flipped(away, 1)

        def moves():
            return [
                ((which, pl.multiple_of(behind(ahead) * own_rows, own_rows), 0), (ahead, which * own_rows, 0), (own_rows, ff_half))
                for ahead in slots
                for which in (0, 1)
            ]

        return relayout([mine, away], [(2 * own_rows, ff_half)] * size, bf16, moves)

    def row_blocks(total):
        wide = total.shape[1]
        return relayout(
            [total],
            [(own_rows, wide)] * size,
            bf16,
            lambda: [
                ((0, pl.multiple_of(behind(ahead) * own_rows, own_rows), 0), (ahead, 0, 0), (own_rows, wide))
                for ahead in slots
            ],
        )

    d_hidden = grad_out + d_sum
    d_gain_attn = jnp.sum(d_hidden * a_proj * a_scale, 0)
    da_low = norm_back(a_proj, a_scale, d_hidden * gain_attn).astype(bf16)
    d_attended = against(da_low, w_out_all).astype(bf16)
    d_attended = relayout(
        [d_attended],
        [(rows, part)] * size,
        bf16,
        lambda: [((0, 0, part_column(behind(ahead))), (ahead, 0, 0), (rows, part)) for ahead in slots],
    )
    all_ups = stacked(d_ups, 56 * 2**20)
    d_attended, cube_gate.got, da_low, all_ups = together(d_attended, cube_gate.got, da_low, all_ups)
    d_attended = send_ahead(d_attended, "seq")
    cube_gate.step()
    d_up = grad_halves(h_all, all_ups, False)
    d_w_out = grad_halves(attended, da_low, True)
    d_attended, d_w_out, cube_gate.got, d_up = together(d_attended, d_w_out, cube_gate.got, d_up)
    d_attended = in_order(d_attended, "seq")

    cube_up = CubeScatter(d_up)
    cube_up.step()
    gate_got = send_ahead(ff_rows(cube_gate.finish()), "seq")
    d_query, d_key, d_value = attend_back(query, key, value, d_attended, seg_ids)
    d_query, gate_got, cube_up.got, d_w_out = together(d_query, gate_got, cube_up.got, d_w_out)
    cube_up.step()
    dots, d_gain_qk = unrope(d_query, d_key, qkv, squares, cosine, sine_tab, gain_qk, width)
    dots = small_sum(dots.T, "seq")
    dots, cube_up.got, d_w_out = together(dots, cube_up.got, d_w_out)
    up_send = ff_rows(cube_up.finish())
    up_got = send_ahead(up_send, "seq")
    cube_out = CubeScatter(d_w_out, core=True)
    cube_out.step()
    d_qkv = raw_grad(d_query, d_key, d_value, qkv, squares, dots.T, cosine, sine_tab, gain_qk, width)
    d_slots = relayout(
        [d_qkv],
        [(rows, 3 * part)] * size,
        bf16,
        lambda: [((0, part_row(before(back)), 0), (back, 0, 0), (rows, 3 * part)) for back in slots],
    )
    d_slots, cube_out.got = together(d_slots, cube_out.got)
    cube_out.prepare()
    first, d_qkv, d_slots, d_gain_qk, up_got, cube_out.away, dms, d_gain_attn = together(
        against(d_slots[1], w_qkv).astype(bf16), d_qkv, d_slots, d_gain_qk, up_got, cube_out.away, dms, d_gain_attn
    )
    got = next_one(first, "seq")
    cube_out.send()
    d_gain_qk = lax.dynamic_update_slice_in_dim(jnp.zeros((2, width), f32), d_gain_qk, here * part, 1)
    d_gains = jnp.concatenate([d_gain_qk, d_gain_attn[None], d_gain_ffn[None]], 0)
    d_w_qkv = grad_halves(x_all, d_qkv, True)
    shares = [against(d_slots[2], w_qkv)]
    got, d_w_qkv, shares, cube_out.got, d_slots, dms, d_gains = together(
        got, d_w_qkv, shares, cube_out.got, d_slots, dms, d_gains
    )
    cube_qkv = CubeScatter(d_w_qkv, core=True)
    for back in range(2, size):
        got = next_one((shares[back - 2] + got.astype(f32)).astype(bf16), "seq")
        if back == 2:
            cube_qkv.step()
            cube_out.step()
            shares += [against(d_slots[at], w_qkv) for at in [*slots[3:], 0]]
            got, shares, cube_out.got, cube_qkv.got, dms = together(got, shares, cube_out.got, cube_qkv.got, dms)
        elif back == 3:
            cube_qkv.step()
            out_got = send_ahead(row_blocks(cube_out.finish()), "seq")
            d_down = grad_halves(stacked(inners, 56 * 2**20), stacked(dms, 56 * 2**20), False)
            got, cube_qkv.got, d_down = together(got, cube_qkv.got, d_down)
    cube_qkv.step()
    cube_qkv.got, d_down = together(cube_qkv.got, d_down)
    cube_down = CubeScatter(d_down)
    cube_down.step()
    d_w_qkv = row_blocks(cube_qkv.finish())
    d_w_qkv, out_got = together(d_w_qkv, out_got)
    d_w_qkv = send_ahead(d_w_qkv, "seq")
    d_down = cube_down.finish()
    d_gains = small_sum(d_gains.reshape(-1), "seq")
    for bit in [1] + cube_bits()[0]:
        d_gains = d_gains + flipped(d_gains, bit)
    d_gains = lax.dynamic_slice_in_dim(
        d_gains.reshape(4, width), (lax.axis_index("dp") * size + here) * own_rows, own_rows, 1
    )
    d_tokens = d_hidden + shares[-1] + got.astype(f32)
    d_w_out = sum(g.astype(f32) for g in out_got)
    d_w_qkv = relayout(
        d_w_qkv,
        [(own_rows, width)] * 3,
        f32,
        lambda: [
            ((back, 0, which * part), (which, 0, part_column(before(back))), (own_rows, part))
            for back in slots
            for which in range(3)
        ],
    )
    d_w_gate, d_w_up = ff_unpack(gate_got), ff_unpack(up_got)
    return (
        out,
        d_tokens.reshape(tokens.shape),
        d_w_qkv[0],
        d_w_qkv[1],
        d_w_qkv[2],
        d_w_out,
        d_gains[0],
        d_gains[1],
        d_gains[2],
        d_w_gate,
        d_w_up,
        d_down,
        d_gains[3],
    )


def solution(mesh):
    rows = P("dp", "seq", None)
    mat = P(("dp", "seq"), None)
    vec = P(("dp", "seq"))
    in_specs = (rows, P("dp", None), mat, mat, mat, mat, vec, vec, vec, mat, mat, mat, vec, rows)
    out_specs = (rows, rows, mat, mat, mat, mat, vec, vec, vec, mat, mat, mat, vec)
    return jax.shard_map(local, mesh=mesh, in_specs=in_specs, out_specs=out_specs, check_vma=False)
```

```python
import functools

import jax
import jax.numpy as jnp
from jax import lax
from jax.experimental import pallas as pl
from jax.experimental.pallas import tpu as pltpu
from jax.sharding import PartitionSpec as P

H = 16
HD = 128
DOCS = 4

epsilon = 1e-06
rope_base = 500000.0
masked_score = -1e30
bf16 = jnp.bfloat16
f32 = jnp.float32


def product(left, right):
    return jnp.dot(left, right, preferred_element_type=f32)


def against(left, right):
    return lax.dot_general(left, right, (((1,), (1,)), ((), ())), preferred_element_type=f32)


def weight_grad(left, right):
    return lax.dot_general(left, right, (((0,), (0,)), ((), ())), preferred_element_type=f32)


def rms_scale(values):
    return lax.rsqrt(jnp.mean(values * values, -1, keepdims=True) + epsilon)


def norm_back(values, scale_rows, grad_vals):
    return scale_rows * grad_vals - values * scale_rows**3 * jnp.mean(
        grad_vals * values, -1, keepdims=True
    )


def positions(seg_ids):
    doc_ids = jnp.arange(DOCS, dtype=jnp.int32)
    starts = jnp.sum((seg_ids[..., None, :] < doc_ids[:, None]).astype(jnp.int32), -1)
    one_hot = (seg_ids[..., None] == doc_ids).astype(jnp.int32)
    token_start = jnp.sum(one_hot * starts[..., None, :], axis=-1)
    return jnp.arange(seg_ids.shape[-1], dtype=jnp.int32) - token_start


def rope_tables(position_ids):
    freqs = rope_base ** (-jnp.arange(HD // 2, dtype=f32) * 2.0 / HD)
    angles = position_ids.astype(f32)[..., None] * freqs
    cosine = jnp.cos(angles)
    sine_tab = jnp.sin(angles)
    return (
        jnp.concatenate([cosine, cosine], -1),
        jnp.concatenate([sine_tab, sine_tab], -1),
    )


def contract(left, right, left_dim, right_dim):
    return lax.dot_general(left, right, (((left_dim,), (right_dim,)), ((), ())), preferred_element_type=f32)


def vmem(shape, index=None):
    return pl.BlockSpec(shape, index or (lambda *_: (0,) * len(shape)))


def kernel_params(grid=0):
    return pltpu.CompilerParams(vmem_limit_bytes=48 * 2**20)


def relayout_body(moves, count, *refs):
    ins, outs = refs[:count], refs[count:]
    for (src, src_row, src_col), (dst, dst_row, dst_col), (rows, cols) in moves():
        outs[dst][pl.ds(dst_row, rows), pl.ds(dst_col, cols)] = ins[src][
            pl.ds(src_row, rows), pl.ds(src_col, cols)
        ].astype(outs[dst].dtype)


def relayout(arrays, shapes, dtype, moves):
    outs = [jax.ShapeDtypeStruct(shape, dtype) for shape in shapes]
    size = sum(a.size * a.dtype.itemsize for a in [*arrays, *outs])
    return pl.pallas_call(
        functools.partial(relayout_body, moves, len(arrays)),
        in_specs=[vmem(a.shape) for a in arrays],
        out_specs=[vmem(o.shape) for o in outs],
        out_shape=outs,
        compiler_params=kernel_params(),
        cost_estimate=pl.CostEstimate(flops=0, bytes_accessed=size, transcendentals=0),
    )(*arrays)


def turned(values):
    lane = lax.broadcasted_iota(jnp.int32, values.shape, 1)
    rolled = pltpu.roll(values, HD // 2, 1)
    return jnp.where(lane < HD // 2, -rolled, rolled)


def query_key_body(width, raw_ref, squares_ref, cos_ref, sin_ref, gain_ref, q_ref, k_ref, v_ref):
    part = q_ref.shape[1]
    scales = lax.rsqrt(squares_ref[...] / width + epsilon)
    for which, out in enumerate((q_ref, k_ref)):
        for first in range(0, part, HD):
            gain = gain_ref[which : which + 1, first : first + HD]
            unit = raw_ref[:, which * part + first : which * part + first + HD] * scales[:, which : which + 1] * gain
            out[:, first : first + HD] = (unit * cos_ref[...] + turned(unit) * sin_ref[...]).astype(bf16)
    v_ref[...] = raw_ref[:, 2 * part :].astype(bf16)


def query_key(raw, squares, cosine, sine_tab, gains, width):
    tokens, part = raw.shape[0], raw.shape[1] // 3
    block = min(256, tokens)
    shape = jax.ShapeDtypeStruct((tokens, part), bf16)

    def by_rows(cols):
        return vmem((block, cols), lambda at: (at, 0))

    return pl.pallas_call(
        functools.partial(query_key_body, width),
        grid=(tokens // block,),
        in_specs=[by_rows(3 * part), by_rows(2), by_rows(HD), by_rows(HD), vmem(gains.shape)],
        out_specs=[by_rows(part)] * 3,
        out_shape=[shape] * 3,
        compiler_params=kernel_params(),
    )(raw, squares, cosine, sine_tab, gains)


def ffn_backward_body(steps, left_ref, down_w, gate_ref, up_ref, gate_w, up_w, d_gate_ref, d_up_ref, share_ref):
    step = pl.program_id(0)
    d_inner = contract(left_ref[...], down_w[...], 1, 1)
    gate = gate_ref[...]
    sigmoid = jax.nn.sigmoid(gate)
    d_gate = (d_inner * up_ref[...] * sigmoid * (1.0 + gate * (1.0 - sigmoid))).astype(bf16)
    d_up = (d_inner * (gate * sigmoid)).astype(bf16)
    d_gate_ref[...] = d_gate
    d_up_ref[...] = d_up
    share = contract(d_gate, gate_w[...], 1, 1) + contract(d_up, up_w[...], 1, 1)

    @pl.when(step == 0)
    def _():
        share_ref[...] = share

    if steps > 1:

        @pl.when(step > 0)
        def _():
            share_ref[...] += share


def ffn_backward(left, gate, up, w_down, w_gate, w_up):
    rows, width = left.shape
    extent = gate.shape[1]
    tile = min(512, extent)
    by_columns = vmem((rows, tile), lambda at: (0, at))
    return pl.pallas_call(
        functools.partial(ffn_backward_body, extent // tile),
        grid=(extent // tile,),
        in_specs=[
            vmem(left.shape),
            vmem((tile, width), lambda at: (at, 0)),
            by_columns,
            by_columns,
            vmem((width, tile), lambda at: (0, at)),
            vmem((width, tile), lambda at: (0, at)),
        ],
        out_specs=[by_columns, by_columns, vmem(left.shape)],
        out_shape=[
            jax.ShapeDtypeStruct(gate.shape, bf16),
            jax.ShapeDtypeStruct(gate.shape, bf16),
            jax.ShapeDtypeStruct(left.shape, f32),
        ],
        compiler_params=kernel_params(),
        cost_estimate=pl.CostEstimate(
            flops=6 * rows * width * extent, bytes_accessed=6 * width * extent, transcendentals=rows * extent
        ),
    )(left, w_down, gate, up, w_gate, w_up)


def grad_halves_body(left_ref, right_ref, one_ref, two_ref):
    total = contract(left_ref[...], right_ref[...], 0, 0).astype(bf16)
    cut = one_ref.shape[1]
    one_ref[...] = total[:, :cut]
    two_ref[...] = total[:, cut:]


def grad_halves(left, right, core):
    bits = (lax.axis_size("dp") - 1).bit_length() - (not core)
    (tokens, depth), cut = left.shape, right.shape[1] // 2
    block = min(256, depth)
    half = jax.ShapeDtypeStruct((depth, cut), bf16)
    halves = pl.pallas_call(
        grad_halves_body,
        grid=(depth // block,),
        in_specs=[vmem((tokens, block), lambda at: (0, at)), vmem(right.shape)],
        out_specs=[vmem((block, cut), lambda at: (at, 0))] * 2,
        out_shape=[half, half],
        compiler_params=kernel_params(),
        cost_estimate=pl.CostEstimate(
            flops=4 * tokens * depth * cut, bytes_accessed=4 * tokens * depth, transcendentals=0
        ),
    )(left, right)
    return [half.reshape((2,) * bits + (-1, cut)) for half in halves]


def key_weights(query, key, seg_query, seg_key, first, count):
    scores = contract(key, query, 1, 1) * HD ** (-0.5)
    shape = scores.shape
    allowed = (seg_key == seg_query) & (
        lax.broadcasted_iota(jnp.int32, shape, 0) <= first + lax.broadcasted_iota(jnp.int32, shape, 1)
    )
    scores = jnp.where(allowed, scores, masked_score)
    expos = jnp.exp(scores - jnp.max(scores, 0, keepdims=True))
    return expos * (1.0 / jnp.sum(expos, 0, keepdims=True))


def attend_body(blocks, q_ref, k_ref, v_ref, seg_q_ref, seg_k_ref, out_ref):
    rows = q_ref.shape[0]
    for at in range(blocks):
        seen = (at + 1) * rows

        @pl.when(pl.program_id(1) == at)
        def _():
            probs = key_weights(
                q_ref[...], k_ref[:seen], seg_q_ref[...], seg_k_ref[:seen], at * rows, seen
            ).astype(bf16)
            out_ref[...] = contract(probs, v_ref[:seen], 0, 0).astype(bf16)


def attention_specs(tokens, block):
    by_query = vmem((block, HD), lambda head, at: (at, head))
    by_head = vmem((tokens, HD), lambda head, at: (0, head))
    return by_query, by_head, [vmem((1, block), lambda head, at: (0, at)), vmem((tokens, 1))]


def attend(query, key, value, seg_ids):
    tokens, part = query.shape
    block = min(256, tokens)
    by_query, by_head, segs = attention_specs(tokens, block)
    return pl.pallas_call(
        functools.partial(attend_body, tokens // block),
        grid=(part // HD, tokens // block),
        in_specs=[by_query, by_head, by_head, *segs],
        out_specs=by_query,
        out_shape=jax.ShapeDtypeStruct(query.shape, bf16),
        compiler_params=kernel_params(),
    )(query, key, value, seg_ids[None, :], seg_ids[:, None])


def attend_back_body(
    blocks, q_ref, k_ref, v_ref, g_ref, seg_q_ref, seg_k_ref, dq_ref, dk_ref, dv_ref, dk_sum, dv_sum
):
    rows = q_ref.shape[0]
    scale = HD ** (-0.5)
    for at in range(blocks):
        seen = (at + 1) * rows

        @pl.when(pl.program_id(1) == at)
        def _():
            query, grad = q_ref[...], g_ref[...]
            probs = key_weights(query, k_ref[:seen], seg_q_ref[...], seg_k_ref[:seen], at * rows, seen)
            d_probs = contract(v_ref[:seen], grad, 1, 1)
            inner = jnp.sum(probs * d_probs, 0, keepdims=True)
            d_scores = (probs * (d_probs - inner)).astype(bf16)
            dq_ref[...] = (contract(d_scores, k_ref[:seen], 0, 0) * scale).astype(bf16)
            d_key = contract(d_scores, query, 1, 0) * scale
            d_value = contract(probs.astype(bf16), grad, 1, 0)
            old = seen - rows
            dk_sum[old:seen] = d_key[old:]
            dv_sum[old:seen] = d_value[old:]
            if at:
                dk_sum[:old] += d_key[:old]
                dv_sum[:old] += d_value[:old]
            if at == blocks - 1:
                dk_ref[...] = dk_sum[...].astype(bf16)
                dv_ref[...] = dv_sum[...].astype(bf16)


def attend_back(query, key, value, grad, seg_ids):
    tokens, part = query.shape
    block = min(256, tokens)
    by_query, by_head, segs = attention_specs(tokens, block)
    shape = jax.ShapeDtypeStruct(query.shape, bf16)
    return pl.pallas_call(
        functools.partial(attend_back_body, tokens // block),
        grid=(part // HD, tokens // block),
        in_specs=[by_query, by_head, by_head, by_query, *segs],
        out_specs=[by_query, by_head, by_head],
        out_shape=[shape] * 3,
        scratch_shapes=[pltpu.VMEM((tokens, HD), f32)] * 2,
        compiler_params=kernel_params(),
    )(query, key, value, grad, seg_ids[None, :], seg_ids[:, None])


def rope_back(grad, cosine, sine_tab):
    return grad * cosine - turned(grad * sine_tab)


def unrope_body(width, dq_ref, dk_ref, raw_ref, squares_ref, cos_ref, sin_ref, gain_ref, dots_ref, gains_ref):
    part = dq_ref.shape[1]
    scales = lax.rsqrt(squares_ref[...] / width + epsilon)

    @pl.when(pl.program_id(0) == 0)
    def _():
        gains_ref[...] = jnp.zeros_like(gains_ref)

    for which, ref in enumerate((dq_ref, dk_ref)):
        dots = 0.0
        for first in range(0, part, HD):
            raw = raw_ref[:, which * part + first : which * part + first + HD]
            grad = rope_back(ref[:, first : first + HD].astype(f32), cos_ref[...], sin_ref[...])
            both = grad * raw
            gain = gain_ref[which : which + 1, first : first + HD]
            dots = dots + jnp.sum(both * gain, 1, keepdims=True)
            gains_ref[which : which + 1, first : first + HD] += jnp.sum(
                both * scales[:, which : which + 1], 0, keepdims=True
            )
        dots_ref[:, which : which + 1] = dots


def unrope(d_query, d_key, raw, squares, cosine, sine_tab, gains, width):
    tokens, part = d_query.shape
    block = min(256, tokens)

    def by_rows(cols):
        return vmem((block, cols), lambda at: (at, 0))

    return pl.pallas_call(
        functools.partial(unrope_body, width),
        grid=(tokens // block,),
        in_specs=[by_rows(part)] * 2
        + [by_rows(3 * part), by_rows(2), by_rows(HD), by_rows(HD), vmem(gains.shape)],
        out_specs=[by_rows(2), vmem((2, part))],
        out_shape=[jax.ShapeDtypeStruct((tokens, 2), f32), jax.ShapeDtypeStruct((2, part), f32)],
        compiler_params=kernel_params(),
    )(d_query, d_key, raw, squares, cosine, sine_tab, gains)


def raw_grad_body(width, dq_ref, dk_ref, dv_ref, raw_ref, squares_ref, dots_ref, cos_ref, sin_ref, gain_ref, out_ref):
    part = dq_ref.shape[1]
    scales = lax.rsqrt(squares_ref[...] / width + epsilon)
    cubes = scales * scales * scales * dots_ref[...] / width
    for which, ref in enumerate((dq_ref, dk_ref)):
        for first in range(0, part, HD):
            at = slice(which * part + first, which * part + first + HD)
            grad = rope_back(ref[:, first : first + HD].astype(f32), cos_ref[...], sin_ref[...])
            grad = grad * gain_ref[which : which + 1, first : first + HD]
            out_ref[:, at] = (
                scales[:, which : which + 1] * grad - raw_ref[:, at] * cubes[:, which : which + 1]
            ).astype(bf16)
    out_ref[:, 2 * part :] = dv_ref[...]


def raw_grad(d_query, d_key, d_value, raw, squares, dots, cosine, sine_tab, gains, width):
    tokens, part = d_query.shape
    block = min(256, tokens)

    def by_rows(cols):
        return vmem((block, cols), lambda at: (at, 0))

    return pl.pallas_call(
        functools.partial(raw_grad_body, width),
        grid=(tokens // block,),
        in_specs=[by_rows(part)] * 3
        + [by_rows(3 * part), by_rows(2), by_rows(2), by_rows(HD), by_rows(HD), vmem(gains.shape)],
        out_specs=by_rows(3 * part),
        out_shape=jax.ShapeDtypeStruct((tokens, 3 * part), bf16),
        compiler_params=kernel_params(),
    )(d_query, d_key, d_value, raw, squares, dots, cosine, sine_tab, gains)


def together(*trees):
    return lax.optimization_barrier(trees)


def next_one(block, axis):
    size = lax.axis_size(axis)
    return lax.ppermute(block, axis, [(i, (i + 1) % size) for i in range(size)])


def flipped(block, bit):
    size = lax.axis_size("dp")
    return lax.ppermute(block, "dp", [(i, i ^ bit) for i in range(size)])


def exchange(blocks, axis):
    size, here = lax.axis_size(axis), lax.axis_index(axis)
    got = []
    for step in range(size):
        block = lax.dynamic_index_in_dim(blocks, lax.rem(here + step, size), 0, keepdims=False)
        if step:
            block = lax.ppermute(block, axis, [(i, (i + step) % size) for i in range(size)])
        got.append(block)
    return got


def send_ahead(blocks, axis):
    size = lax.axis_size(axis)
    return [blocks[0]] + [
        lax.ppermute(blocks[step], axis, [(i, (i + step) % size) for i in range(size)]) for step in range(1, size)
    ]


def share_out(block, axis):
    size = lax.axis_size(axis)
    return [block] + [
        lax.ppermute(block, axis, [(i, (i + step) % size) for i in range(size)]) for step in range(1, size)
    ]


def assemble_body(parts, places, count, cuts, *refs):
    pieces, outs, (held, in_sems, out_sems) = refs[:count], refs[count : count + len(cuts)], refs[count + len(cuts) :]
    reads, writes, first = [], [], 0
    for at, ((which, start, rows), place) in enumerate(zip(parts, places())):
        here = held.at[pl.ds(first, rows)]
        reads.append(pltpu.make_async_copy(pieces[which].at[pl.ds(start, rows)], here, in_sems.at[at]))
        writes.append(
            [
                pltpu.make_async_copy(
                    held.at[pl.ds(first, rows), pl.ds(left, wide)],
                    out.at[pl.ds(place, rows)],
                    out_sems.at[at * len(cuts) + n],
                )
                for n, (out, (left, wide)) in enumerate(zip(outs, cuts))
            ]
        )
        first += rows
    for read in reads:
        read.start()
    for read, copies in zip(reads, writes):
        read.wait()
        for write in copies:
            write.start()
    for copies in writes:
        for write in copies:
            write.wait()


def assemble(pieces, parts, places, cuts=None, room=0):
    shape = (sum(rows for _, _, rows in parts), pieces[0].shape[1])
    several, cuts = cuts is not None, cuts or [(0, shape[1])]
    anywhere = pl.BlockSpec(memory_space=pl.ANY)
    dtype = pieces[0].dtype
    size = shape[0] * shape[1] * dtype.itemsize
    results = pl.pallas_call(
        functools.partial(assemble_body, parts, places, len(pieces), cuts),
        in_specs=[anywhere] * len(pieces),
        out_specs=[anywhere] * len(cuts),
        out_shape=[jax.ShapeDtypeStruct((shape[0], wide), dtype) for _, wide in cuts],
        scratch_shapes=[
            pltpu.VMEM(shape, dtype),
            pltpu.SemaphoreType.DMA((len(parts),)),
            pltpu.SemaphoreType.DMA((len(parts) * len(cuts),)),
        ],
        compiler_params=pltpu.CompilerParams(vmem_limit_bytes=max(room, size + 2**20)),
        cost_estimate=pl.CostEstimate(flops=0, bytes_accessed=2 * size, transcendentals=0),
    )(*pieces)
    return results if several else results[0]


def stacked(pieces, room=0):
    parts = [(at, 0, p.shape[0]) for at, p in enumerate(pieces)]
    places = [sum(rows for _, _, rows in parts[:at]) for at in range(len(parts))]
    return assemble(pieces, parts, lambda: places, room=room)


def in_order(slots, axis, first=0, rows=None):
    size, rows = len(slots), rows or slots[0].shape[0]

    def places():
        here = lax.axis_index(axis)
        return [pl.multiple_of(lax.rem(here + (size - back), size) * rows, rows) for back in range(size)]

    return assemble(slots, [(at, first, rows) for at in range(size)], places)


def cube_bits():
    bits = [1 << b for b in range(1, (lax.axis_size("dp") - 1).bit_length())]
    return bits, bits[1:] + bits[:1]


class CubeGather:
    def __init__(self, pair, core=False):
        self.arrays = [[block] for block in pair]
        self.masks = [[[0]] for _ in pair]
        self.orders = [list(bits) + [1] * core for bits in cube_bits()]
        self.new = []

    def step(self):
        for at, arrays in enumerate(self.arrays):
            if len(arrays) > 1:
                self.arrays[at] = [stacked(arrays)]
                self.masks[at] = [sum(self.masks[at], [])]
        self.new = [flipped(arrays[0], order[0]) for arrays, order in zip(self.arrays, self.orders)]

    def set(self, new):
        for at, block in enumerate(new):
            bit = self.orders[at].pop(0)
            self.arrays[at].append(block)
            self.masks[at].append([m ^ bit for m in self.masks[at][0]])
        self.new = []

    def finish(self):
        self.set(self.new)
        while self.orders[0]:
            self.step()
            self.set(self.new)


def cube_join(cube, firsts, rows, fold=1, cuts=None):
    pieces, parts, where = [], [], []
    for (own, first), arrays, masks in zip(firsts, cube.arrays, cube.masks):
        step = arrays[0].shape[0] // len(masks[0])
        for array, blocks in zip(arrays, masks):
            for at, mask in enumerate(blocks):
                parts.append((len(pieces), at * step, step))
                where.append((own ^ mask, first))
            pieces.append(array)

    def places():
        here = lax.axis_index("dp")
        return [pl.multiple_of((here ^ mask) // fold * rows + first, step) for mask, first in where]

    return assemble(pieces, parts, places, cuts)


class CubeScatter:
    def __init__(self, pair, core=False):
        self.totals, self.got = list(pair), None
        self.orders = [[1] * core + list(bits) for bits in cube_bits()]
        self.dims = [sorted(order, reverse=True) for order in self.orders]

    def add(self):
        if self.got:
            self.totals = [t.astype(f32) + g.astype(f32) for t, g in zip(self.totals, self.got)]
        self.got = None
        return self.totals

    def prepare(self):
        self.add()
        self.away, self.bits = [], [order.pop(0) for order in self.orders]
        for which, (total, bit) in enumerate(zip(self.totals, self.bits)):
            at = self.dims[which].index(bit)
            self.dims[which].remove(bit)
            mine = (lax.axis_index("dp") // bit) % 2
            self.away.append(lax.dynamic_index_in_dim(total, 1 - mine, at, keepdims=False).astype(bf16))
            self.totals[which] = lax.dynamic_index_in_dim(total, mine, at, keepdims=False)

    def send(self):
        self.got = [flipped(away, bit) for away, bit in zip(self.away, self.bits)]

    def step(self):
        self.prepare()
        self.send()

    def finish(self):
        while self.orders[0]:
            self.step()
        return jnp.concatenate(self.add(), 1)


def small_sum(values, axis):
    return sum(share_out(values.reshape(-1), axis)).reshape(values.shape)


def local(
    tokens,
    segments,
    w_query,
    w_key,
    w_value,
    w_out,
    g_query,
    g_key,
    g_attn,
    w_gate,
    w_up,
    w_down,
    g_ffn,
    d_out,
):
    seqs, local_len, width = tokens.shape
    rows = seqs * local_len
    copies, size = lax.axis_size("dp"), lax.axis_size("seq")
    here = lax.axis_index("seq")
    total_len = size * local_len
    part = width // size
    heads = H // size
    own_rows = w_gate.shape[0]
    ff_width = w_gate.shape[1]
    ff_part = ff_width // size
    ff_own = w_down.shape[0]
    tok_rows = tokens.reshape(rows, width)

    side = width // copies
    pairs = copies // 2
    ff_half = ff_part // 2
    slots = range(size)

    def before(back):
        return lax.rem(lax.axis_index("seq") + (size - back), size)

    def behind(ahead):
        return lax.rem(lax.axis_index("seq") + ahead, size)

    def ff_column(pair, other, seq_at):
        return pl.multiple_of(((pair * 2 + (lax.rem(lax.axis_index("dp"), 2) ^ other)) * size + seq_at) * ff_own, ff_own)

    def ff_pack(weight):
        if ff_own % 128:
            core = lax.rem(lax.axis_index("dp"), 2)
            blocks = weight.reshape(own_rows, pairs, 2, size, ff_own).transpose(2, 3, 0, 1, 4)
            blocks = blocks.reshape(2, size, own_rows, ff_half)
            blocks = jnp.concatenate(
                [lax.dynamic_index_in_dim(blocks, c, 0, keepdims=False) for c in (core, 1 - core)], 1
            )
            return [lax.dynamic_index_in_dim(blocks, behind(ahead), 0, keepdims=False) for ahead in slots]
        return relayout(
            [weight],
            [(2 * own_rows, ff_half)] * size,
            bf16,
            lambda: [
                ((0, 0, ff_column(pair, other, behind(ahead))), (ahead, other * own_rows, pair * ff_own), (own_rows, ff_own))
                for ahead in slots
                for other in (0, 1)
                for pair in range(pairs)
            ],
        )

    def ff_unpack(got):
        if ff_own % 128:
            core = lax.rem(lax.axis_index("dp"), 2)
            joined = in_order(got, "seq").reshape(size, 2, own_rows, pairs, ff_own)
            joined = jnp.where(core == 0, joined, joined[:, ::-1])
            return joined.transpose(2, 3, 1, 0, 4).reshape(own_rows, ff_width).astype(f32)
        return relayout(
            got,
            [(own_rows, ff_width)],
            f32,
            lambda: [
                ((back, other * own_rows, pair * ff_own), (0, 0, ff_column(pair, other, before(back))), (own_rows, ff_own))
                for back in slots
                for other in (0, 1)
                for pair in range(pairs)
            ],
        )[0]

    def ff_pair(got):
        mine, away = [in_order(got, "seq", first, own_rows) for first in (0, own_rows)]
        return [mine, flipped(away, 1)]

    def two_parts(got):
        joined = in_order(got, "seq")
        return [joined[: side // 2], joined[side // 2 :]]

    def part_column(seq_at):
        return pl.multiple_of(seq_at * part, part)

    def part_row(seq_at):
        return pl.multiple_of(seq_at * rows, rows)

    lanes = 128
    own_gains = jnp.stack([g_query, g_key, g_attn, g_ffn], 1)
    own_gains = jnp.pad(own_gains, ((0, 0), (0, lanes - own_gains.shape[1])))
    qkv_send = relayout(
        [w_query, w_key, w_value, own_gains],
        [(own_rows, 3 * part + lanes)] * size,
        bf16,
        lambda: [
            ((which, 0, part_column(behind(ahead))), (ahead, 0, which * part), (own_rows, part))
            for ahead in slots
            for which in range(3)
        ]
        + [((3, 0, 0), (ahead, 0, 3 * part), (own_rows, lanes)) for ahead in slots],
    )
    qkv_got = send_ahead(qkv_send, "seq")
    cube_down = CubeGather([w_down[: ff_own // 2], w_down[ff_own // 2 :]])
    cube_down.step()
    gate_send, up_send = ff_pack(w_gate), ff_pack(w_up)
    qkv_got, new, gate_send, up_send, x_own = together(qkv_got, cube_down.new, gate_send, up_send, tok_rows)
    cube_down.set(new)

    gate_got = send_ahead(gate_send, "seq")
    cube_qkv = CubeGather(two_parts(qkv_got), core=True)
    cube_qkv.step()
    gate_got, new, up_send = together(gate_got, cube_qkv.new, up_send)
    cube_qkv.set(new)
    up_got = send_ahead(up_send, "seq")
    cube_qkv.step()
    cube_gate = CubeGather(ff_pair(gate_got))
    up_got, new, x_own, gate_own = together(up_got, cube_qkv.new, x_own, cube_gate.arrays)
    cube_qkv.set(new)
    cube_gate.arrays = gate_own
    cube_up = CubeGather(ff_pair(up_got))
    cosine, sine_tab = rope_tables(positions(segments).reshape(total_len))

    x_slots = [x_own]
    for at in range(size - 1):
        x_next = next_one(x_slots[-1], "seq")
        if at == 0:
            cube_gate.step()
            cube_down.step()
            x_next, new = together(x_next, cube_gate.new)
            cube_gate.set(new)
        elif at == 1:
            cube_gate.step()
            cube_qkv.step()
            x_next, new, more, cosine, sine_tab = together(x_next, cube_down.new, cube_qkv.new, cosine, sine_tab)
            cube_down.set(new)
            cube_qkv.set(more)
        elif at == size - 2:
            cube_up.step()
            x_next, new, w_out_own = together(x_next, cube_gate.new, w_out)
            cube_gate.set(new)
        x_slots.append(x_next)
    cube_qkv.finish()
    w_qkv, gains = cube_join(
        cube_qkv, ((0, 0), (0, side // 2)), side, cuts=[(0, 3 * part), (3 * part, lanes)]
    )

    x_all = in_order(x_slots, "seq")
    qkv = product(x_all, w_qkv)
    squares = jnp.stack([jnp.sum(jnp.square(qkv[:, first : first + part]), -1) for first in (0, part)], 0)
    squares = small_sum(squares, "seq")
    gains = gains[:, :4].T.astype(f32)
    gain_attn, gain_ffn = gains[2], gains[3]
    gain_qk = lax.dynamic_slice_in_dim(gains[:2], here * part, part, 1)
    squares, gain_qk, w_out_own, new = together(squares, gain_qk, w_out_own, cube_up.new)
    cube_up.set(new)
    out_got = share_out(w_out_own, "seq")
    cube_up.step()
    squares = squares.T
    query, key, value = query_key(qkv, squares, cosine, sine_tab, gain_qk, width)
    seg_ids = segments.reshape(total_len)
    attended = attend(query, key, value, seg_ids)
    attended = relayout(
        [attended],
        [(rows, part)] * size,
        bf16,
        lambda: [((0, part_row(behind(ahead)), 0), (ahead, 0, 0), (rows, part)) for ahead in slots],
    )
    attended, out_got, new = together(attended, out_got, cube_up.new)
    cube_up.set(new)
    attended = send_ahead(attended, "seq")
    cube_out = CubeGather(two_parts(out_got), core=True)
    cube_out.step()
    cube_out.set(cube_out.new)
    cube_out.step()
    for cube in (cube_down, cube_gate, cube_up):
        cube.finish()
    w_down_part = cube_join(cube_down, ((0, 0), (0, ff_own // 2)), ff_own, 2)
    w_gate_part, w_up_part = [cube_join(cube, ((0, 0), (1, 0)), side) for cube in (cube_gate, cube_up)]
    attended, new, w_down_part, w_gate_part, w_up_part = together(
        attended, cube_out.new, w_down_part, w_gate_part, w_up_part
    )
    cube_out.set(new)
    cube_out.finish()
    w_out_all = cube_join(cube_out, ((0, 0), (0, side // 2)), side)
    attended = relayout(
        attended,
        [(rows, width)],
        bf16,
        lambda: [((back, 0, 0), (0, 0, part_column(before(back))), (rows, part)) for back in slots],
    )[0]

    a_proj = product(attended, w_out_all)
    a_scale = rms_scale(a_proj)
    hidden = tok_rows.astype(f32) + a_proj * a_scale * gain_attn

    def ring(block, work, beside=lambda: ()):
        got, own, held = None, None, block
        for at in range(size):
            later = next_one(block, "seq") if at < size - 1 else None
            share = work(stacked([held, flipped(held, 1)]))
            share, away = share[:rows], share[rows:].astype(bf16)
            if later is not None:
                later, share, away, got = together(later, share, away, got)
            share = share + flipped(away, 1).astype(f32)
            if at == 0:
                own = share
            else:
                if at > 1:
                    share = share + got.astype(f32)
                send, held = together(share.astype(bf16), later)
                got = next_one(send, "seq")
            block, held = later, later if at == 0 else held
        got, extra = together(got, beside(send))
        return own + got.astype(f32), extra

    h_slots, gates, ups, inners = [], [], [], []

    def forward(h_low):
        gate = product(h_low, w_gate_part)
        up = product(h_low, w_up_part)
        inner = (jax.nn.silu(gate) * up).astype(bf16)
        h_slots.append(h_low)
        gates.append(gate)
        ups.append(up)
        inners.append(inner)
        return product(inner, w_down_part)

    m_proj, h_all = ring(hidden.astype(bf16), forward, lambda send: stacked(h_slots, 56 * 2**20))
    m_scale = rms_scale(m_proj)
    out = (hidden + m_proj * m_scale * gain_ffn).astype(bf16).reshape(tokens.shape)
    grad_out = d_out.reshape(rows, width).astype(f32)
    d_gain_ffn = jnp.sum(grad_out * m_proj * m_scale, 0)
    dm_low = norm_back(m_proj, m_scale, grad_out * gain_ffn).astype(bf16)
    dms, d_gates, d_ups = [], [], []

    def backward(dm_slot):
        at = len(dms)
        gate, up = gates[at], ups[at]
        if at == size - 1:
            d_gate, d_up, share = ffn_backward(dm_slot, gate, up, w_down_part, w_gate_part, w_up_part)
            dms.append(dm_slot)
            d_gates.append(d_gate)
            d_ups.append(d_up)
            return share
        d_inner = against(dm_slot, w_down_part)
        sigmoid_gate = jax.nn.sigmoid(gate)
        d_gate = (d_inner * up * sigmoid_gate * (1.0 + gate * (1.0 - sigmoid_gate))).astype(bf16)
        d_up = (d_inner * (gate * sigmoid_gate)).astype(bf16)
        dms.append(dm_slot)
        d_gates.append(d_gate)
        d_ups.append(d_up)
        return against(d_gate, w_gate_part) + against(d_up, w_up_part)

    def grads(send):
        _, all_gates = together(send, stacked(d_gates, 56 * 2**20))
        return grad_halves(h_all, all_gates, False)

    d_sum, d_gate = ring(dm_low, backward, grads)
    cube_gate = CubeScatter(d_gate)
    cube_gate.step()

    def ff_rows(total):
        core = lax.rem(lax.axis_index("dp"), 2)
        total = total.astype(bf16).reshape(2, side, ff_half)
        mine, away = [lax.dynamic_index_in_dim(total, c, 0, keepdims=False) for c in (core, 1 - core)]
        away = flipped(away, 1)

        def moves():
            return [
                ((which, pl.multiple_of(behind(ahead) * own_rows, own_rows), 0), (ahead, which * own_rows, 0), (own_rows, ff_half))
                for ahead in slots
                for which in (0, 1)
            ]

        return relayout([mine, away], [(2 * own_rows, ff_half)] * size, bf16, moves)

    def row_blocks(total):
        wide = total.shape[1]
        return relayout(
            [total],
            [(own_rows, wide)] * size,
            bf16,
            lambda: [
                ((0, pl.multiple_of(behind(ahead) * own_rows, own_rows), 0), (ahead, 0, 0), (own_rows, wide))
                for ahead in slots
            ],
        )

    d_hidden = grad_out + d_sum
    d_gain_attn = jnp.sum(d_hidden * a_proj * a_scale, 0)
    da_low = norm_back(a_proj, a_scale, d_hidden * gain_attn).astype(bf16)
    d_attended = against(da_low, w_out_all).astype(bf16)
    d_attended = relayout(
        [d_attended],
        [(rows, part)] * size,
        bf16,
        lambda: [((0, 0, part_column(behind(ahead))), (ahead, 0, 0), (rows, part)) for ahead in slots],
    )
    all_ups = stacked(d_ups, 56 * 2**20)
    d_attended, cube_gate.got, da_low, all_ups = together(d_attended, cube_gate.got, da_low, all_ups)
    d_attended = send_ahead(d_attended, "seq")
    cube_gate.step()
    d_up = grad_halves(h_all, all_ups, False)
    d_w_out = grad_halves(attended, da_low, True)
    d_attended, d_w_out, cube_gate.got, d_up = together(d_attended, d_w_out, cube_gate.got, d_up)
    d_attended = in_order(d_attended, "seq")

    cube_up = CubeScatter(d_up)
    cube_up.step()
    gate_got = send_ahead(ff_rows(cube_gate.finish()), "seq")
    d_query, d_key, d_value = attend_back(query, key, value, d_attended, seg_ids)
    d_query, gate_got, cube_up.got, d_w_out = together(d_query, gate_got, cube_up.got, d_w_out)
    cube_up.step()
    dots, d_gain_qk = unrope(d_query, d_key, qkv, squares, cosine, sine_tab, gain_qk, width)
    dots = small_sum(dots.T, "seq")
    dots, cube_up.got, d_w_out = together(dots, cube_up.got, d_w_out)
    up_send = ff_rows(cube_up.finish())
    up_got = send_ahead(up_send, "seq")
    cube_out = CubeScatter(d_w_out, core=True)
    cube_out.step()
    d_qkv = raw_grad(d_query, d_key, d_value, qkv, squares, dots.T, cosine, sine_tab, gain_qk, width)
    d_slots = relayout(
        [d_qkv],
        [(rows, 3 * part)] * size,
        bf16,
        lambda: [((0, part_row(before(back)), 0), (back, 0, 0), (rows, 3 * part)) for back in slots],
    )
    d_slots, cube_out.got = together(d_slots, cube_out.got)
    cube_out.prepare()
    first, d_qkv, d_slots, d_gain_qk, up_got, cube_out.away, dms, d_gain_attn = together(
        against(d_slots[1], w_qkv).astype(bf16), d_qkv, d_slots, d_gain_qk, up_got, cube_out.away, dms, d_gain_attn
    )
    got = next_one(first, "seq")
    cube_out.send()
    d_gain_qk = lax.dynamic_update_slice_in_dim(jnp.zeros((2, width), f32), d_gain_qk, here * part, 1)
    d_gains = jnp.concatenate([d_gain_qk, d_gain_attn[None], d_gain_ffn[None]], 0)
    d_w_qkv = grad_halves(x_all, d_qkv, True)
    shares = [against(d_slots[2], w_qkv)]
    got, d_w_qkv, shares, cube_out.got, d_slots, dms, d_gains = together(
        got, d_w_qkv, shares, cube_out.got, d_slots, dms, d_gains
    )
    cube_qkv = CubeScatter(d_w_qkv, core=True)
    for back in range(2, size):
        got = next_one((shares[back - 2] + got.astype(f32)).astype(bf16), "seq")
        if back == 2:
            cube_qkv.step()
            cube_out.step()
            shares += [against(d_slots[at], w_qkv) for at in [*slots[3:], 0]]
            got, shares, cube_out.got, cube_qkv.got, dms = together(got, shares, cube_out.got, cube_qkv.got, dms)
        elif back == 3:
            cube_qkv.step()
            out_got = send_ahead(row_blocks(cube_out.finish()), "seq")
            d_down = grad_halves(stacked(inners, 56 * 2**20), stacked(dms, 56 * 2**20), False)
            got, cube_qkv.got, d_down = together(got, cube_qkv.got, d_down)
    cube_qkv.step()
    cube_qkv.got, d_down = together(cube_qkv.got, d_down)
    cube_down = CubeScatter(d_down)
    cube_down.step()
    d_w_qkv = row_blocks(cube_qkv.finish())
    d_w_qkv, out_got = together(d_w_qkv, out_got)
    d_w_qkv = send_ahead(d_w_qkv, "seq")
    d_down = cube_down.finish()
    d_gains = small_sum(d_gains.reshape(-1), "seq")
    for bit in [1] + cube_bits()[0]:
        d_gains = d_gains + flipped(d_gains, bit)
    d_gains = lax.dynamic_slice_in_dim(
        d_gains.reshape(4, width), (lax.axis_index("dp") * size + here) * own_rows, own_rows, 1
    )
    d_tokens = d_hidden + shares[-1] + got.astype(f32)
    d_w_out = sum(g.astype(f32) for g in out_got)
    d_w_qkv = relayout(
        d_w_qkv,
        [(own_rows, width)] * 3,
        f32,
        lambda: [
            ((back, 0, which * part), (which, 0, part_column(before(back))), (own_rows, part))
            for back in slots
            for which in range(3)
        ],
    )
    d_w_gate, d_w_up = ff_unpack(gate_got), ff_unpack(up_got)
    return (
        out,
        d_tokens.reshape(tokens.shape),
        d_w_qkv[0],
        d_w_qkv[1],
        d_w_qkv[2],
        d_w_out,
        d_gains[0],
        d_gains[1],
        d_gains[2],
        d_w_gate,
        d_w_up,
        d_down,
        d_gains[3],
    )


def solution(mesh):
    rows = P("dp", "seq", None)
    mat = P(("dp", "seq"), None)
    vec = P(("dp", "seq"))
    in_specs = (rows, P("dp", None), mat, mat, mat, mat, vec, vec, vec, mat, mat, mat, vec, rows)
    out_specs = (rows, rows, mat, mat, mat, mat, vec, vec, vec, mat, mat, mat, vec)
    return jax.shard_map(local, mesh=mesh, in_specs=in_specs, out_specs=out_specs, check_vma=False)
```
